512 devices in a mesh: child: 2 (over x_hi), row: 16 (over z, x_lo), col: 16 (over y, core).
Axes of the slice: x: 4 (x_hi: 2, x_lo: 2; x = x_hi * 2 + x_lo), y: 8, z: 8, core: 2. Of those that a mesh axis runs over, the one named last changes fastest.
Arguments:
- contrib: float32 [2, 8192, 8192], P('child', 'row', 'col'), may hold values from -0.0625 to 0.0625
- assembled: float32 [2, 8192, 16384], P('child', 'row', 'col'), may hold values from -0.0625 to 0.0625
- pattern: int32 [64, 64], P('row', 'col'), may hold values 0 or 1
- omega: float32 [16384, 256], P('col', 'row'), may hold values from -6 to 6
- row_maps: int32 [2, 8192], P('child'), may hold values from 0 to 16383, as said below
- leaf_bounds: int32 [16], P('row'), may hold values from 448 to 576
Outputs:
- bases: float32 [16384, 256], P('row', ('child', 'col'))
- coupling: float32 [16, 2, 256, 256], P('row', None, ('child', 'col'))
The draws below stay inside these ranges and needn't reach their ends.
Inputs may be any that keep to these rules, and one draw needn't show every extreme that they name: `row_maps`: for each child, entries k * 512 to (k + 1) * 512 - 1 are distinct, rising, and lie in k * 1024 to (k + 1) * 1024 - 1.
All inputs are finite; a program needn't handle non-finite values. No bound on the sum of `pattern` on one device may be relied on, other than what follows from the above.
Results may differ from the reference program's by a relative error of at most 0.0003.
Values sent between devices are 32-bit elements; how exact they have to be, the bound alone decides.
No kernel may reach another device: no remote copies, remote signals or barrier semaphores. Data moves between devices by JAX's collectives and lax.ppermute only.
A program may use at most 64 MiB of HBM per device.

```python
import jax
import jax.numpy as jnp
from jax import lax

TR = 512
R = 256
BT = 256
PW = 1024
FC = 8192
PF = 16384
N_ROW = 16


def draw_row_maps(key, part):
    blocks = FC // TR
    keys = jax.random.split(jax.random.fold_in(key, 17), 2 * blocks)

    def select(single_key):
        return jnp.sort(jax.random.permutation(single_key, PW)[:TR].astype(jnp.int32))
    picked = jax.vmap(select)(keys).reshape(2, blocks, TR)
    offsets = (jnp.arange(blocks, dtype=jnp.int32) * PW)[None, :, None]
    return (picked + offsets).reshape(2, FC).astype(jnp.int32)


def set_ends(array, key, least, largest):
    index_at = [jax.random.randint(jax.random.fold_in(key, axis), (), 0, length) for axis, length in enumerate(array.shape)]
    longest = array.shape.index(max(array.shape))
    next_to = index_at[:longest] + [(index_at[longest] + 1) % array.shape[longest]] + index_at[longest + 1:]
    return array.at[tuple(index_at)].set(least).at[tuple(next_to)].set(largest)


def level_of(rng, shape, cuts, least, top_value):
    gain, own = 1.0, jax.random.fold_in(rng, 6)
    for position, blocks in cuts:
        heights = jnp.exp(jax.random.uniform(jax.random.fold_in(own, position), (blocks,), jnp.float32, least / len(cuts), top_value / len(cuts)))
        gain = gain * jnp.repeat(heights, shape[position] // blocks).reshape([-1 if axis == position else 1 for axis in range(len(shape))])
    return gain


def centred(own_key, extent, deviation, most, cuts=(), kind=jnp.bfloat16):
    drawn = jax.random.normal(own_key, extent, jnp.float32) * deviation
    if len(cuts) > 0:
        drawn = level_of(own_key, extent, cuts, -0.22, 0.18) * drawn
    return jnp.clip(drawn, min=-most, max=most).astype(kind)


def setup_inputs(seed: int = 0) -> dict:
    splits = jax.random.split(jax.random.key(seed), 7)
    return {
        "contrib": centred(splits[0], (2, FC, FC), FC ** -0.5, 0.0625, ((0, 2), (1, 16), (2, 16)), jnp.float32),
        "assembled": centred(splits[1], (2, PF // 2, PF), (PF // 2) ** -0.5, 0.0625, ((0, 2), (1, 16), (2, 16)), jnp.float32),
        "pattern": set_ends((jax.random.randint(splits[2], (PF // BT, PF // BT), 0, 2) < 1).astype(jnp.int32), jax.random.fold_in(splits[2], 1), 0, 1),
        "omega": centred(splits[3], (PF, R), 1.0, 6.0, ((0, 16), (1, 16)), jnp.float32),
        "row_maps": draw_row_maps(jax.random.fold_in(splits[6], 71), 0),
        "leaf_bounds": set_ends(jax.random.randint(splits[5], (N_ROW,), PW // 2 - PW // 16, PW // 2 + PW // 16 + 1), jax.random.fold_in(splits[5], 1), PW // 2 - PW // 16, (PW // 2 + PW // 16 + 1) - 1).astype(jnp.int32),
    }


highest = lax.Precision.HIGHEST

def leaf_factors(window, leaf_bound):
    positions = jnp.arange(window.shape[0], dtype=jnp.int32)
    first_leaf = (positions < leaf_bound)[:, None]
    head_count = leaf_bound.astype(jnp.float32)
    tail_count = (window.shape[0] - leaf_bound).astype(jnp.float32)
    head_gram = jnp.dot(jnp.where(first_leaf, window, 0.0).T, window, precision=highest) / head_count
    tail_gram = jnp.dot(jnp.where(first_leaf, 0.0, window).T, window, precision=highest) / tail_count
    return jnp.linalg.cholesky(jnp.stack([head_gram, tail_gram]))

def leaf_bases(window, first_leaf, factors):
    head_part = lax.linalg.triangular_solve(factors[0], window, left_side=False, lower=True, transpose_a=True)
    tail_part = lax.linalg.triangular_solve(factors[1], window, left_side=False, lower=True, transpose_a=True)
    return jnp.where(first_leaf, head_part, tail_part)

def reference(contrib, assembled, pattern, omega, row_maps, leaf_bounds):
    samples = jnp.zeros((PF, R), jnp.float32)

    def window_term(window_index):
        zero_start = jnp.zeros((), jnp.int32)
        row_start = (window_index * TR).astype(jnp.int32)
        row_block = lax.dynamic_slice(assembled, (zero_start, row_start, zero_start), (2, TR, PF)).reshape(PW, PF)
        tile_start = (window_index * (PW // BT)).astype(jnp.int32)
        tiles = lax.dynamic_slice_in_dim(pattern, tile_start, PW // BT, 0).astype(jnp.float32)
        masked = (row_block.reshape(PW // BT, BT, PF // BT, BT) * tiles[:, None, :, None]).reshape(PW, PF)
        return jnp.dot(masked, omega, precision=highest)
    samples = samples + lax.map(window_term, jnp.arange(N_ROW, dtype=jnp.int32)).reshape(PF, R)
    for child_index in range(2):
        picked = jnp.take(omega, row_maps[child_index], axis=0)
        product = jnp.dot(contrib[child_index], picked, precision=highest)
        samples = samples.at[row_maps[child_index]].add(product)
    windows = samples.reshape(N_ROW, PW, R)
    factors = jax.vmap(leaf_factors)(windows, leaf_bounds)
    positions = jnp.arange(PW, dtype=jnp.int32)
    first_leaf = (positions[None, :] < leaf_bounds[:, None])[:, :, None]
    bases = jax.vmap(leaf_bases)(windows, first_leaf, factors).reshape(PF, R)
    partner = jnp.arange(N_ROW, dtype=jnp.int32) ^ 1
    sibling = jnp.take(factors, partner, axis=0)
    coupling = jnp.einsum('wlab,wlac->wlbc', factors, sibling, precision=highest)
    return (bases, coupling)
```

```python
import jax
import jax.numpy as jnp
from jax import lax
from jax.sharding import Mesh, PartitionSpec as P

R = 256
BT = 256

high = lax.Precision.HIGH
highest = lax.Precision.HIGHEST

SWAP = [(0, 1), (1, 0)]


def dot_nt(a, b, precision=high):
    return lax.dot_general(a, b, (((1,), (1,)), ((), ())), precision=precision)


def window_leaves(window, leaf_bound, counts):
    window_rows = window.shape[0]
    upper = window_rows // 2 + window_rows // 16
    lower = window_rows // 2 - window_rows // 16
    positions = jnp.arange(window_rows, dtype=jnp.int32)
    first_leaf = (positions < leaf_bound)[:, None]
    head_rows = window[:upper]
    tail_rows = window[lower:]
    head_masked = jnp.where(first_leaf[:upper], head_rows, 0.0)
    tail_masked = jnp.where(first_leaf[lower:], 0.0, tail_rows)
    head_gram = jnp.dot(head_masked.T, head_rows, precision=highest)
    tail_gram = jnp.dot(tail_masked.T, tail_rows, precision=highest)
    factors = jnp.linalg.cholesky(jnp.stack([head_gram, tail_gram]) / counts)
    head_part = lax.linalg.triangular_solve(
        factors[0], head_rows, left_side=False, lower=True, transpose_a=True
    )
    tail_part = lax.linalg.triangular_solve(
        factors[1], tail_rows, left_side=False, lower=True, transpose_a=True
    )
    middle = jnp.where(first_leaf[lower:upper], head_part[lower:], tail_part[: upper - lower])
    whole = jnp.concatenate([head_part[:lower], middle, tail_part[upper - lower :]], axis=0)
    return (factors, whole)


def local(contrib, assembled, pattern, omega, row_maps, leaf_bounds):
    tile_rows = contrib.shape[1]
    tile_cols = contrib.shape[2]
    window_rows = omega.shape[0]
    own_cols_count = omega.shape[1]
    z_count = lax.axis_size("z")
    groups = lax.axis_size("child") * lax.axis_size("y")
    child = lax.axis_index("child")
    xl = lax.axis_index("xl")
    core = lax.axis_index("core")
    row_pos = lax.axis_index(("z", "xl"))
    col_pos = lax.axis_index(("y", "core"))
    width = R // (2 * groups)
    child_maps = row_maps[0]
    column_maps = (
        lax.dynamic_slice_in_dim(child_maps, col_pos * tile_cols, tile_cols) - col_pos * window_rows
    )
    target_maps = (
        lax.dynamic_slice_in_dim(child_maps, row_pos * tile_rows, tile_rows) - row_pos * window_rows
    )
    places = jnp.arange(window_rows, dtype=jnp.int32)
    pick = (places[:, None] == column_maps[None, :]).astype(jnp.float32)
    spread = (target_maps[:, None] == places[None, :]).astype(jnp.float32)
    pattern_rows = lax.dynamic_slice_in_dim(
        pattern, child * (tile_rows // BT), tile_rows // BT, 0
    ).astype(jnp.float32)
    masked = (
        assembled[0].reshape(tile_rows // BT, BT, window_rows // BT, BT)
        * pattern_rows[:, None, :, None]
    ).reshape(tile_rows, window_rows)

    lines = omega.T
    own = lax.all_to_all(
        jnp.broadcast_to(lines, (z_count, own_cols_count, window_rows)), "z", 0, 0
    )
    other = lax.ppermute(own, "xl", SWAP)

    def partial(omega_lines):
        picked = jnp.dot(omega_lines, pick, precision=high)
        product = dot_nt(picked, contrib[0])
        sparse = dot_nt(omega_lines, masked)
        spread_out = jnp.dot(product, spread, precision=high)
        zero = jnp.zeros_like(sparse)
        placed = jnp.concatenate(
            [jnp.where(child == 0, sparse, zero), jnp.where(child == 0, zero, sparse)], axis=1
        )
        return (spread_out + placed).reshape(z_count, width, window_rows)

    def half(gathered):
        split = gathered.reshape(z_count, 2, width, window_rows)
        give = lax.dynamic_index_in_dim(split, 1 - core, 1, keepdims=False)
        keep = lax.dynamic_index_in_dim(split, core, 1, keepdims=False)
        arrived = lax.ppermute(partial(give.reshape(-1, window_rows)), "core", SWAP)
        return partial(keep.reshape(-1, window_rows)) + arrived

    parts = jnp.concatenate([half(own), half(other)], axis=0)
    terms = lax.all_to_all(parts, ("child", "y"), 0, 0)
    samples = jnp.sum(terms, axis=0)
    mine = lax.all_to_all(
        jnp.broadcast_to(samples, (groups, width, window_rows)), ("child", "y"), 0, 0
    )
    theirs = lax.ppermute(mine, "core", SWAP)
    pair = jnp.where(core == 0, jnp.stack([mine, theirs]), jnp.stack([theirs, mine]))
    pair = pair.reshape(2, 2, z_count, width, window_rows)
    pair = jnp.where(xl == 0, pair, pair[:, ::-1])
    window = pair.transpose(2, 1, 0, 3, 4).reshape(R, window_rows)

    leaf_bound = leaf_bounds[0]
    counts = jnp.stack([leaf_bound, window_rows - leaf_bound]).astype(jnp.float32)[:, None, None]
    factors, whole = window_leaves(window.T, leaf_bound, counts)
    group_pos = child * lax.axis_size("y") * 2 + col_pos
    bases = lax.dynamic_slice_in_dim(whole, group_pos * width, width, 1)
    own_cols = lax.dynamic_slice_in_dim(factors, group_pos * width, width, 2)
    sibling = lax.ppermute(factors, "xl", SWAP)
    coupling = jnp.einsum("lab,lac->lbc", own_cols, sibling, precision=highest)
    return (bases, coupling[None])


def solution(mesh):
    fine = Mesh(mesh.devices.reshape(2, 8, 2, 8, 2), ("child", "z", "xl", "y", "core"))
    row, col = ("z", "xl"), ("y", "core")
    in_specs = (
        P("child", row, col),
        P("child", row, col),
        P(row, col),
        P(col, row),
        P("child", None),
        P(row),
    )
    out_specs = (P(row, ("child",) + col), P(row, None, ("child",) + col, None))
    return jax.shard_map(local, mesh=fine, in_specs=in_specs, out_specs=out_specs, check_vma=False)
```

```python
import jax
import jax.numpy as jnp
from jax import lax
from jax.experimental import pallas as pl
from jax.experimental.pallas import tpu as pltpu
from jax.sharding import Mesh, PartitionSpec as P

R = 256
BT = 256
HALF = 128

f32, bf16 = jnp.float32, jnp.bfloat16
highest = lax.Precision.HIGHEST
SWAP = [(0, 1), (1, 0)]
NT = (((1,), (1,)), ((), ()))
TN = (((0,), (0,)), ((), ()))
VMEM = pl.BlockSpec(memory_space=pltpu.VMEM)
SMEM = pl.BlockSpec(memory_space=pltpu.SMEM)
PARAMS = pltpu.CompilerParams(vmem_limit_bytes=40 << 20)


def shape(*sizes, dtype=f32):
    return jax.ShapeDtypeStruct(sizes, dtype)


def dot(a, b, dims, precision=None):
    return lax.dot_general(a, b, dims, precision=precision, preferred_element_type=f32)


def two_parts(a):
    top = a.astype(bf16)
    return top, (a - top.astype(f32)).astype(bf16)


def operator_kernel(scalars, pattern, contrib, assembled, columns, targets, top, low, c_top, c_low, pick):
    step = pl.program_id(0)
    rows, cols = top.shape
    child = scalars[0]

    @pl.when(step == 0)
    def _():
        c_top[...], c_low[...] = two_parts(contrib[...])
        places = lax.broadcasted_iota(jnp.int32, pick.shape, 0)
        pick[...] = (places == columns[...]).astype(f32).astype(bf16)

    places = lax.broadcasted_iota(jnp.int32, (rows, targets.shape[1]), 0) + step * rows
    spread = (places == targets[...]).astype(f32).astype(bf16)
    high_rows = dot(spread, c_top[...], (((1,), (0,)), ((), ()))).astype(bf16)
    low_rows = dot(spread, c_low[...], (((1,), (0,)), ((), ()))).astype(bf16)
    total = dot(high_rows, pick[...], NT) + dot(low_rows, pick[...], NT)
    per_half = pl.num_programs(0) // 2
    here = (step // per_half == child).astype(f32)
    tile_row = child * per_half + step % per_half
    for tile in range(cols // BT):
        lanes = slice(tile * BT, (tile + 1) * BT)
        keep = pattern[tile_row, tile].astype(f32) * here
        top[:, lanes], low[:, lanes] = two_parts(total[:, lanes] + assembled[:, lanes] * keep)


def build_operator(scalars, pattern, contrib, assembled, columns, targets):
    tile_rows, tile_cols = contrib.shape
    window_rows = assembled.shape[1]
    steps = window_rows // BT
    block = pl.BlockSpec((BT, window_rows), lambda i: (i, 0))
    return pl.pallas_call(
        operator_kernel,
        grid=(steps,),
        in_specs=[
            SMEM,
            SMEM,
            pl.BlockSpec((tile_rows, tile_cols), lambda i: (0, 0)),
            pl.BlockSpec((BT, window_rows), lambda i: (i % (steps // 2), 0)),
            pl.BlockSpec((1, tile_cols), lambda i: (0, 0)),
            pl.BlockSpec((1, tile_rows), lambda i: (0, 0)),
        ],
        out_specs=[block, block],
        out_shape=[shape(window_rows, window_rows, dtype=bf16)] * 2,
        scratch_shapes=[
            pltpu.VMEM((tile_rows, tile_cols), bf16),
            pltpu.VMEM((tile_rows, tile_cols), bf16),
            pltpu.VMEM((window_rows, tile_cols), bf16),
        ],
        compiler_params=PARAMS,
        cost_estimate=pl.CostEstimate(flops=4 * 10**9, bytes_accessed=8 * 10**6, transcendentals=0),
    )(scalars, pattern, contrib, assembled, columns, targets)


def apply_kernel(scalars, lines, top, low, give, keep, h_top, h_low):
    core = scalars[2]
    count, _, width, depth = lines.shape

    @pl.when(pl.program_id(0) == 0)
    def _():
        both = jnp.concatenate(
            [lines[:, pl.ds(1 - core, 1)].reshape(-1, depth), lines[:, pl.ds(core, 1)].reshape(-1, depth)]
        )
        h_top[...], h_low[...] = two_parts(both)

    out = (
        dot(h_top[...], top[...], NT) + dot(h_top[...], low[...], NT) + dot(h_low[...], top[...], NT)
    )
    give[...] = out[: count * width].reshape(give.shape)
    keep[...] = out[count * width :].reshape(keep.shape)


def apply_operator(scalars, gathered, top, low):
    count, both, depth = gathered.shape
    width = both // 2
    window_rows = top.shape[0]
    lines = gathered.reshape(count, 2, width, depth)
    out_block = pl.BlockSpec((count, width, BT), lambda i: (0, 0, i))
    in_block = pl.BlockSpec((BT, depth), lambda i: (i, 0))
    return pl.pallas_call(
        apply_kernel,
        grid=(window_rows // BT,),
        in_specs=[SMEM, pl.BlockSpec(lines.shape, lambda i: (0, 0, 0, 0)), in_block, in_block],
        out_specs=[out_block, out_block],
        out_shape=[shape(count, width, window_rows)] * 2,
        scratch_shapes=[pltpu.VMEM((count * both, depth), bf16)] * 2,
        compiler_params=PARAMS,
        cost_estimate=pl.CostEstimate(flops=10**9, bytes_accessed=6 * 10**6, transcendentals=0),
    )(scalars, lines, top, low)


def rank_update(u):
    a = u.astype(bf16).astype(f32)
    b = (u - a).astype(bf16).astype(f32)
    c = u - a - b
    left = jnp.concatenate([a, a, b, b, a, c], 0).astype(bf16)
    right = jnp.concatenate([a, b, a, b, c, a], 0).astype(bf16)
    return dot(left[:, :HALF], right, TN)


def factor_panel(block, r):
    panel = block[pl.ds(r, 8), :]
    tiles = panel.shape[1] // 128
    pivot = pltpu.roll(panel[:, :128], 128 - r, 1)
    rows = [
        [jnp.broadcast_to(panel[j : j + 1, t * 128 : (t + 1) * 128], (8, 128)) for t in range(tiles)]
        for j in range(8)
    ]
    spread = [jnp.broadcast_to(pivot[j : j + 1], (8, 128)) for j in range(8)]
    a = [
        [jnp.broadcast_to(spread[j][:, i : i + 1], (8, 128)) if i >= j else None for j in range(8)]
        for i in range(8)
    ]
    for j in range(8):
        inverse = lax.rsqrt(a[j][j])
        column = {i: a[i][j] * inverse for i in range(j + 1, 8)}
        for k in range(j + 1, 8):
            for i in range(k, 8):
                a[i][k] = a[i][k] - column[i] * column[k]
        rows[j] = [v * inverse for v in rows[j]]
        for k in range(j + 1, 8):
            rows[k] = [v - column[k] * w for v, w in zip(rows[k], rows[j])]
    sub = lax.broadcasted_iota(jnp.int32, (8, 128), 0)
    lane = lax.broadcasted_iota(jnp.int32, (8, 128), 1)
    out = []
    for t in range(tiles):
        u = rows[7][t]
        for j in range(7):
            u = jnp.where(sub == j, rows[j][t], u)
        if t == 0:
            u = jnp.where(lane >= sub + r, u, 0.0)
        out.append(u)
    return jnp.concatenate(out, 1)


def unit(size):
    return (
        lax.broadcasted_iota(jnp.int32, (size, size), 0) == lax.broadcasted_iota(jnp.int32, (size, size), 1)
    ).astype(f32)


def factor_block(blocks, store):
    def panel(p, carry):
        r = pl.multiple_of(p * 8, 8)
        for leaf, block in enumerate(blocks):
            u = factor_panel(block, r)
            store(leaf, r, u)
            block[...] -= rank_update(u)
        return carry

    lax.fori_loop(0, HALF // 8, panel, 0)


def head_kernel(scalars, mine, theirs, window, u_head, x_head, rest, gram, s0, s1):
    xl, core, bound = scalars[1], scalars[2], scalars[3]
    count = mine.shape[0] // 2
    window_rows = mine.shape[2]
    for block in range(2 * count):
        start = block % count * 32 + (block // count ^ xl) * 16
        window[pl.ds(pl.multiple_of(start + core * 8, 8), 8), :] = mine[block]
        window[pl.ds(pl.multiple_of(start + (1 - core) * 8, 8), 8), :] = theirs[block]
    edge = window_rows // 2 + HALF
    lane = lax.broadcasted_iota(jnp.int32, (R, edge), 1)
    head = window[:, :edge]
    tail = window[:, window_rows - edge :]
    gram[0] = dot(jnp.where(lane < bound, head, 0.0), head, NT, highest)
    gram[1] = dot(jnp.where(lane + (window_rows - edge) < bound, 0.0, tail), tail, NT, highest)
    blocks = (s0, s1)
    for leaf in range(2):
        rows = jnp.where(leaf == 0, bound, window_rows - bound)
        count_rows = jnp.full((1, 1), rows, jnp.int32).astype(f32)
        gram[leaf] = gram[leaf] / count_rows
        blocks[leaf][:, :R] = gram[leaf, :HALF, :]
        blocks[leaf][:, R:] = unit(HALF)

    def store(leaf, r, u):
        u_head[leaf, pl.ds(r, 8), :] = u[:, :R]
        x_head[leaf, pl.ds(r, 8), :] = u[:, R:]

    factor_block(blocks, store)
    for leaf in range(2):
        side = u_head[leaf, :, HALF:]
        change = dot(side, jnp.concatenate([side, x_head[leaf]], 1), TN, highest)
        rest[leaf, :, :HALF] = gram[leaf, HALF:, HALF:] - change[:, :HALF]
        rest[leaf, :, HALF:] = -change[:, HALF:]


def factor_head(scalars, mine, theirs):
    window_rows = mine.shape[2]
    return pl.pallas_call(
        head_kernel,
        in_specs=[SMEM, VMEM, VMEM],
        out_specs=[VMEM] * 4,
        out_shape=[
            shape(R, window_rows),
            shape(2, HALF, R),
            shape(2, HALF, HALF),
            shape(2, HALF, R),
        ],
        scratch_shapes=[pltpu.VMEM((2, R, R), f32)] + [pltpu.VMEM((HALF, R + HALF), f32)] * 2,
        compiler_params=PARAMS,
    )(scalars, mine, theirs)


def tail_kernel(scalars, u_head, x_head, rest, u_tail, u_own, x_own, x_tail, s0, s1):
    group = scalars[4]
    blocks = (s0, s1)
    for leaf in range(2):
        blocks[leaf][:, :R] = rest[leaf]
        blocks[leaf][:, R:] = unit(HALF)

    def store(leaf, r, u):
        u_tail[leaf, pl.ds(r, 8), :] = u[:, :HALF]
        x_tail[leaf, pl.ds(r, 8), :] = u[:, HALF:]

    factor_block(blocks, store)
    start = pl.multiple_of(group % (HALF // 8) * 8, 8)
    in_head = group < HALF // 8
    for leaf in range(2):
        own = pl.ds(start, 8)
        zero = jnp.zeros((8, HALF), f32)
        u_own[leaf] = jnp.where(
            in_head, u_head[leaf, own, :], jnp.concatenate([zero, u_tail[leaf, own, :]], 1)
        )
        x_own[leaf] = jnp.where(
            in_head, jnp.concatenate([x_head[leaf, own, :], zero], 1), x_tail[leaf, own, :]
        )


def factor_tail(scalars, u_head, x_head, rest):
    return pl.pallas_call(
        tail_kernel,
        in_specs=[SMEM] + [VMEM] * 3,
        out_specs=[VMEM] * 3,
        out_shape=[shape(2, HALF, HALF), shape(2, 8, R), shape(2, 8, R)],
        scratch_shapes=[pltpu.VMEM((2, HALF, R), f32)] + [pltpu.VMEM((HALF, R + HALF), f32)] * 2,
        compiler_params=PARAMS,
        cost_estimate=pl.CostEstimate(flops=8 * 10**9, bytes_accessed=10**6, transcendentals=0),
    )(scalars, u_head, x_head, rest)


def bases_kernel(scalars, window, x_own, out):
    both = jnp.concatenate([x_own[0], x_own[1]], 0)
    solved = dot(both, window[...], (((1,), (0,)), ((), ())), highest)
    lane = lax.broadcasted_iota(jnp.int32, out.shape, 1)
    out[...] = jnp.where(lane < scalars[3], solved[:8], solved[8:])


def coupling_kernel(u_own, sib_head, sib_tail, out):
    for leaf in range(2):
        own = u_own[leaf]
        out[leaf, :, :HALF] = dot(own, sib_head[leaf], NT, highest)
        out[leaf, :, HALF:] = dot(own[:, HALF:], sib_tail[leaf], NT, highest)


def local(contrib, assembled, pattern, omega, row_maps, leaf_bounds):
    tile_rows, tile_cols = contrib.shape[1:]
    window_rows, own_count = omega.shape
    z_count = lax.axis_size("z")
    groups = lax.axis_size("child") * lax.axis_size("y")
    width = R // (2 * groups)
    child = lax.axis_index("child")
    row_pos = lax.axis_index(("z", "xl"))
    col_pos = lax.axis_index(("y", "core"))
    columns = lax.dynamic_slice_in_dim(row_maps, col_pos * tile_cols, tile_cols, 1) - col_pos * window_rows
    targets = lax.dynamic_slice_in_dim(row_maps, row_pos * tile_rows, tile_rows, 1) - row_pos * window_rows
    scalars = jnp.stack(
        [
            child,
            lax.axis_index("xl"),
            lax.axis_index("core"),
            leaf_bounds[0],
            lax.axis_index(("child", "y", "core")),
        ]
    ).astype(jnp.int32)

    own = lax.all_to_all(jnp.broadcast_to(omega.T, (z_count, own_count, window_rows)), "z", 0, 0)
    top, low = build_operator(scalars, pattern, contrib[0], assembled[0], columns, targets)
    other = lax.ppermute(own, "xl", SWAP)

    def half(gathered):
        give, keep = apply_operator(scalars, gathered, top, low)
        return keep + lax.ppermute(give, "core", SWAP)

    parts = jnp.concatenate([half(own), half(other)], axis=0)
    terms = lax.all_to_all(parts, ("child", "y"), 0, 0)
    samples = jnp.sum(terms, axis=0)
    mine = lax.all_to_all(
        jnp.broadcast_to(samples, (groups, width, window_rows)), ("child", "y"), 0, 0
    )
    theirs = lax.ppermute(mine, "core", SWAP)

    window, u_head, x_head, rest = factor_head(scalars, mine, theirs)
    sib_head = lax.ppermute(u_head, "xl", SWAP)
    u_tail, u_own, x_own = factor_tail(scalars, u_head, x_head, rest)
    sib_tail = lax.ppermute(u_tail, "xl", SWAP)
    bases = pl.pallas_call(
        bases_kernel,
        in_specs=[SMEM, VMEM, VMEM],
        out_specs=VMEM,
        out_shape=shape(width, window_rows),
        compiler_params=PARAMS,
        cost_estimate=pl.CostEstimate(flops=10**9, bytes_accessed=10**6, transcendentals=0),
    )(scalars, window, x_own)
    coupling = pl.pallas_call(
        coupling_kernel,
        in_specs=[VMEM] * 3,
        out_specs=VMEM,
        out_shape=shape(2, width, R),
        compiler_params=PARAMS,
    )(u_own, sib_head, sib_tail)
    return (bases.T, coupling[None])


def solution(mesh):
    fine = Mesh(mesh.devices.reshape(2, 8, 2, 8, 2), ("child", "z", "xl", "y", "core"))
    row, col = ("z", "xl"), ("y", "core")
    in_specs = (
        P("child", row, col),
        P("child", row, col),
        P(row, col),
        P(col, row),
        P("child", None),
        P(row),
    )
    out_specs = (P(row, ("child",) + col), P(row, None, ("child",) + col, None))
    return jax.shard_map(local, mesh=fine, in_specs=in_specs, out_specs=out_specs, check_vma=False)
```

```python
import jax
import jax.numpy as jnp
from jax import lax
from jax.experimental import pallas as pl
from jax.experimental.pallas import tpu as pltpu
from jax.sharding import Mesh, PartitionSpec as P

R = 256
BT = 256
HALF = 128

f32, bf16 = jnp.float32, jnp.bfloat16
highest = lax.Precision.HIGHEST
SWAP = [(0, 1), (1, 0)]
NN = (((1,), (0,)), ((), ()))
NT = (((1,), (1,)), ((), ()))
TN = (((0,), (0,)), ((), ()))
VMEM = pl.BlockSpec(memory_space=pltpu.VMEM)
SMEM = pl.BlockSpec(memory_space=pltpu.SMEM)
PARAMS = pltpu.CompilerParams(vmem_limit_bytes=16 << 20)


def shape(*sizes, dtype=f32):
    return jax.ShapeDtypeStruct(sizes, dtype)


def dot(a, b, dims, precision=None):
    return lax.dot_general(a, b, dims, precision=precision, preferred_element_type=f32)


def two_parts(a):
    top = a.astype(bf16)
    return top, (a - top.astype(f32)).astype(bf16)


def operator_kernel(scalars, pattern, contrib, assembled, columns, targets, top, low, built, c_top, c_low, spread):
    step = pl.program_id(0)
    child = scalars[0]
    rows = top.shape[0]
    tile_rows, tile_cols = contrib.shape

    @pl.when(step == 0)
    def _():
        c_top[...], c_low[...] = two_parts(contrib[...])
        places = lax.broadcasted_iota(jnp.int32, spread.shape, 0)
        spread[...] = (places == targets[...]).astype(f32).astype(bf16)
        built[...] = jnp.zeros_like(built)

    places = lax.broadcasted_iota(jnp.int32, (rows, tile_cols), 0) + step * rows
    pick = (places == columns[...]).astype(f32).astype(bf16)
    high_rows = dot(pick, c_top[...], NT).astype(bf16)
    low_rows = dot(pick, c_low[...], NT).astype(bf16)
    total = dot(high_rows, spread[...], NT) + dot(low_rows, spread[...], NT)
    tiles = tile_rows // BT
    for half in range(2):
        here = (child == half).astype(f32)
        for tile in range(tiles):
            keep = pattern[half * tiles + tile, step].astype(f32) * here
            lanes = slice(half * tile_rows + tile * BT, half * tile_rows + (tile + 1) * BT)
            entries = assembled[tile * BT : (tile + 1) * BT, :].T
            top[:, lanes], low[:, lanes] = two_parts(total[:, lanes] + entries * keep)


def build_operator(scalars, pattern, contrib, assembled, columns, targets):
    tile_rows, tile_cols = contrib.shape
    window_rows = assembled.shape[1]
    block = pl.BlockSpec((BT, window_rows), lambda i: (i, 0))
    return pl.pallas_call(
        operator_kernel,
        grid=(window_rows // BT,),
        in_specs=[
            SMEM,
            SMEM,
            pl.BlockSpec((tile_rows, tile_cols), lambda i: (0, 0)),
            pl.BlockSpec((tile_rows, BT), lambda i: (0, i)),
            pl.BlockSpec((1, tile_cols), lambda i: (0, 0)),
            pl.BlockSpec((1, tile_rows), lambda i: (0, 0)),
        ],
        out_specs=[block, block, pl.BlockSpec((8, 128), lambda i: (0, 0))],
        out_shape=[shape(window_rows, window_rows, dtype=bf16)] * 2 + [shape(8, 128)],
        scratch_shapes=[
            pltpu.VMEM((tile_rows, tile_cols), bf16),
            pltpu.VMEM((tile_rows, tile_cols), bf16),
            pltpu.VMEM((window_rows, tile_rows), bf16),
        ],
        compiler_params=PARAMS,
        cost_estimate=pl.CostEstimate(flops=4 * 10**9, bytes_accessed=8 * 10**6, transcendentals=0),
    )(scalars, pattern, contrib, assembled, columns, targets)


def apply_kernel(scalars, built, lines, top, low, give, keep):
    core = scalars[2]
    count, _, width, depth = lines.shape
    rows = count * width
    ordered = jnp.concatenate(
        [lines[:, pl.ds(1 - core, 1)].reshape(rows, depth), lines[:, pl.ds(core, 1)].reshape(rows, depth)]
    )
    high_lines, low_lines = two_parts(ordered)
    both = jnp.concatenate([high_lines, low_lines])
    for tile in range(top.shape[1] // BT):
        lanes = slice(tile * BT, (tile + 1) * BT)
        wide = dot(both, top[:, lanes], NN)
        out = wide[: 2 * rows] + wide[2 * rows :] + dot(high_lines, low[:, lanes], NN)
        give[:, :, lanes] = out[:rows].reshape(count, width, BT)
        keep[:, :, lanes] = out[rows:].reshape(count, width, BT)


def apply_operator(scalars, built, gathered, top, low):
    count, both, depth = gathered.shape
    width = both // 2
    window_rows = top.shape[1]
    lines = gathered.reshape(count, 2, width, depth)
    return pl.pallas_call(
        apply_kernel,
        in_specs=[SMEM, VMEM, VMEM, VMEM, VMEM],
        out_specs=[VMEM, VMEM],
        out_shape=[shape(count, width, window_rows)] * 2,
        compiler_params=PARAMS,
        cost_estimate=pl.CostEstimate(flops=10**9, bytes_accessed=6 * 10**6, transcendentals=0),
    )(scalars, built, lines, top, low)


def spread_out(row_or_column):
    return jnp.broadcast_to(row_or_column, (8, 128))


def lane_tiles(a):
    return [a[:, t : t + 128] for t in range(0, a.shape[1], 128)]


def rank_update(block, u, start):
    a = u.astype(bf16).astype(f32)
    b = (u - a).astype(bf16).astype(f32)
    c = u - a - b
    left = jnp.concatenate([v[:, :HALF] for v in (a, a, b, b, a, c)], 0).T[start:].astype(bf16)
    right = jnp.concatenate([a, b, a, b, c, a], 0).astype(bf16)
    block[start:, :] -= dot(left, right, NN)


def factor_panel(panel, upcoming, r):
    sub = lax.broadcasted_iota(jnp.int32, (8, 128), 0)
    lane = lax.broadcasted_iota(jnp.int32, (8, 128), 1)
    rows = lane_tiles(panel)
    columns = [spread_out(rows[0][:, r + j : r + j + 1]) for j in range(8)]
    solved = []
    for j in range(8):
        inverse = lax.rsqrt(spread_out(columns[j][j : j + 1]))
        column = columns[j] * inverse
        solved.append([spread_out(v[j : j + 1]) * inverse for v in rows])
        below = jnp.where(sub > j, column, 0.0)
        rows = [v - below * w for v, w in zip(rows, solved[j])]
        for k in range(j + 1, 8):
            columns[k] = columns[k] - column * spread_out(column[k : k + 1])
    if upcoming is not None:
        after = lane_tiles(upcoming)
        pick = lane == sub + (r + 8)
        for j in range(8):
            column = spread_out(jnp.sum(jnp.where(pick, solved[j][0], 0.0), axis=1, keepdims=True))
            after = [v - column * w for v, w in zip(after, solved[j])]
        upcoming = jnp.concatenate(after, 1)
    out = []
    for t in range(len(rows)):
        u = solved[7][t]
        for j in range(7):
            u = jnp.where(sub == j, solved[j][t], u)
        if t == 0:
            u = jnp.where(lane >= sub + r, u, 0.0)
        out.append(u)
    return jnp.concatenate(out, 1), upcoming


def unit(size):
    return (
        lax.broadcasted_iota(jnp.int32, (size, size), 0) == lax.broadcasted_iota(jnp.int32, (size, size), 1)
    ).astype(f32)


def factor_block(blocks, store):
    panels = [block[:8, :] for block in blocks]
    found = [None] * len(blocks)
    for r in range(0, HALF, 8):
        for leaf, block in enumerate(blocks):
            start = (r + 8) // 16 * 16
            if found[leaf] is not None and start < HALF:
                rank_update(block, found[leaf], start)
        for leaf, block in enumerate(blocks):
            upcoming = block[r + 8 : r + 16, :] if r + 8 < HALF else None
            found[leaf], panels[leaf] = factor_panel(panels[leaf], upcoming, r)
            store(leaf, r, found[leaf])


def head_kernel(scalars, mine, theirs, window, u_head, x_head, rest, gram, s0, s1):
    xl, core, bound = scalars[1], scalars[2], scalars[3]
    count = mine.shape[0] // 2
    window_rows = mine.shape[2]
    for block in range(2 * count):
        start = block % count * 32 + (block // count ^ xl) * 16
        window[pl.ds(pl.multiple_of(start + core * 8, 8), 8), :] = mine[block]
        window[pl.ds(pl.multiple_of(start + (1 - core) * 8, 8), 8), :] = theirs[block]
    edge = window_rows // 2 + HALF
    lane = lax.broadcasted_iota(jnp.int32, (R, edge), 1)
    head = window[:, :edge]
    tail = window[:, window_rows - edge :]
    gram[0] = dot(jnp.where(lane < bound, head, 0.0), head, NT, highest)
    gram[1] = dot(jnp.where(lane + (window_rows - edge) < bound, 0.0, tail), tail, NT, highest)
    blocks = (s0, s1)
    for leaf in range(2):
        rows = jnp.where(leaf == 0, bound, window_rows - bound)
        count_rows = jnp.full((1, 1), rows, jnp.int32).astype(f32)
        gram[leaf] = gram[leaf] / count_rows
        blocks[leaf][:, :R] = gram[leaf, :HALF, :]
        blocks[leaf][:, R:] = unit(HALF)

    def store(leaf, r, u):
        u_head[leaf, r : r + 8, :] = u[:, :R]
        x_head[leaf, r : r + 8, :] = u[:, R:]

    factor_block(blocks, store)
    for leaf in range(2):
        side = u_head[leaf, :, HALF:]
        change = dot(side, jnp.concatenate([side, x_head[leaf]], 1), TN, highest)
        rest[leaf, :, :HALF] = gram[leaf, HALF:, HALF:] - change[:, :HALF]
        rest[leaf, :, HALF:] = -change[:, HALF:]


def factor_head(scalars, mine, theirs):
    window_rows = mine.shape[2]
    return pl.pallas_call(
        head_kernel,
        in_specs=[SMEM, VMEM, VMEM],
        out_specs=[VMEM] * 4,
        out_shape=[
            shape(R, window_rows),
            shape(2, HALF, R),
            shape(2, HALF, HALF),
            shape(2, HALF, R),
        ],
        scratch_shapes=[pltpu.VMEM((2, R, R), f32)] + [pltpu.VMEM((HALF, R + HALF), f32)] * 2,
        compiler_params=PARAMS,
    )(scalars, mine, theirs)


def tail_kernel(scalars, u_head, x_head, rest, u_tail, u_own, x_own, x_tail, s0, s1):
    group = scalars[4]
    blocks = (s0, s1)
    for leaf in range(2):
        blocks[leaf][:, :R] = rest[leaf]
        blocks[leaf][:, R:] = unit(HALF)

    def store(leaf, r, u):
        u_tail[leaf, r : r + 8, :] = u[:, :HALF]
        x_tail[leaf, r : r + 8, :] = u[:, HALF:]

    factor_block(blocks, store)
    start = pl.multiple_of(group % (HALF // 8) * 8, 8)
    in_head = group < HALF // 8
    for leaf in range(2):
        own = pl.ds(start, 8)
        zero = jnp.zeros((8, HALF), f32)
        u_own[leaf] = jnp.where(
            in_head, u_head[leaf, own, :], jnp.concatenate([zero, u_tail[leaf, own, :]], 1)
        )
        x_own[leaf] = jnp.where(
            in_head, jnp.concatenate([x_head[leaf, own, :], zero], 1), x_tail[leaf, own, :]
        )


def factor_tail(scalars, u_head, x_head, rest):
    return pl.pallas_call(
        tail_kernel,
        in_specs=[SMEM] + [VMEM] * 3,
        out_specs=[VMEM] * 3,
        out_shape=[shape(2, HALF, HALF), shape(2, 8, R), shape(2, 8, R)],
        scratch_shapes=[pltpu.VMEM((2, HALF, R), f32)] + [pltpu.VMEM((HALF, R + HALF), f32)] * 2,
        compiler_params=PARAMS,
        cost_estimate=pl.CostEstimate(flops=8 * 10**9, bytes_accessed=10**6, transcendentals=0),
    )(scalars, u_head, x_head, rest)


def bases_kernel(scalars, window, x_own, out):
    both = jnp.concatenate([x_own[0], x_own[1]], 0)
    solved = dot(both, window[...], NN, highest)
    lane = lax.broadcasted_iota(jnp.int32, out.shape, 1)
    out[...] = jnp.where(lane < scalars[3], solved[:8], solved[8:])


def coupling_kernel(u_own, sib_head, sib_tail, out):
    for leaf in range(2):
        own = u_own[leaf]
        out[leaf, :, :HALF] = dot(own, sib_head[leaf], NT, highest)
        out[leaf, :, HALF:] = dot(own[:, HALF:], sib_tail[leaf], NT, highest)


def local(contrib, assembled, pattern, omega, row_maps, leaf_bounds):
    tile_rows, tile_cols = contrib.shape[1:]
    window_rows, own_count = omega.shape
    z_count = lax.axis_size("z")
    groups = lax.axis_size("child") * lax.axis_size("y")
    width = R // (2 * groups)
    child = lax.axis_index("child")
    row_pos = lax.axis_index(("z", "xl"))
    col_pos = lax.axis_index(("y", "core"))
    columns = lax.dynamic_slice_in_dim(row_maps, col_pos * tile_cols, tile_cols, 1) - col_pos * window_rows
    targets = lax.dynamic_slice_in_dim(row_maps, row_pos * tile_rows, tile_rows, 1) - row_pos * window_rows
    scalars = jnp.stack(
        [
            child,
            lax.axis_index("xl"),
            lax.axis_index("core"),
            leaf_bounds[0],
            lax.axis_index(("child", "y", "core")),
        ]
    ).astype(jnp.int32)

    own = lax.all_to_all(jnp.broadcast_to(omega.T, (z_count, own_count, window_rows)), "z", 0, 0)
    top, low, built = build_operator(scalars, pattern, contrib[0], assembled[0], columns, targets)
    own, built = lax.optimization_barrier((own, built))
    other = lax.ppermute(own, "xl", SWAP)

    def half(gathered):
        give, keep = apply_operator(scalars, built, gathered, top, low)
        return keep + lax.ppermute(give, "core", SWAP)

    parts = jnp.concatenate([half(own), half(other)], axis=0)
    terms = lax.all_to_all(parts, ("child", "y"), 0, 0)
    samples = jnp.sum(terms, axis=0)
    mine = lax.all_to_all(
        jnp.broadcast_to(samples, (groups, width, window_rows)), ("child", "y"), 0, 0
    )
    theirs = lax.ppermute(mine, "core", SWAP)

    window, u_head, x_head, rest = factor_head(scalars, mine, theirs)
    sib_head = lax.ppermute(u_head, "xl", SWAP)
    u_tail, u_own, x_own = factor_tail(scalars, u_head, x_head, rest)
    sib_tail = lax.ppermute(u_tail, "xl", SWAP)
    bases = pl.pallas_call(
        bases_kernel,
        in_specs=[SMEM, VMEM, VMEM],
        out_specs=VMEM,
        out_shape=shape(width, window_rows),
        compiler_params=PARAMS,
        cost_estimate=pl.CostEstimate(flops=10**9, bytes_accessed=10**6, transcendentals=0),
    )(scalars, window, x_own)
    coupling = pl.pallas_call(
        coupling_kernel,
        in_specs=[VMEM] * 3,
        out_specs=VMEM,
        out_shape=shape(2, width, R),
        compiler_params=PARAMS,
    )(u_own, sib_head, sib_tail)
    return (bases.T, coupling[None])


def solution(mesh):
    fine = Mesh(mesh.devices.reshape(2, 8, 2, 8, 2), ("child", "z", "xl", "y", "core"))
    row, col = ("z", "xl"), ("y", "core")
    in_specs = (
        P("child", row, col),
        P("child", row, col),
        P(row, col),
        P(col, row),
        P("child", None),
        P(row),
    )
    out_specs = (P(row, ("child",) + col), P(row, None, ("child",) + col, None))
    return jax.shard_map(local, mesh=fine, in_specs=in_specs, out_specs=out_specs, check_vma=False)
```

```python
import jax
import jax.numpy as jnp
from jax import lax
from jax.experimental import pallas as pl
from jax.experimental.pallas import tpu as pltpu
from jax.sharding import Mesh, PartitionSpec as P

R = 256
BT = 256
HALF = 128

f32, bf16 = jnp.float32, jnp.bfloat16
highest = lax.Precision.HIGHEST
SWAP = [(0, 1), (1, 0)]
NN = (((1,), (0,)), ((), ()))
NT = (((1,), (1,)), ((), ()))
TN = (((0,), (0,)), ((), ()))
VMEM = pl.BlockSpec(memory_space=pltpu.VMEM)
SMEM = pl.BlockSpec(memory_space=pltpu.SMEM)
PARAMS = pltpu.CompilerParams(vmem_limit_bytes=16 << 20)


def shape(*sizes, dtype=f32):
    return jax.ShapeDtypeStruct(sizes, dtype)


def dot(a, b, dims, precision=None):
    return lax.dot_general(a, b, dims, precision=precision, preferred_element_type=f32)


def two_parts(a):
    top = a.astype(bf16)
    return top, (a - top.astype(f32)).astype(bf16)


def copies_kernel(lines, out):
    for copy in range(out.shape[0]):
        out[copy] = lines[...]


def operator_kernel(scalars, pattern, own, sibling, assembled, columns, targets, top, low, built, parts, spread):
    step = pl.program_id(0)
    child = scalars[0]
    rows, half_rows = top.shape
    tile_cols = own.shape[1]

    @pl.when(step == 0)
    def _():
        places = lax.broadcasted_iota(jnp.int32, (half_rows, targets.shape[1]), 0) + child * half_rows
        for source, block in enumerate((own, sibling)):
            parts[source, 0], parts[source, 1] = two_parts(block[...])
            spread[source] = (places == targets[source : source + 1, :]).astype(f32).astype(bf16)
        built[...] = jnp.zeros_like(built)

    places = lax.broadcasted_iota(jnp.int32, (rows, tile_cols), 0) + step * rows
    total = jnp.zeros((rows, half_rows), f32)
    for source in range(2):
        pick = (places == columns[source : source + 1, :]).astype(f32).astype(bf16)
        for part in range(2):
            picked = dot(pick, parts[source, part], NT).astype(bf16)
            total = total + dot(picked, spread[source], NT)
    tiles = half_rows // BT
    for tile in range(tiles):
        keep = pattern[child * tiles + tile, step].astype(f32)
        lanes = slice(tile * BT, (tile + 1) * BT)
        entries = assembled[lanes, :].T
        top[:, lanes], low[:, lanes] = two_parts(total[:, lanes] + entries * keep)


def build_operator(scalars, pattern, own, sibling, assembled, columns, targets):
    tile_rows, tile_cols = own.shape
    window_rows = assembled.shape[1]
    half_rows = assembled.shape[0]
    block = pl.BlockSpec((BT, half_rows), lambda i: (i, 0))
    whole = pl.BlockSpec((tile_rows, tile_cols), lambda i: (0, 0))
    return pl.pallas_call(
        operator_kernel,
        grid=(window_rows // BT,),
        in_specs=[
            SMEM,
            SMEM,
            whole,
            whole,
            pl.BlockSpec((half_rows, BT), lambda i: (0, i)),
            pl.BlockSpec((2, tile_cols), lambda i: (0, 0)),
            pl.BlockSpec((2, tile_rows), lambda i: (0, 0)),
        ],
        out_specs=[block, block, pl.BlockSpec((8, 128), lambda i: (0, 0))],
        out_shape=[shape(window_rows, half_rows, dtype=bf16)] * 2 + [shape(8, 128)],
        scratch_shapes=[
            pltpu.VMEM((2, 2, tile_rows, tile_cols), bf16),
            pltpu.VMEM((2, half_rows, tile_rows), bf16),
        ],
        compiler_params=PARAMS,
        cost_estimate=pl.CostEstimate(flops=4 * 10**9, bytes_accessed=8 * 10**6, transcendentals=0),
    )(scalars, pattern, own, sibling, assembled, columns, targets)


def apply_kernel(scalars, built, *refs):
    *pieces, top, low, give, keep = refs
    core = scalars[2]
    count, width, _ = give.shape
    depth = top.shape[0]
    rows = count * width
    ordered = jnp.concatenate(
        [
            piece[:, pl.ds(side, 1)].reshape(-1, depth)
            for side in (1 - core, core)
            for piece in pieces
        ]
    )
    high_lines, low_lines = two_parts(ordered)
    both = jnp.concatenate([high_lines, low_lines])
    for tile in range(top.shape[1] // BT):
        lanes = slice(tile * BT, (tile + 1) * BT)
        wide = dot(both, top[:, lanes], NN)
        out = wide[: 2 * rows] + wide[2 * rows :] + dot(high_lines, low[:, lanes], NN)
        give[:, :, lanes] = out[:rows].reshape(count, width, BT)
        keep[:, :, lanes] = out[rows:].reshape(count, width, BT)


def apply_operator(scalars, built, pieces, top, low):
    count = sum(piece.shape[0] for piece in pieces)
    width = pieces[0].shape[1] // 2
    depth, half_rows = top.shape
    lines = [piece.reshape(piece.shape[0], 2, width, depth) for piece in pieces]
    return pl.pallas_call(
        apply_kernel,
        in_specs=[SMEM] + [VMEM] * (3 + len(lines)),
        out_specs=[VMEM, VMEM],
        out_shape=[shape(count, width, half_rows)] * 2,
        compiler_params=PARAMS,
        cost_estimate=pl.CostEstimate(flops=10**9, bytes_accessed=6 * 10**6, transcendentals=0),
    )(scalars, built, *lines, top, low)


def spread_out(row_or_column):
    return jnp.broadcast_to(row_or_column, (8, 128))


def lane_tiles(a):
    return [a[:, t : t + 128] for t in range(0, a.shape[1], 128)]


def rank_update(block, u, start):
    a = u.astype(bf16).astype(f32)
    b = (u - a).astype(bf16).astype(f32)
    c = u - a - b
    left = jnp.concatenate([v[:, :HALF] for v in (a, a, b, b, a, c)], 0).T[start:].astype(bf16)
    right = jnp.concatenate([a, b, a, b, c, a], 0).astype(bf16)
    block[start:, :] -= dot(left, right, NN)


def factor_panel(panel, upcoming, r):
    sub = lax.broadcasted_iota(jnp.int32, (8, 128), 0)
    lane = lax.broadcasted_iota(jnp.int32, (8, 128), 1)
    rows = lane_tiles(panel)
    columns = [spread_out(rows[0][:, r + j : r + j + 1]) for j in range(8)]
    solved = []
    for j in range(8):
        inverse = lax.rsqrt(spread_out(columns[j][j : j + 1]))
        column = columns[j] * inverse
        solved.append([spread_out(v[j : j + 1]) * inverse for v in rows])
        below = jnp.where(sub > j, column, 0.0)
        rows = [v - below * w for v, w in zip(rows, solved[j])]
        for k in range(j + 1, 8):
            columns[k] = columns[k] - column * spread_out(column[k : k + 1])
    if upcoming is not None:
        after = lane_tiles(upcoming)
        pick = lane == sub + (r + 8)
        for j in range(8):
            column = spread_out(jnp.sum(jnp.where(pick, solved[j][0], 0.0), axis=1, keepdims=True))
            after = [v - column * w for v, w in zip(after, solved[j])]
        upcoming = jnp.concatenate(after, 1)
    out = []
    for t in range(len(rows)):
        u = solved[7][t]
        for j in range(7):
            u = jnp.where(sub == j, solved[j][t], u)
        if t == 0:
            u = jnp.where(lane >= sub + r, u, 0.0)
        out.append(u)
    return jnp.concatenate(out, 1), upcoming


def unit(size):
    return (
        lax.broadcasted_iota(jnp.int32, (size, size), 0) == lax.broadcasted_iota(jnp.int32, (size, size), 1)
    ).astype(f32)


def factor_block(blocks, store):
    panels = [block[:8, :] for block in blocks]
    found = [None] * len(blocks)
    for r in range(0, HALF, 8):
        for leaf, block in enumerate(blocks):
            start = (r + 8) // 16 * 16
            if found[leaf] is not None and start < HALF:
                rank_update(block, found[leaf], start)
        for leaf, block in enumerate(blocks):
            upcoming = block[r + 8 : r + 16, :] if r + 8 < HALF else None
            found[leaf], panels[leaf] = factor_panel(panels[leaf], upcoming, r)
            store(leaf, r, found[leaf])


def head_kernel(scalars, mine, theirs, window, u_head, x_head, rest, gram, s0, s1):
    xl, core, bound = scalars[1], scalars[2], scalars[3]
    count = mine.shape[0] // 2
    half_rows = mine.shape[2]
    window_rows = 2 * half_rows
    for block in range(2 * count):
        lanes = slice(block // count * half_rows, (block // count + 1) * half_rows)
        for side in range(2):
            start = block % count * 32 + (side ^ xl) * 16
            for source, at in ((mine, core), (theirs, 1 - core)):
                there = pl.ds(pl.multiple_of(start + at * 8, 8), 8)
                window[there, lanes] = source[block, side * 8 : side * 8 + 8, :]
    edge = window_rows // 2 + HALF
    lane = lax.broadcasted_iota(jnp.int32, (R, edge), 1)
    head = window[:, :edge]
    tail = window[:, window_rows - edge :]
    gram[0] = dot(jnp.where(lane < bound, head, 0.0), head, NT, highest)
    gram[1] = dot(jnp.where(lane + (window_rows - edge) < bound, 0.0, tail), tail, NT, highest)
    blocks = (s0, s1)
    for leaf in range(2):
        rows = jnp.where(leaf == 0, bound, window_rows - bound)
        count_rows = jnp.full((1, 1), rows, jnp.int32).astype(f32)
        gram[leaf] = gram[leaf] / count_rows
        blocks[leaf][:, :R] = gram[leaf, :HALF, :]
        blocks[leaf][:, R:] = unit(HALF)

    def store(leaf, r, u):
        u_head[leaf, r : r + 8, :] = u[:, :R]
        x_head[leaf, r : r + 8, :] = u[:, R:]

    factor_block(blocks, store)
    for leaf in range(2):
        side = u_head[leaf, :, HALF:]
        change = dot(side, jnp.concatenate([side, x_head[leaf]], 1), TN, highest)
        rest[leaf, :, :HALF] = gram[leaf, HALF:, HALF:] - change[:, :HALF]
        rest[leaf, :, HALF:] = -change[:, HALF:]


def factor_head(scalars, mine, theirs):
    window_rows = 2 * mine.shape[2]
    return pl.pallas_call(
        head_kernel,
        in_specs=[SMEM, VMEM, VMEM],
        out_specs=[VMEM] * 4,
        out_shape=[
            shape(R, window_rows),
            shape(2, HALF, R),
            shape(2, HALF, HALF),
            shape(2, HALF, R),
        ],
        scratch_shapes=[pltpu.VMEM((2, R, R), f32)] + [pltpu.VMEM((HALF, R + HALF), f32)] * 2,
        compiler_params=PARAMS,
    )(scalars, mine, theirs)


def tail_kernel(scalars, u_head, x_head, rest, u_tail, u_own, x_own, x_tail, s0, s1):
    group = scalars[4]
    blocks = (s0, s1)
    for leaf in range(2):
        blocks[leaf][:, :R] = rest[leaf]
        blocks[leaf][:, R:] = unit(HALF)

    def store(leaf, r, u):
        u_tail[leaf, r : r + 8, :] = u[:, :HALF]
        x_tail[leaf, r : r + 8, :] = u[:, HALF:]

    factor_block(blocks, store)
    start = pl.multiple_of(group % (HALF // 8) * 8, 8)
    in_head = group < HALF // 8
    for leaf in range(2):
        own = pl.ds(start, 8)
        zero = jnp.zeros((8, HALF), f32)
        u_own[leaf] = jnp.where(
            in_head, u_head[leaf, own, :], jnp.concatenate([zero, u_tail[leaf, own, :]], 1)
        )
        x_own[leaf] = jnp.where(
            in_head, jnp.concatenate([x_head[leaf, own, :], zero], 1), x_tail[leaf, own, :]
        )


def factor_tail(scalars, u_head, x_head, rest):
    return pl.pallas_call(
        tail_kernel,
        in_specs=[SMEM] + [VMEM] * 3,
        out_specs=[VMEM] * 3,
        out_shape=[shape(2, HALF, HALF), shape(2, 8, R), shape(2, 8, R)],
        scratch_shapes=[pltpu.VMEM((2, HALF, R), f32)] + [pltpu.VMEM((HALF, R + HALF), f32)] * 2,
        compiler_params=PARAMS,
        cost_estimate=pl.CostEstimate(flops=8 * 10**9, bytes_accessed=10**6, transcendentals=0),
    )(scalars, u_head, x_head, rest)


def bases_kernel(scalars, window, x_own, out):
    both = jnp.concatenate([x_own[0], x_own[1]], 0)
    solved = dot(both, window[...], NN, highest)
    lane = lax.broadcasted_iota(jnp.int32, out.shape, 1)
    out[...] = jnp.where(lane < scalars[3], solved[:8], solved[8:])


def coupling_kernel(u_own, sib_head, sib_tail, out):
    for leaf in range(2):
        own = u_own[leaf]
        out[leaf, :, :HALF] = dot(own, sib_head[leaf], NT, highest)
        out[leaf, :, HALF:] = dot(own[:, HALF:], sib_tail[leaf], NT, highest)


def local(contrib, assembled, pattern, omega, row_maps, leaf_bounds):
    tile_rows, tile_cols = contrib.shape[1:]
    window_rows, own_count = omega.shape
    half_rows = assembled.shape[1]
    z_count, y_count = lax.axis_size("z"), lax.axis_size("y")
    groups = lax.axis_size("child") * y_count
    width = R // (2 * groups)
    child = lax.axis_index("child")
    row_pos = lax.axis_index(("z", "xl"))
    col_pos = lax.axis_index(("y", "core"))
    sibling_block = lax.ppermute(contrib[0], "child", SWAP)
    columns = lax.dynamic_slice_in_dim(row_maps, col_pos * tile_cols, tile_cols, 1) - col_pos * window_rows
    targets = lax.dynamic_slice_in_dim(row_maps, row_pos * tile_rows, tile_rows, 1) - row_pos * window_rows
    maps = jnp.stack([columns, targets])
    sibling_maps = lax.ppermute(maps, "child", SWAP)
    scalars = jnp.stack(
        [
            child,
            lax.axis_index("xl"),
            lax.axis_index("core"),
            leaf_bounds[0],
            lax.axis_index(("child", "y", "core")),
        ]
    ).astype(jnp.int32)

    copies = pl.pallas_call(
        copies_kernel,
        in_specs=[VMEM],
        out_specs=VMEM,
        out_shape=shape(z_count, own_count, window_rows),
        compiler_params=PARAMS,
    )(omega.T)
    own = lax.all_to_all(copies, "z", 0, 0)
    both_maps = jnp.concatenate([maps, sibling_maps], axis=1)
    top, low, built = build_operator(
        scalars, pattern, contrib[0], sibling_block, assembled[0], both_maps[0], both_maps[1]
    )
    own, built = lax.optimization_barrier((own, built))
    ring = lax.axis_size("child") * lax.axis_size("xl")
    other = [
        lax.ppermute(piece, ("child", "xl"), [(i, (i + step) % ring) for i in range(ring)])
        for piece, step in ((own[: z_count // 2], 1), (own[z_count // 2 :], -1))
    ]

    def half(pieces):
        give, keep = apply_operator(scalars, built, pieces, top, low)
        return keep + lax.ppermute(give, "core", SWAP)

    parts = jnp.concatenate([half([own]), half(other)], axis=1)
    terms = lax.all_to_all(parts, "y", 0, 0)
    samples = jnp.sum(terms, axis=0)
    mine = lax.all_to_all(
        jnp.broadcast_to(samples, (groups,) + samples.shape), ("child", "y"), 0, 0
    )
    theirs = lax.ppermute(mine, "core", SWAP)

    window, u_head, x_head, rest = factor_head(scalars, mine, theirs)
    sib_head = lax.ppermute(u_head, "xl", SWAP)
    u_tail, u_own, x_own = factor_tail(scalars, u_head, x_head, rest)
    sib_tail = lax.ppermute(u_tail, "xl", SWAP)
    bases = pl.pallas_call(
        bases_kernel,
        in_specs=[SMEM, VMEM, VMEM],
        out_specs=VMEM,
        out_shape=shape(width, window_rows),
        compiler_params=PARAMS,
        cost_estimate=pl.CostEstimate(flops=10**9, bytes_accessed=10**6, transcendentals=0),
    )(scalars, window, x_own)
    coupling = pl.pallas_call(
        coupling_kernel,
        in_specs=[VMEM] * 3,
        out_specs=VMEM,
        out_shape=shape(2, width, R),
        compiler_params=PARAMS,
    )(u_own, sib_head, sib_tail)
    return (bases.T, coupling[None])


def solution(mesh):
    fine = Mesh(mesh.devices.reshape(2, 8, 2, 8, 2), ("child", "z", "xl", "y", "core"))
    row, col = ("z", "xl"), ("y", "core")
    in_specs = (
        P("child", row, col),
        P("child", row, col),
        P(row, col),
        P(col, row),
        P("child", None),
        P(row),
    )
    out_specs = (P(row, ("child",) + col), P(row, None, ("child",) + col, None))
    return jax.shard_map(local, mesh=fine, in_specs=in_specs, out_specs=out_specs, check_vma=False)
```

```python
import jax
import jax.numpy as jnp
from jax import lax
from jax.experimental import pallas as pl
from jax.experimental.pallas import tpu as pltpu
from jax.sharding import Mesh, PartitionSpec as P

R = 256
BT = 256
HALF = 128

f32, bf16 = jnp.float32, jnp.bfloat16
highest = lax.Precision.HIGHEST
SWAP = [(0, 1), (1, 0)]
NN = (((1,), (0,)), ((), ()))
NT = (((1,), (1,)), ((), ()))
TN = (((0,), (0,)), ((), ()))
VMEM = pl.BlockSpec(memory_space=pltpu.VMEM)
SMEM = pl.BlockSpec(memory_space=pltpu.SMEM)
PARAMS = pltpu.CompilerParams(vmem_limit_bytes=16 << 20)


def shape(*sizes, dtype=f32):
    return jax.ShapeDtypeStruct(sizes, dtype)


def dot(a, b, dims, precision=None):
    return lax.dot_general(a, b, dims, precision=precision, preferred_element_type=f32)


def two_parts(a):
    top = a.astype(bf16)
    return top, (a - top.astype(f32)).astype(bf16)


def copies_kernel(lines, out):
    for copy in range(out.shape[0]):
        out[copy] = lines[...]


def child_terms(child, block, targets, spread_rows, half_rows):
    places = lax.broadcasted_iota(jnp.int32, (half_rows, targets.shape[1]), 0) + child * half_rows
    spread = (places == targets[...]).astype(f32).astype(bf16)
    for part, piece in enumerate(two_parts(block[...])):
        spread_rows[part] = dot(spread, piece, NN).astype(bf16)


def picked_terms(columns, spread_rows, start, rows):
    places = lax.broadcasted_iota(jnp.int32, (rows, columns.shape[1]), 0) + start
    pick = (places == columns[...]).astype(f32).astype(bf16)
    return dot(pick, spread_rows[0], NT) + dot(pick, spread_rows[1], NT)


def own_kernel(scalars, pattern, block, assembled, columns, targets, total, built, spread_rows):
    child = scalars[0]
    window_rows, half_rows = total.shape
    child_terms(child, block, targets, spread_rows, half_rows)
    tiles = half_rows // BT
    for step in range(window_rows // BT):
        rows = slice(step * BT, (step + 1) * BT)
        terms = picked_terms(columns, spread_rows, step * BT, BT)
        for tile in range(tiles):
            keep = pattern[child * tiles + tile, step].astype(f32)
            lanes = slice(tile * BT, (tile + 1) * BT)
            total[rows, lanes] = terms[:, lanes] + assembled[lanes, rows].T * keep
    built[...] = jnp.zeros_like(built)


def sibling_kernel(scalars, own_total, block, maps, top, low, spread_rows, total, arrived):
    window_rows, half_rows = total.shape
    fetch = pltpu.make_async_copy(own_total, total, arrived)
    fetch.start()
    child_terms(scalars[0], block, maps.at[1], spread_rows, half_rows)
    fetch.wait()
    for step in range(window_rows // BT):
        rows = slice(step * BT, (step + 1) * BT)
        terms = picked_terms(maps.at[0], spread_rows, step * BT, BT)
        top[rows, :], low[rows, :] = two_parts(total[rows, :] + terms)


def own_operator(scalars, pattern, block, assembled, columns, targets):
    half_rows, window_rows = assembled.shape
    return pl.pallas_call(
        own_kernel,
        in_specs=[SMEM, SMEM] + [VMEM] * 4,
        out_specs=[VMEM, VMEM],
        out_shape=[shape(window_rows, half_rows), shape(8, 128)],
        scratch_shapes=[pltpu.VMEM((2, half_rows, block.shape[1]), bf16)],
        compiler_params=PARAMS,
        cost_estimate=pl.CostEstimate(flops=2 * 10**9, bytes_accessed=5 * 10**6, transcendentals=0),
    )(scalars, pattern, block, assembled, columns, targets)


def whole_operator(scalars, total, block, maps):
    window_rows, half_rows = total.shape
    return pl.pallas_call(
        sibling_kernel,
        in_specs=[SMEM, pl.BlockSpec(memory_space=pltpu.HBM)] + [VMEM] * 2,
        out_specs=[VMEM, VMEM],
        out_shape=[shape(window_rows, half_rows, dtype=bf16)] * 2,
        scratch_shapes=[
            pltpu.VMEM((2, half_rows, block.shape[1]), bf16),
            pltpu.VMEM((window_rows, half_rows), f32),
            pltpu.SemaphoreType.DMA,
        ],
        compiler_params=PARAMS,
        cost_estimate=pl.CostEstimate(flops=2 * 10**9, bytes_accessed=5 * 10**6, transcendentals=0),
    )(scalars, total, block, maps)


def apply_kernel(scalars, built, *refs):
    *pieces, top, low, give, keep = refs
    core = scalars[2]
    count, width, _ = give.shape
    depth = top.shape[0]
    rows = count * width
    ordered = jnp.concatenate(
        [
            piece[:, pl.ds(side, 1)].reshape(-1, depth)
            for side in (1 - core, core)
            for piece in pieces
        ]
    )
    high_lines, low_lines = two_parts(ordered)
    both = jnp.concatenate([high_lines, low_lines])
    for tile in range(top.shape[1] // BT):
        lanes = slice(tile * BT, (tile + 1) * BT)
        wide = dot(both, top[:, lanes], NN)
        out = wide[: 2 * rows] + wide[2 * rows :] + dot(high_lines, low[:, lanes], NN)
        give[:, :, lanes] = out[:rows].reshape(count, width, BT)
        keep[:, :, lanes] = out[rows:].reshape(count, width, BT)


def apply_operator(scalars, built, pieces, top, low):
    count = sum(piece.shape[0] for piece in pieces)
    width = pieces[0].shape[1] // 2
    depth, half_rows = top.shape
    lines = [piece.reshape(piece.shape[0], 2, width, depth) for piece in pieces]
    return pl.pallas_call(
        apply_kernel,
        in_specs=[SMEM] + [VMEM] * (3 + len(lines)),
        out_specs=[VMEM, VMEM],
        out_shape=[shape(count, width, half_rows)] * 2,
        compiler_params=PARAMS,
        cost_estimate=pl.CostEstimate(flops=10**9, bytes_accessed=6 * 10**6, transcendentals=0),
    )(scalars, built, *lines, top, low)


def spread_out(row_or_column):
    return jnp.broadcast_to(row_or_column, (8, 128))


def lane_tiles(a):
    return [a[:, t : t + 128] for t in range(0, a.shape[1], 128)]


def rank_update(block, u, start):
    a = u.astype(bf16).astype(f32)
    b = (u - a).astype(bf16).astype(f32)
    c = u - a - b
    left = jnp.concatenate([v[:, :HALF] for v in (a, a, b, b, a, c)], 0).T[start:].astype(bf16)
    right = jnp.concatenate([a, b, a, b, c, a], 0).astype(bf16)
    block[start:, :] -= dot(left, right, NN)


def factor_panel(panel, upcoming, r):
    sub = lax.broadcasted_iota(jnp.int32, (8, 128), 0)
    lane = lax.broadcasted_iota(jnp.int32, (8, 128), 1)
    rows = lane_tiles(panel)
    columns = [spread_out(rows[0][:, r + j : r + j + 1]) for j in range(8)]
    solved = []
    for j in range(8):
        inverse = lax.rsqrt(spread_out(columns[j][j : j + 1]))
        column = columns[j] * inverse
        solved.append([spread_out(v[j : j + 1]) * inverse for v in rows])
        below = jnp.where(sub > j, column, 0.0)
        rows = [v - below * w for v, w in zip(rows, solved[j])]
        for k in range(j + 1, 8):
            columns[k] = columns[k] - column * spread_out(column[k : k + 1])
    if upcoming is not None:
        after = lane_tiles(upcoming)
        pick = lane == sub + (r + 8)
        for j in range(8):
            column = spread_out(jnp.sum(jnp.where(pick, solved[j][0], 0.0), axis=1, keepdims=True))
            after = [v - column * w for v, w in zip(after, solved[j])]
        upcoming = jnp.concatenate(after, 1)
    out = []
    for t in range(len(rows)):
        u = solved[7][t]
        for j in range(7):
            u = jnp.where(sub == j, solved[j][t], u)
        if t == 0:
            u = jnp.where(lane >= sub + r, u, 0.0)
        out.append(u)
    return jnp.concatenate(out, 1), upcoming


def unit(size):
    return (
        lax.broadcasted_iota(jnp.int32, (size, size), 0) == lax.broadcasted_iota(jnp.int32, (size, size), 1)
    ).astype(f32)


def factor_block(blocks, store):
    panels = [block[:8, :] for block in blocks]
    found = [None] * len(blocks)
    for r in range(0, HALF, 8):
        for leaf, block in enumerate(blocks):
            start = (r + 8) // 16 * 16
            if found[leaf] is not None and start < HALF:
                rank_update(block, found[leaf], start)
        for leaf, block in enumerate(blocks):
            upcoming = block[r + 8 : r + 16, :] if r + 8 < HALF else None
            found[leaf], panels[leaf] = factor_panel(panels[leaf], upcoming, r)
            store(leaf, r, found[leaf])


def head_kernel(scalars, mine, theirs, window, u_head, x_head, rest, gram, s0, s1):
    xl, core, bound = scalars[1], scalars[2], scalars[3]
    count = mine.shape[0] // 2
    half_rows = mine.shape[2]
    window_rows = 2 * half_rows
    for block in range(2 * count):
        lanes = slice(block // count * half_rows, (block // count + 1) * half_rows)
        for side in range(2):
            start = block % count * 32 + (side ^ xl) * 16
            for source, at in ((mine, core), (theirs, 1 - core)):
                there = pl.ds(pl.multiple_of(start + at * 8, 8), 8)
                window[there, lanes] = source[block, side * 8 : side * 8 + 8, :]
    edge = window_rows // 2 + HALF
    lane = lax.broadcasted_iota(jnp.int32, (R, edge), 1)
    head = window[:, :edge]
    tail = window[:, window_rows - edge :]
    for leaf, (inside, leaf_rows) in enumerate(
        ((lane < bound, head), (lane + (window_rows - edge) >= bound, tail))
    ):
        high_rows, low_rows = two_parts(leaf_rows)
        masked = two_parts(jnp.where(inside, leaf_rows, 0.0))[0]
        cross = dot(masked, low_rows, NT)
        gram[leaf] = dot(masked, high_rows, NT) + cross + cross.T
    blocks = (s0, s1)
    for leaf in range(2):
        rows = jnp.where(leaf == 0, bound, window_rows - bound)
        count_rows = jnp.full((1, 1), rows, jnp.int32).astype(f32)
        gram[leaf] = gram[leaf] / count_rows
        blocks[leaf][:, :R] = gram[leaf, :HALF, :]
        blocks[leaf][:, R:] = unit(HALF)

    def store(leaf, r, u):
        u_head[leaf, r : r + 8, :] = u[:, :R]
        x_head[leaf, r : r + 8, :] = u[:, R:]

    factor_block(blocks, store)
    for leaf in range(2):
        side = u_head[leaf, :, HALF:]
        change = dot(side, jnp.concatenate([side, x_head[leaf]], 1), TN, highest)
        rest[leaf, :, :HALF] = gram[leaf, HALF:, HALF:] - change[:, :HALF]
        rest[leaf, :, HALF:] = -change[:, HALF:]


def factor_head(scalars, mine, theirs):
    window_rows = 2 * mine.shape[2]
    return pl.pallas_call(
        head_kernel,
        in_specs=[SMEM, VMEM, VMEM],
        out_specs=[VMEM] * 4,
        out_shape=[
            shape(R, window_rows),
            shape(2, HALF, R),
            shape(2, HALF, HALF),
            shape(2, HALF, R),
        ],
        scratch_shapes=[pltpu.VMEM((2, R, R), f32)] + [pltpu.VMEM((HALF, R + HALF), f32)] * 2,
        compiler_params=PARAMS,
    )(scalars, mine, theirs)


def tail_kernel(scalars, u_head, x_head, rest, u_tail, u_own, x_own, x_tail, s0, s1):
    group = scalars[4]
    blocks = (s0, s1)
    for leaf in range(2):
        blocks[leaf][:, :R] = rest[leaf]
        blocks[leaf][:, R:] = unit(HALF)

    def store(leaf, r, u):
        u_tail[leaf, r : r + 8, :] = u[:, :HALF]
        x_tail[leaf, r : r + 8, :] = u[:, HALF:]

    factor_block(blocks, store)
    start = pl.multiple_of(group % (HALF // 8) * 8, 8)
    in_head = group < HALF // 8
    for leaf in range(2):
        own = pl.ds(start, 8)
        zero = jnp.zeros((8, HALF), f32)
        u_own[leaf] = jnp.where(
            in_head, u_head[leaf, own, :], jnp.concatenate([zero, u_tail[leaf, own, :]], 1)
        )
        x_own[leaf] = jnp.where(
            in_head, jnp.concatenate([x_head[leaf, own, :], zero], 1), x_tail[leaf, own, :]
        )


def factor_tail(scalars, u_head, x_head, rest):
    return pl.pallas_call(
        tail_kernel,
        in_specs=[SMEM] + [VMEM] * 3,
        out_specs=[VMEM] * 3,
        out_shape=[shape(2, HALF, HALF), shape(2, 8, R), shape(2, 8, R)],
        scratch_shapes=[pltpu.VMEM((2, HALF, R), f32)] + [pltpu.VMEM((HALF, R + HALF), f32)] * 2,
        compiler_params=PARAMS,
        cost_estimate=pl.CostEstimate(flops=8 * 10**9, bytes_accessed=10**6, transcendentals=0),
    )(scalars, u_head, x_head, rest)


def bases_kernel(scalars, window, x_own, out):
    both = jnp.concatenate([x_own[0], x_own[1]], 0)
    solved = dot(both, window[...], NN, highest)
    lane = lax.broadcasted_iota(jnp.int32, out.shape, 1)
    out[...] = jnp.where(lane < scalars[3], solved[:8], solved[8:])


def coupling_kernel(u_own, sib_head, sib_tail, out):
    for leaf in range(2):
        own = u_own[leaf]
        out[leaf, :, :HALF] = dot(own, sib_head[leaf], NT, highest)
        out[leaf, :, HALF:] = dot(own[:, HALF:], sib_tail[leaf], NT, highest)


def local(contrib, assembled, pattern, omega, row_maps, leaf_bounds):
    tile_rows, tile_cols = contrib.shape[1:]
    window_rows, own_count = omega.shape
    half_rows = assembled.shape[1]
    z_count, y_count = lax.axis_size("z"), lax.axis_size("y")
    groups = lax.axis_size("child") * y_count
    width = R // (2 * groups)
    child = lax.axis_index("child")
    row_pos = lax.axis_index(("z", "xl"))
    col_pos = lax.axis_index(("y", "core"))
    sibling_block = lax.ppermute(contrib[0], "child", SWAP)
    columns = lax.dynamic_slice_in_dim(row_maps, col_pos * tile_cols, tile_cols, 1) - col_pos * window_rows
    targets = lax.dynamic_slice_in_dim(row_maps, row_pos * tile_rows, tile_rows, 1) - row_pos * window_rows
    maps = jnp.stack([columns, targets])
    sibling_maps = lax.ppermute(maps, "child", SWAP)
    scalars = jnp.stack(
        [
            child,
            lax.axis_index("xl"),
            lax.axis_index("core"),
            leaf_bounds[0],
            lax.axis_index(("child", "y", "core")),
        ]
    ).astype(jnp.int32)

    copies = pl.pallas_call(
        copies_kernel,
        in_specs=[VMEM],
        out_specs=VMEM,
        out_shape=shape(z_count, own_count, window_rows),
        compiler_params=PARAMS,
    )(omega.T)
    own = lax.all_to_all(copies, "z", 0, 0)
    total, built = own_operator(scalars, pattern, contrib[0], assembled[0], columns, targets)
    own, built = lax.optimization_barrier((own, built))
    ring = lax.axis_size("child") * lax.axis_size("xl")
    other = [
        lax.ppermute(piece, ("child", "xl"), [(i, (i + step) % ring) for i in range(ring)])
        for piece, step in ((own[: z_count // 2], 1), (own[z_count // 2 :], -1))
    ]

    sibling_block, sibling_maps = lax.optimization_barrier((sibling_block, sibling_maps))
    top, low = whole_operator(scalars, total, sibling_block, sibling_maps)

    def half(pieces):
        give, keep = apply_operator(scalars, built, pieces, top, low)
        return keep + lax.ppermute(give, "core", SWAP)

    parts = jnp.concatenate([half([own]), half(other)], axis=1)
    terms = lax.all_to_all(parts, "y", 0, 0)
    samples = jnp.sum(terms, axis=0)
    mine = lax.all_to_all(
        jnp.broadcast_to(samples, (groups,) + samples.shape), ("child", "y"), 0, 0
    )
    theirs = lax.ppermute(mine, "core", SWAP)

    window, u_head, x_head, rest = factor_head(scalars, mine, theirs)
    sib_head = lax.ppermute(u_head, "xl", SWAP)
    u_tail, u_own, x_own = factor_tail(scalars, u_head, x_head, rest)
    sib_tail = lax.ppermute(u_tail, "xl", SWAP)
    bases = pl.pallas_call(
        bases_kernel,
        in_specs=[SMEM, VMEM, VMEM],
        out_specs=VMEM,
        out_shape=shape(width, window_rows),
        compiler_params=PARAMS,
        cost_estimate=pl.CostEstimate(flops=10**9, bytes_accessed=10**6, transcendentals=0),
    )(scalars, window, x_own)
    coupling = pl.pallas_call(
        coupling_kernel,
        in_specs=[VMEM] * 3,
        out_specs=VMEM,
        out_shape=shape(2, width, R),
        compiler_params=PARAMS,
    )(u_own, sib_head, sib_tail)
    return (bases.T, coupling[None])


def solution(mesh):
    fine = Mesh(mesh.devices.reshape(2, 8, 2, 8, 2), ("child", "z", "xl", "y", "core"))
    row, col = ("z", "xl"), ("y", "core")
    in_specs = (
        P("child", row, col),
        P("child", row, col),
        P(row, col),
        P(col, row),
        P("child", None),
        P(row),
    )
    out_specs = (P(row, ("child",) + col), P(row, None, ("child",) + col, None))
    return jax.shard_map(local, mesh=fine, in_specs=in_specs, out_specs=out_specs, check_vma=False)
```

```python
import jax
import jax.numpy as jnp
from jax import lax
from jax.experimental import pallas as pl
from jax.experimental.pallas import tpu as pltpu
from jax.sharding import Mesh, PartitionSpec as P

R = 256
BT = 256
HALF = 128

f32, bf16 = jnp.float32, jnp.bfloat16
highest = lax.Precision.HIGHEST
SWAP = [(0, 1), (1, 0)]
NN = (((1,), (0,)), ((), ()))
NT = (((1,), (1,)), ((), ()))
TN = (((0,), (0,)), ((), ()))
VMEM = pl.BlockSpec(memory_space=pltpu.VMEM)
SMEM = pl.BlockSpec(memory_space=pltpu.SMEM)
PARAMS = pltpu.CompilerParams(vmem_limit_bytes=16 << 20)


def shape(*sizes, dtype=f32):
    return jax.ShapeDtypeStruct(sizes, dtype)


def dot(a, b, dims, precision=None):
    return lax.dot_general(a, b, dims, precision=precision, preferred_element_type=f32)


def two_parts(a):
    top = a.astype(bf16)
    return top, (a - top.astype(f32)).astype(bf16)


def copies_kernel(lines, out):
    for copy in range(out.shape[0]):
        out[copy] = lines[...]


def child_terms(child, block, targets, spread_rows, half_rows):
    places = lax.broadcasted_iota(jnp.int32, (half_rows, targets.shape[1]), 0) + child * half_rows
    spread = (places == targets[...]).astype(f32).astype(bf16)
    for part, piece in enumerate(two_parts(block[...])):
        spread_rows[part] = dot(spread, piece, NN).astype(bf16)


def picked_terms(columns, spread_rows, start, rows):
    places = lax.broadcasted_iota(jnp.int32, (rows, columns.shape[1]), 0) + start
    pick = (places == columns[...]).astype(f32).astype(bf16)
    return dot(pick, spread_rows[0], NT) + dot(pick, spread_rows[1], NT)


def own_kernel(scalars, pattern, block, assembled, columns, targets, total, spread_rows):
    child = scalars[0]
    window_rows, half_rows = total.shape
    child_terms(child, block, targets, spread_rows, half_rows)
    tiles = half_rows // BT
    for step in range(window_rows // BT):
        rows = slice(step * BT, (step + 1) * BT)
        terms = picked_terms(columns, spread_rows, step * BT, BT)
        for tile in range(tiles):
            keep = pattern[child * tiles + tile, step].astype(f32)
            lanes = slice(tile * BT, (tile + 1) * BT)
            total[rows, lanes] = terms[:, lanes] + assembled[lanes, rows].T * keep


def sibling_kernel(scalars, total, block, maps, top, low, spread_rows):
    window_rows, half_rows = total.shape
    child_terms(scalars[0], block, maps.at[1], spread_rows, half_rows)
    for step in range(window_rows // BT):
        rows = slice(step * BT, (step + 1) * BT)
        terms = picked_terms(maps.at[0], spread_rows, step * BT, BT)
        top[rows, :], low[rows, :] = two_parts(total[rows, :] + terms)


def own_operator(scalars, pattern, block, assembled, columns, targets):
    half_rows, window_rows = assembled.shape
    return pl.pallas_call(
        own_kernel,
        in_specs=[SMEM, SMEM] + [VMEM] * 4,
        out_specs=VMEM,
        out_shape=shape(window_rows, half_rows),
        scratch_shapes=[pltpu.VMEM((2, half_rows, block.shape[1]), bf16)],
        compiler_params=PARAMS,
        cost_estimate=pl.CostEstimate(flops=2 * 10**9, bytes_accessed=5 * 10**6, transcendentals=0),
    )(scalars, pattern, block, assembled, columns, targets)


def whole_operator(scalars, total, block, maps):
    window_rows, half_rows = total.shape
    return pl.pallas_call(
        sibling_kernel,
        in_specs=[SMEM] + [VMEM] * 3,
        out_specs=[VMEM, VMEM],
        out_shape=[shape(window_rows, half_rows, dtype=bf16)] * 2,
        scratch_shapes=[
            pltpu.VMEM((2, half_rows, block.shape[1]), bf16),
        ],
        compiler_params=PARAMS,
        cost_estimate=pl.CostEstimate(flops=2 * 10**9, bytes_accessed=5 * 10**6, transcendentals=0),
    )(scalars, total, block, maps)


def apply_kernel(scalars, own, ahead, behind, top, low, give, keep):
    core = scalars[2]
    count, width, half_rows = give.shape
    depth = top.shape[0]
    rows = count * width
    ordered = jnp.concatenate(
        [
            piece[:, pl.ds(side, 1)].reshape(-1, depth)
            for side in (1 - core, core)
            for piece in (own, ahead, behind)
        ]
    )
    high_lines, low_lines = two_parts(ordered)
    for tile in range(half_rows // BT):
        lanes = slice(tile * BT, (tile + 1) * BT)
        out = (
            dot(high_lines, top[:, lanes], NN)
            + dot(low_lines, top[:, lanes], NN)
            + dot(high_lines, low[:, lanes], NN)
        )
        for target, start in ((give, 0), (keep, rows)):
            for side in range(2):
                part = out[start + side * rows // 2 : start + (side + 1) * rows // 2]
                there = slice(side * width // 2, (side + 1) * width // 2)
                target[:, there, lanes] = part.reshape(count, width // 2, BT)


def apply_operator(scalars, own, ahead, behind, top, low):
    count, width, depth = own.shape
    half_rows = top.shape[1]
    lines = [v.reshape(v.shape[0], 2, width // 2, depth) for v in (own, ahead, behind)]
    return pl.pallas_call(
        apply_kernel,
        in_specs=[SMEM] + [VMEM] * 5,
        out_specs=[VMEM, VMEM],
        out_shape=[shape(count, width, half_rows)] * 2,
        compiler_params=PARAMS,
        cost_estimate=pl.CostEstimate(flops=10**9, bytes_accessed=6 * 10**6, transcendentals=0),
    )(scalars, *lines, top, low)


def spread_out(row_or_column):
    return jnp.broadcast_to(row_or_column, (8, 128))


def lane_tiles(a):
    return [a[:, t : t + 128] for t in range(0, a.shape[1], 128)]


def rank_update(block, u, start):
    a = u.astype(bf16).astype(f32)
    b = (u - a).astype(bf16).astype(f32)
    c = u - a - b
    left = jnp.concatenate([v[:, :HALF] for v in (a, a, b, b, a, c)], 0).T[start:].astype(bf16)
    right = jnp.concatenate([a, b, a, b, c, a], 0).astype(bf16)
    block[start:, :] -= dot(left, right, NN)


def factor_panel(panel, upcoming, r):
    sub = lax.broadcasted_iota(jnp.int32, (8, 128), 0)
    lane = lax.broadcasted_iota(jnp.int32, (8, 128), 1)
    rows = lane_tiles(panel)
    columns = [spread_out(rows[0][:, r + j : r + j + 1]) for j in range(8)]
    solved = []
    for j in range(8):
        inverse = lax.rsqrt(spread_out(columns[j][j : j + 1]))
        column = columns[j] * inverse
        solved.append([spread_out(v[j : j + 1]) * inverse for v in rows])
        below = jnp.where(sub > j, column, 0.0)
        rows = [v - below * w for v, w in zip(rows, solved[j])]
        for k in range(j + 1, 8):
            columns[k] = columns[k] - column * spread_out(column[k : k + 1])
    if upcoming is not None:
        after = lane_tiles(upcoming)
        pick = lane == sub + (r + 8)
        for j in range(8):
            column = spread_out(jnp.sum(jnp.where(pick, solved[j][0], 0.0), axis=1, keepdims=True))
            after = [v - column * w for v, w in zip(after, solved[j])]
        upcoming = jnp.concatenate(after, 1)
    out = []
    for t in range(len(rows)):
        u = solved[7][t]
        for j in range(7):
            u = jnp.where(sub == j, solved[j][t], u)
        if t == 0:
            u = jnp.where(lane >= sub + r, u, 0.0)
        out.append(u)
    return jnp.concatenate(out, 1), upcoming


def unit(size):
    return (
        lax.broadcasted_iota(jnp.int32, (size, size), 0) == lax.broadcasted_iota(jnp.int32, (size, size), 1)
    ).astype(f32)


def factor_block(blocks, store):
    panels = [block[:8, :] for block in blocks]
    found = [None] * len(blocks)
    for r in range(0, HALF, 8):
        for leaf, block in enumerate(blocks):
            start = (r + 8) // 16 * 16
            if found[leaf] is not None and start < HALF:
                rank_update(block, found[leaf], start)
        for leaf, block in enumerate(blocks):
            upcoming = block[r + 8 : r + 16, :] if r + 8 < HALF else None
            found[leaf], panels[leaf] = factor_panel(panels[leaf], upcoming, r)
            store(leaf, r, found[leaf])


def head_kernel(scalars, mine, theirs, window, u_head, x_head, rest, gram, s0, s1):
    xl, core, bound = scalars[1], scalars[2], scalars[3]
    count = mine.shape[0] // 2
    half_rows = mine.shape[2]
    window_rows = 2 * half_rows
    for block in range(2 * count):
        lanes = slice(block // count * half_rows, (block // count + 1) * half_rows)
        for side in range(2):
            start = block % count * 32 + (side ^ xl) * 16
            for source, at in ((mine, core), (theirs, 1 - core)):
                there = pl.ds(pl.multiple_of(start + at * 8, 8), 8)
                window[there, lanes] = source[block, side * 8 : side * 8 + 8, :]
    edge = window_rows // 2 + HALF
    lane = lax.broadcasted_iota(jnp.int32, (R, edge), 1)
    head = window[:, :edge]
    tail = window[:, window_rows - edge :]
    for leaf, (inside, leaf_rows) in enumerate(
        ((lane < bound, head), (lane + (window_rows - edge) >= bound, tail))
    ):
        high_rows, low_rows = two_parts(leaf_rows)
        masked = two_parts(jnp.where(inside, leaf_rows, 0.0))[0]
        cross = dot(masked, low_rows, NT)
        gram[leaf] = dot(masked, high_rows, NT) + cross + cross.T
    blocks = (s0, s1)
    for leaf in range(2):
        rows = jnp.where(leaf == 0, bound, window_rows - bound)
        count_rows = jnp.full((1, 1), rows, jnp.int32).astype(f32)
        gram[leaf] = gram[leaf] / count_rows
        blocks[leaf][:, :R] = gram[leaf, :HALF, :]
        blocks[leaf][:, R:] = unit(HALF)

    def store(leaf, r, u):
        u_head[leaf, r : r + 8, :] = u[:, :R]
        x_head[leaf, r : r + 8, :] = u[:, R:]

    factor_block(blocks, store)
    for leaf in range(2):
        side = u_head[leaf, :, HALF:]
        change = dot(side, jnp.concatenate([side, x_head[leaf]], 1), TN, highest)
        rest[leaf, :, :HALF] = gram[leaf, HALF:, HALF:] - change[:, :HALF]
        rest[leaf, :, HALF:] = -change[:, HALF:]


def factor_head(scalars, mine, theirs):
    window_rows = 2 * mine.shape[2]
    return pl.pallas_call(
        head_kernel,
        in_specs=[SMEM, VMEM, VMEM],
        out_specs=[VMEM] * 4,
        out_shape=[
            shape(R, window_rows),
            shape(2, HALF, R),
            shape(2, HALF, HALF),
            shape(2, HALF, R),
        ],
        scratch_shapes=[pltpu.VMEM((2, R, R), f32)] + [pltpu.VMEM((HALF, R + HALF), f32)] * 2,
        compiler_params=PARAMS,
    )(scalars, mine, theirs)


def tail_kernel(scalars, u_head, x_head, rest, u_tail, u_own, x_own, x_tail, s0, s1):
    group = scalars[4]
    blocks = (s0, s1)
    for leaf in range(2):
        blocks[leaf][:, :R] = rest[leaf]
        blocks[leaf][:, R:] = unit(HALF)

    def store(leaf, r, u):
        u_tail[leaf, r : r + 8, :] = u[:, :HALF]
        x_tail[leaf, r : r + 8, :] = u[:, HALF:]

    factor_block(blocks, store)
    start = pl.multiple_of(group % (HALF // 8) * 8, 8)
    in_head = group < HALF // 8
    for leaf in range(2):
        own = pl.ds(start, 8)
        zero = jnp.zeros((8, HALF), f32)
        u_own[leaf] = jnp.where(
            in_head, u_head[leaf, own, :], jnp.concatenate([zero, u_tail[leaf, own, :]], 1)
        )
        x_own[leaf] = jnp.where(
            in_head, jnp.concatenate([x_head[leaf, own, :], zero], 1), x_tail[leaf, own, :]
        )


def factor_tail(scalars, u_head, x_head, rest):
    return pl.pallas_call(
        tail_kernel,
        in_specs=[SMEM] + [VMEM] * 3,
        out_specs=[VMEM] * 3,
        out_shape=[shape(2, HALF, HALF), shape(2, 8, R), shape(2, 8, R)],
        scratch_shapes=[pltpu.VMEM((2, HALF, R), f32)] + [pltpu.VMEM((HALF, R + HALF), f32)] * 2,
        compiler_params=PARAMS,
        cost_estimate=pl.CostEstimate(flops=8 * 10**9, bytes_accessed=10**6, transcendentals=0),
    )(scalars, u_head, x_head, rest)


def bases_kernel(scalars, window, x_own, out):
    both = jnp.concatenate([x_own[0], x_own[1]], 0)
    solved = dot(both, window[...], NN, highest)
    lane = lax.broadcasted_iota(jnp.int32, out.shape, 1)
    out[...] = jnp.where(lane < scalars[3], solved[:8], solved[8:])


def coupling_kernel(u_own, sib_head, sib_tail, out):
    for leaf in range(2):
        own = u_own[leaf]
        out[leaf, :, :HALF] = dot(own, sib_head[leaf], NT, highest)
        out[leaf, :, HALF:] = dot(own[:, HALF:], sib_tail[leaf], NT, highest)


def local(contrib, assembled, pattern, omega, row_maps, leaf_bounds):
    tile_rows, tile_cols = contrib.shape[1:]
    window_rows, own_count = omega.shape
    half_rows = assembled.shape[1]
    z_count, y_count = lax.axis_size("z"), lax.axis_size("y")
    groups = lax.axis_size("child") * y_count
    width = R // (2 * groups)
    child = lax.axis_index("child")
    row_pos = lax.axis_index(("z", "xl"))
    col_pos = lax.axis_index(("y", "core"))
    sibling_block = lax.ppermute(contrib[0], "child", SWAP)
    columns = lax.dynamic_slice_in_dim(row_maps, col_pos * tile_cols, tile_cols, 1) - col_pos * window_rows
    targets = lax.dynamic_slice_in_dim(row_maps, row_pos * tile_rows, tile_rows, 1) - row_pos * window_rows
    maps = jnp.stack([columns, targets])
    sibling_maps = lax.ppermute(maps, "child", SWAP)
    scalars = jnp.stack(
        [
            child,
            lax.axis_index("xl"),
            lax.axis_index("core"),
            leaf_bounds[0],
            lax.axis_index(("child", "y", "core")),
        ]
    ).astype(jnp.int32)

    copies = pl.pallas_call(
        copies_kernel,
        in_specs=[VMEM],
        out_specs=VMEM,
        out_shape=shape(z_count, own_count, window_rows),
        compiler_params=PARAMS,
    )(omega.T)
    own = lax.all_to_all(copies, "z", 0, 0)
    total = own_operator(scalars, pattern, contrib[0], assembled[0], columns, targets)
    ring = lax.axis_size("child") * lax.axis_size("xl")
    other = [
        lax.ppermute(piece, ("child", "xl"), [(i, (i + step) % ring) for i in range(ring)])
        for piece, step in ((own[: z_count // 2], 1), (own[z_count // 2 :], -1))
    ]

    sibling_block, sibling_maps = lax.optimization_barrier((sibling_block, sibling_maps))
    top, low = whole_operator(scalars, total, sibling_block, sibling_maps)

    give, keep = apply_operator(scalars, own, *other, top, low)
    parts = keep + lax.ppermute(give, "core", SWAP)
    terms = lax.all_to_all(parts, "y", 0, 0)
    samples = jnp.sum(terms, axis=0)
    mine = lax.all_to_all(
        jnp.broadcast_to(samples, (groups,) + samples.shape), ("child", "y"), 0, 0
    )
    theirs = lax.ppermute(mine, "core", SWAP)

    window, u_head, x_head, rest = factor_head(scalars, mine, theirs)
    sib_head = lax.ppermute(u_head, "xl", SWAP)
    u_tail, u_own, x_own = factor_tail(scalars, u_head, x_head, rest)
    sib_tail = lax.ppermute(u_tail, "xl", SWAP)
    bases = pl.pallas_call(
        bases_kernel,
        in_specs=[SMEM, VMEM, VMEM],
        out_specs=VMEM,
        out_shape=shape(width, window_rows),
        compiler_params=PARAMS,
        cost_estimate=pl.CostEstimate(flops=10**9, bytes_accessed=10**6, transcendentals=0),
    )(scalars, window, x_own)
    coupling = pl.pallas_call(
        coupling_kernel,
        in_specs=[VMEM] * 3,
        out_specs=VMEM,
        out_shape=shape(2, width, R),
        compiler_params=PARAMS,
    )(u_own, sib_head, sib_tail)
    return (bases.T, coupling[None])


def solution(mesh):
    fine = Mesh(mesh.devices.reshape(2, 8, 2, 8, 2), ("child", "z", "xl", "y", "core"))
    row, col = ("z", "xl"), ("y", "core")
    in_specs = (
        P("child", row, col),
        P("child", row, col),
        P(row, col),
        P(col, row),
        P("child", None),
        P(row),
    )
    out_specs = (P(row, ("child",) + col), P(row, None, ("child",) + col, None))
    return jax.shard_map(local, mesh=fine, in_specs=in_specs, out_specs=out_specs, check_vma=False)
```

```python
import jax
import jax.numpy as jnp
from jax import lax
from jax.experimental import pallas as pl
from jax.experimental.pallas import tpu as pltpu
from jax.sharding import Mesh, PartitionSpec as P

R = 256
BT = 256
HALF = 128

f32, bf16 = jnp.float32, jnp.bfloat16
highest = lax.Precision.HIGHEST
SWAP = [(0, 1), (1, 0)]
NN = (((1,), (0,)), ((), ()))
NT = (((1,), (1,)), ((), ()))
TN = (((0,), (0,)), ((), ()))
VMEM = pl.BlockSpec(memory_space=pltpu.VMEM)
SMEM = pl.BlockSpec(memory_space=pltpu.SMEM)
PARAMS = pltpu.CompilerParams(vmem_limit_bytes=16 << 20)


def shape(*sizes, dtype=f32):
    return jax.ShapeDtypeStruct(sizes, dtype)


def dot(a, b, dims, precision=None):
    return lax.dot_general(a, b, dims, precision=precision, preferred_element_type=f32)


def two_parts(a):
    top = a.astype(bf16)
    return top, (a - top.astype(f32)).astype(bf16)


def copies_kernel(lines, out):
    for copy in range(out.shape[0]):
        out[copy] = lines[...]


def child_terms(child, block, targets, spread_rows, half_rows):
    places = lax.broadcasted_iota(jnp.int32, (half_rows, targets.shape[1]), 0) + child * half_rows
    spread = (places == targets[...]).astype(f32).astype(bf16)
    for part, piece in enumerate(two_parts(block[...])):
        spread_rows[part] = dot(spread, piece, NN).astype(bf16)


def picked_terms(columns, spread_rows, start, rows):
    places = lax.broadcasted_iota(jnp.int32, (rows, columns.shape[1]), 0) + start
    pick = (places == columns[...]).astype(f32).astype(bf16)
    return dot(pick, spread_rows[0], NT) + dot(pick, spread_rows[1], NT)


def own_kernel(scalars, pattern, block, assembled, columns, targets, total, spread_rows):
    child = scalars[0]
    window_rows, half_rows = total.shape
    child_terms(child, block, targets, spread_rows, half_rows)
    tiles = half_rows // BT
    for step in range(window_rows // BT):
        rows = slice(step * BT, (step + 1) * BT)
        terms = picked_terms(columns, spread_rows, step * BT, BT)
        for tile in range(tiles):
            keep = pattern[child * tiles + tile, step].astype(f32)
            lanes = slice(tile * BT, (tile + 1) * BT)
            total[rows, lanes] = terms[:, lanes] + assembled[lanes, rows].T * keep


def sibling_kernel(scalars, total, block, maps, top, low, spread_rows):
    window_rows, half_rows = total.shape
    child_terms(scalars[0], block, maps.at[1], spread_rows, half_rows)
    for step in range(window_rows // BT):
        rows = slice(step * BT, (step + 1) * BT)
        terms = picked_terms(maps.at[0], spread_rows, step * BT, BT)
        top[rows, :], low[rows, :] = two_parts(total[rows, :] + terms)


def own_operator(scalars, pattern, block, assembled, columns, targets):
    half_rows, window_rows = assembled.shape
    return pl.pallas_call(
        own_kernel,
        in_specs=[SMEM, SMEM] + [VMEM] * 4,
        out_specs=VMEM,
        out_shape=shape(window_rows, half_rows),
        scratch_shapes=[pltpu.VMEM((2, half_rows, block.shape[1]), bf16)],
        compiler_params=PARAMS,
        cost_estimate=pl.CostEstimate(flops=2 * 10**9, bytes_accessed=5 * 10**6, transcendentals=0),
    )(scalars, pattern, block, assembled, columns, targets)


def whole_operator(scalars, total, block, maps):
    window_rows, half_rows = total.shape
    return pl.pallas_call(
        sibling_kernel,
        in_specs=[SMEM] + [VMEM] * 3,
        out_specs=[VMEM, VMEM],
        out_shape=[shape(window_rows, half_rows, dtype=bf16)] * 2,
        scratch_shapes=[
            pltpu.VMEM((2, half_rows, block.shape[1]), bf16),
        ],
        compiler_params=PARAMS,
        cost_estimate=pl.CostEstimate(flops=2 * 10**9, bytes_accessed=5 * 10**6, transcendentals=0),
    )(scalars, total, block, maps)


def apply_kernel(own, ahead, behind, top, low, parts):
    count, sides, width, half_rows = parts.shape
    depth = top.shape[0]
    rows = count * width
    ordered = jnp.concatenate(
        [
            piece[:, side].reshape(-1, depth)
            for side in range(sides)
            for piece in (own, ahead, behind)
        ]
    )
    high_lines, low_lines = two_parts(ordered)
    for tile in range(half_rows // BT):
        lanes = slice(tile * BT, (tile + 1) * BT)
        out = (
            dot(high_lines, top[:, lanes], NN)
            + dot(low_lines, top[:, lanes], NN)
            + dot(high_lines, low[:, lanes], NN)
        )
        for side in range(sides):
            for piece in range(2):
                start = side * rows + piece * rows // 2
                there = slice(piece * width // 2, (piece + 1) * width // 2)
                parts[:, side, there, lanes] = out[start : start + rows // 2].reshape(
                    count, width // 2, BT
                )


def apply_operator(own, ahead, behind, top, low):
    count, width, depth = own.shape
    half_rows = top.shape[1]
    lines = [v.reshape(v.shape[0], 2, width // 2, depth) for v in (own, ahead, behind)]
    return pl.pallas_call(
        apply_kernel,
        in_specs=[VMEM] * 5,
        out_specs=VMEM,
        out_shape=shape(count, 2, width, half_rows),
        compiler_params=PARAMS,
        cost_estimate=pl.CostEstimate(flops=10**9, bytes_accessed=6 * 10**6, transcendentals=0),
    )(*lines, top, low)


def spread_out(row_or_column):
    return jnp.broadcast_to(row_or_column, (8, 128))


def lane_tiles(a):
    return [a[:, t : t + 128] for t in range(0, a.shape[1], 128)]


def rank_update(block, u, start):
    a = u.astype(bf16).astype(f32)
    b = (u - a).astype(bf16).astype(f32)
    c = u - a - b
    left = jnp.concatenate([v[:, :HALF] for v in (a, a, b, b, a, c)], 0).T[start:].astype(bf16)
    right = jnp.concatenate([a, b, a, b, c, a], 0).astype(bf16)
    block[start:, :] -= dot(left, right, NN)


def factor_panel(panel, upcoming, r):
    sub = lax.broadcasted_iota(jnp.int32, (8, 128), 0)
    lane = lax.broadcasted_iota(jnp.int32, (8, 128), 1)
    rows = lane_tiles(panel)
    columns = [spread_out(rows[0][:, r + j : r + j + 1]) for j in range(8)]
    solved = []
    for j in range(8):
        inverse = lax.rsqrt(spread_out(columns[j][j : j + 1]))
        column = columns[j] * inverse
        solved.append([spread_out(v[j : j + 1]) * inverse for v in rows])
        below = jnp.where(sub > j, column, 0.0)
        rows = [v - below * w for v, w in zip(rows, solved[j])]
        for k in range(j + 1, 8):
            columns[k] = columns[k] - column * spread_out(column[k : k + 1])
    if upcoming is not None:
        after = lane_tiles(upcoming)
        pick = lane == sub + (r + 8)
        for j in range(8):
            column = spread_out(jnp.sum(jnp.where(pick, solved[j][0], 0.0), axis=1, keepdims=True))
            after = [v - column * w for v, w in zip(after, solved[j])]
        upcoming = jnp.concatenate(after, 1)
    out = []
    for t in range(len(rows)):
        u = solved[7][t]
        for j in range(7):
            u = jnp.where(sub == j, solved[j][t], u)
        if t == 0:
            u = jnp.where(lane >= sub + r, u, 0.0)
        out.append(u)
    return jnp.concatenate(out, 1), upcoming


def unit(size):
    return (
        lax.broadcasted_iota(jnp.int32, (size, size), 0) == lax.broadcasted_iota(jnp.int32, (size, size), 1)
    ).astype(f32)


def factor_block(blocks, store):
    panels = [block[:8, :] for block in blocks]
    found = [None] * len(blocks)
    for r in range(0, HALF, 8):
        for leaf, block in enumerate(blocks):
            start = (r + 8) // 16 * 16
            if found[leaf] is not None and start < HALF:
                rank_update(block, found[leaf], start)
        for leaf, block in enumerate(blocks):
            upcoming = block[r + 8 : r + 16, :] if r + 8 < HALF else None
            found[leaf], panels[leaf] = factor_panel(panels[leaf], upcoming, r)
            store(leaf, r, found[leaf])


def head_kernel(scalars, mine, theirs, window, u_head, x_head, rest, gram, s0, s1):
    xl, core, bound = scalars[1], scalars[2], scalars[3]
    count = mine.shape[0] // 2
    half_rows = mine.shape[2]
    window_rows = 2 * half_rows
    for block in range(2 * count):
        lanes = slice(block // count * half_rows, (block // count + 1) * half_rows)
        for side in range(2):
            start = block % count * 32 + (side ^ xl) * 16
            for source, at in ((mine, core), (theirs, 1 - core)):
                there = pl.ds(pl.multiple_of(start + at * 8, 8), 8)
                window[there, lanes] = source[block, side * 8 : side * 8 + 8, :]
    edge = window_rows // 2 + HALF
    lane = lax.broadcasted_iota(jnp.int32, (R, edge), 1)
    head = window[:, :edge]
    tail = window[:, window_rows - edge :]
    for leaf, (inside, leaf_rows) in enumerate(
        ((lane < bound, head), (lane + (window_rows - edge) >= bound, tail))
    ):
        high_rows, low_rows = two_parts(leaf_rows)
        masked = two_parts(jnp.where(inside, leaf_rows, 0.0))[0]
        cross = dot(masked, low_rows, NT)
        gram[leaf] = dot(masked, high_rows, NT) + cross + cross.T
    blocks = (s0, s1)
    for leaf in range(2):
        rows = jnp.where(leaf == 0, bound, window_rows - bound)
        count_rows = jnp.full((1, 1), rows, jnp.int32).astype(f32)
        gram[leaf] = gram[leaf] / count_rows
        blocks[leaf][:, :R] = gram[leaf, :HALF, :]
        blocks[leaf][:, R:] = unit(HALF)

    def store(leaf, r, u):
        u_head[leaf, r : r + 8, :] = u[:, :R]
        x_head[leaf, r : r + 8, :] = u[:, R:]

    factor_block(blocks, store)
    for leaf in range(2):
        side = u_head[leaf, :, HALF:]
        change = dot(side, jnp.concatenate([side, x_head[leaf]], 1), TN, highest)
        rest[leaf, :, :HALF] = gram[leaf, HALF:, HALF:] - change[:, :HALF]
        rest[leaf, :, HALF:] = -change[:, HALF:]


def factor_head(scalars, mine, theirs):
    window_rows = 2 * mine.shape[2]
    return pl.pallas_call(
        head_kernel,
        in_specs=[SMEM, VMEM, VMEM],
        out_specs=[VMEM] * 4,
        out_shape=[
            shape(R, window_rows),
            shape(2, HALF, R),
            shape(2, HALF, HALF),
            shape(2, HALF, R),
        ],
        scratch_shapes=[pltpu.VMEM((2, R, R), f32)] + [pltpu.VMEM((HALF, R + HALF), f32)] * 2,
        compiler_params=PARAMS,
    )(scalars, mine, theirs)


def tail_kernel(scalars, u_head, x_head, rest, packed, u_own, x_own, u_tail, x_tail, s0, s1):
    group = scalars[4]
    blocks = (s0, s1)
    for leaf in range(2):
        blocks[leaf][:, :R] = rest[leaf]
        blocks[leaf][:, R:] = unit(HALF)

    def store(leaf, r, u):
        u_tail[leaf, r : r + 8, :] = u[:, :HALF]
        x_tail[leaf, r : r + 8, :] = u[:, HALF:]

    factor_block(blocks, store)
    row = lax.broadcasted_iota(jnp.int32, (HALF, HALF), 0)
    column = lax.broadcasted_iota(jnp.int32, (HALF, HALF), 1)
    packed[:HALF, :] = jnp.where(row <= column, u_tail[0], u_tail[1].T)
    diagonal = jnp.sum(jnp.where(row == column, u_tail[1], 0.0), axis=0, keepdims=True)
    packed[HALF:, :] = jnp.broadcast_to(diagonal, (8, HALF))
    start = pl.multiple_of(group % (HALF // 8) * 8, 8)
    in_head = group < HALF // 8
    for leaf in range(2):
        own = pl.ds(start, 8)
        zero = jnp.zeros((8, HALF), f32)
        u_own[leaf] = jnp.where(
            in_head, u_head[leaf, own, :], jnp.concatenate([zero, u_tail[leaf, own, :]], 1)
        )
        x_own[leaf] = jnp.where(
            in_head, jnp.concatenate([x_head[leaf, own, :], zero], 1), x_tail[leaf, own, :]
        )


def factor_tail(scalars, u_head, x_head, rest):
    return pl.pallas_call(
        tail_kernel,
        in_specs=[SMEM] + [VMEM] * 3,
        out_specs=[VMEM] * 3,
        out_shape=[shape(HALF + 8, HALF), shape(2, 8, R), shape(2, 8, R)],
        scratch_shapes=[pltpu.VMEM((2, HALF, HALF), f32), pltpu.VMEM((2, HALF, R), f32)]
        + [pltpu.VMEM((HALF, R + HALF), f32)] * 2,
        compiler_params=PARAMS,
        cost_estimate=pl.CostEstimate(flops=8 * 10**9, bytes_accessed=10**6, transcendentals=0),
    )(scalars, u_head, x_head, rest)


def bases_kernel(scalars, window, x_own, out):
    both = jnp.concatenate([x_own[0], x_own[1]], 0)
    solved = dot(both, window[...], NN, highest)
    lane = lax.broadcasted_iota(jnp.int32, out.shape, 1)
    out[...] = jnp.where(lane < scalars[3], solved[:8], solved[8:])


def coupling_kernel(u_own, sib_head, packed, out):
    row = lax.broadcasted_iota(jnp.int32, (HALF, HALF), 0)
    column = lax.broadcasted_iota(jnp.int32, (HALF, HALF), 1)
    square = packed[:HALF, :]
    second = jnp.where(row > column, square, 0.0).T
    sib_tail = [
        jnp.where(row <= column, square, 0.0),
        jnp.where(row == column, packed[HALF : HALF + 1, :], second),
    ]
    for leaf in range(2):
        own = u_own[leaf]
        out[leaf, :, :HALF] = dot(own, sib_head[leaf], NT, highest)
        out[leaf, :, HALF:] = dot(own[:, HALF:], sib_tail[leaf], NT, highest)


def local(contrib, assembled, pattern, omega, row_maps, leaf_bounds):
    tile_rows, tile_cols = contrib.shape[1:]
    window_rows, own_count = omega.shape
    half_rows = assembled.shape[1]
    z_count, y_count = lax.axis_size("z"), lax.axis_size("y")
    groups = lax.axis_size("child") * y_count
    width = R // (2 * groups)
    child = lax.axis_index("child")
    row_pos = lax.axis_index(("z", "xl"))
    col_pos = lax.axis_index(("y", "core"))
    sibling_block = lax.ppermute(contrib[0], "child", SWAP)
    columns = lax.dynamic_slice_in_dim(row_maps, col_pos * tile_cols, tile_cols, 1) - col_pos * window_rows
    targets = lax.dynamic_slice_in_dim(row_maps, row_pos * tile_rows, tile_rows, 1) - row_pos * window_rows
    maps = jnp.stack([columns, targets])
    sibling_maps = lax.ppermute(maps, "child", SWAP)
    scalars = jnp.stack(
        [
            child,
            lax.axis_index("xl"),
            lax.axis_index("core"),
            leaf_bounds[0],
            lax.axis_index(("child", "y", "core")),
        ]
    ).astype(jnp.int32)

    copies = pl.pallas_call(
        copies_kernel,
        in_specs=[VMEM],
        out_specs=VMEM,
        out_shape=shape(z_count, own_count, window_rows),
        compiler_params=PARAMS,
    )(omega.T)
    own = lax.all_to_all(copies, "z", 0, 0)
    total = own_operator(scalars, pattern, contrib[0], assembled[0], columns, targets)
    ring = lax.axis_size("child") * lax.axis_size("xl")
    other = [
        lax.ppermute(piece, ("child", "xl"), [(i, (i + step) % ring) for i in range(ring)])
        for piece, step in ((own[: z_count // 2], 1), (own[z_count // 2 :], -1))
    ]

    sibling_block, sibling_maps = lax.optimization_barrier((sibling_block, sibling_maps))
    top, low = whole_operator(scalars, total, sibling_block, sibling_maps)

    parts = apply_operator(own, *other, top, low)
    terms = lax.all_to_all(parts.reshape((-1,) + parts.shape[2:]), ("y", "core"), 0, 0)
    samples = jnp.sum(terms, axis=0)
    mine = lax.all_to_all(
        jnp.broadcast_to(samples, (groups,) + samples.shape), ("child", "y"), 0, 0
    )
    theirs = lax.ppermute(mine, "core", SWAP)

    window, u_head, x_head, rest = factor_head(scalars, mine, theirs)
    sib_head = lax.ppermute(u_head, "xl", SWAP)
    u_tail, u_own, x_own = factor_tail(scalars, u_head, x_head, rest)
    sib_tail = lax.ppermute(u_tail, "xl", SWAP)
    bases = pl.pallas_call(
        bases_kernel,
        in_specs=[SMEM, VMEM, VMEM],
        out_specs=VMEM,
        out_shape=shape(width, window_rows),
        compiler_params=PARAMS,
        cost_estimate=pl.CostEstimate(flops=10**9, bytes_accessed=10**6, transcendentals=0),
    )(scalars, window, x_own)
    coupling = pl.pallas_call(
        coupling_kernel,
        in_specs=[VMEM] * 3,
        out_specs=VMEM,
        out_shape=shape(2, width, R),
        compiler_params=PARAMS,
    )(u_own, sib_head, sib_tail)
    return (bases.T, coupling[None])


def solution(mesh):
    fine = Mesh(mesh.devices.reshape(2, 8, 2, 8, 2), ("child", "z", "xl", "y", "core"))
    row, col = ("z", "xl"), ("y", "core")
    in_specs = (
        P("child", row, col),
        P("child", row, col),
        P(row, col),
        P(col, row),
        P("child", None),
        P(row),
    )
    out_specs = (P(row, ("child",) + col), P(row, None, ("child",) + col, None))
    return jax.shard_map(local, mesh=fine, in_specs=in_specs, out_specs=out_specs, check_vma=False)
```

```python
import jax
import jax.numpy as jnp
from jax import lax
from jax.experimental import pallas as pl
from jax.experimental.pallas import tpu as pltpu
from jax.sharding import Mesh, PartitionSpec as P

R = 256
BT = 256
HALF = 128

f32, bf16 = jnp.float32, jnp.bfloat16
highest = lax.Precision.HIGHEST
SWAP = [(0, 1), (1, 0)]
NN = (((1,), (0,)), ((), ()))
NT = (((1,), (1,)), ((), ()))
TN = (((0,), (0,)), ((), ()))
VMEM = pl.BlockSpec(memory_space=pltpu.VMEM)
SMEM = pl.BlockSpec(memory_space=pltpu.SMEM)
PARAMS = pltpu.CompilerParams(vmem_limit_bytes=16 << 20)


def shape(*sizes, dtype=f32):
    return jax.ShapeDtypeStruct(sizes, dtype)


def dot(a, b, dims, precision=None):
    return lax.dot_general(a, b, dims, precision=precision, preferred_element_type=f32)


def two_parts(a):
    top = a.astype(bf16)
    return top, (a - top.astype(f32)).astype(bf16)


def copies_kernel(lines, out):
    for copy in range(out.shape[0]):
        out[copy] = lines[...]


def child_terms(child, block, targets, spread_rows, half_rows):
    places = lax.broadcasted_iota(jnp.int32, (half_rows, targets.shape[1]), 0) + child * half_rows
    spread = (places == targets[...]).astype(f32).astype(bf16)
    for part, piece in enumerate(two_parts(block[...])):
        spread_rows[part] = dot(spread, piece, NN).astype(bf16)


def picked_terms(columns, spread_rows, start, rows):
    places = lax.broadcasted_iota(jnp.int32, (rows, columns.shape[1]), 0) + start
    pick = (places == columns[...]).astype(f32).astype(bf16)
    return dot(pick, spread_rows[0], NT) + dot(pick, spread_rows[1], NT)


def own_kernel(scalars, pattern, block, assembled, columns, targets, total, spread_rows):
    child = scalars[0]
    window_rows, half_rows = total.shape
    child_terms(child, block, targets, spread_rows, half_rows)
    tiles = half_rows // BT
    for step in range(window_rows // BT):
        rows = slice(step * BT, (step + 1) * BT)
        terms = picked_terms(columns, spread_rows, step * BT, BT)
        for tile in range(tiles):
            keep = pattern[child * tiles + tile, step].astype(f32)
            lanes = slice(tile * BT, (tile + 1) * BT)
            total[rows, lanes] = terms[:, lanes] + assembled[lanes, rows].T * keep


def sibling_kernel(scalars, total, block, maps, top, low, spread_rows):
    window_rows, half_rows = total.shape
    child_terms(scalars[0], block, maps.at[1], spread_rows, half_rows)
    for step in range(window_rows // BT):
        rows = slice(step * BT, (step + 1) * BT)
        terms = picked_terms(maps.at[0], spread_rows, step * BT, BT)
        top[rows, :], low[rows, :] = two_parts(total[rows, :] + terms)


def own_operator(scalars, pattern, block, assembled, columns, targets):
    half_rows, window_rows = assembled.shape
    return pl.pallas_call(
        own_kernel,
        in_specs=[SMEM, SMEM] + [VMEM] * 4,
        out_specs=VMEM,
        out_shape=shape(window_rows, half_rows),
        scratch_shapes=[pltpu.VMEM((2, half_rows, block.shape[1]), bf16)],
        compiler_params=PARAMS,
        cost_estimate=pl.CostEstimate(flops=2 * 10**9, bytes_accessed=5 * 10**6, transcendentals=0),
    )(scalars, pattern, block, assembled, columns, targets)


def whole_operator(scalars, total, block, maps):
    window_rows, half_rows = total.shape
    return pl.pallas_call(
        sibling_kernel,
        in_specs=[SMEM] + [VMEM] * 3,
        out_specs=[VMEM, VMEM],
        out_shape=[shape(window_rows, half_rows, dtype=bf16)] * 2,
        scratch_shapes=[
            pltpu.VMEM((2, half_rows, block.shape[1]), bf16),
        ],
        compiler_params=PARAMS,
        cost_estimate=pl.CostEstimate(flops=2 * 10**9, bytes_accessed=5 * 10**6, transcendentals=0),
    )(scalars, total, block, maps)


def apply_kernel(scalars, own, ahead, behind, top, low, give, keep):
    core = scalars[2]
    count, width, half_rows = give.shape
    depth = top.shape[0]
    rows = count * width
    ordered = jnp.concatenate(
        [piece[:, side].reshape(-1, depth) for side in range(2) for piece in (own, ahead, behind)]
    )
    high_lines, low_lines = two_parts(ordered)
    for tile in range(half_rows // BT):
        lanes = slice(tile * BT, (tile + 1) * BT)
        out = (
            dot(high_lines, top[:, lanes], NN)
            + dot(low_lines, top[:, lanes], NN)
            + dot(high_lines, low[:, lanes], NN)
        )
        first, second = out[:rows], out[rows:]
        for target, value in (
            (give, jnp.where(core == 0, second, first)),
            (keep, jnp.where(core == 0, first, second)),
        ):
            for piece in range(2):
                there = slice(piece * width // 2, (piece + 1) * width // 2)
                part = value[piece * rows // 2 : (piece + 1) * rows // 2]
                target[:, there, lanes] = part.reshape(count, width // 2, BT)


def apply_operator(scalars, own, ahead, behind, top, low):
    count, width, depth = own.shape
    half_rows = top.shape[1]
    lines = [v.reshape(v.shape[0], 2, width // 2, depth) for v in (own, ahead, behind)]
    return pl.pallas_call(
        apply_kernel,
        in_specs=[SMEM] + [VMEM] * 5,
        out_specs=[VMEM, VMEM],
        out_shape=[shape(count, width, half_rows)] * 2,
        compiler_params=PARAMS,
        cost_estimate=pl.CostEstimate(flops=10**9, bytes_accessed=6 * 10**6, transcendentals=0),
    )(scalars, *lines, top, low)


def spread_out(row_or_column):
    return jnp.broadcast_to(row_or_column, (8, 128))


def lane_tiles(a):
    return [a[:, t : t + 128] for t in range(0, a.shape[1], 128)]


def rank_update(block, u, start):
    a = u.astype(bf16).astype(f32)
    b = (u - a).astype(bf16).astype(f32)
    c = u - a - b
    left = jnp.concatenate([v[:, :HALF] for v in (a, a, b, b, a, c)], 0).T[start:].astype(bf16)
    right = jnp.concatenate([a, b, a, b, c, a], 0).astype(bf16)
    block[start:, :] -= dot(left, right, NN)


def factor_panel(panel, upcoming, r):
    sub = lax.broadcasted_iota(jnp.int32, (8, 128), 0)
    lane = lax.broadcasted_iota(jnp.int32, (8, 128), 1)
    rows = lane_tiles(panel)
    columns = [spread_out(rows[0][:, r + j : r + j + 1]) for j in range(8)]
    solved = []
    for j in range(8):
        inverse = lax.rsqrt(spread_out(columns[j][j : j + 1]))
        column = columns[j] * inverse
        solved.append([spread_out(v[j : j + 1]) * inverse for v in rows])
        below = jnp.where(sub > j, column, 0.0)
        rows = [v - below * w for v, w in zip(rows, solved[j])]
        for k in range(j + 1, 8):
            columns[k] = columns[k] - column * spread_out(column[k : k + 1])
    if upcoming is not None:
        after = lane_tiles(upcoming)
        pick = lane == sub + (r + 8)
        for j in range(8):
            column = spread_out(jnp.sum(jnp.where(pick, solved[j][0], 0.0), axis=1, keepdims=True))
            after = [v - column * w for v, w in zip(after, solved[j])]
        upcoming = jnp.concatenate(after, 1)
    out = []
    for t in range(len(rows)):
        u = solved[7][t]
        for j in range(7):
            u = jnp.where(sub == j, solved[j][t], u)
        if t == 0:
            u = jnp.where(lane >= sub + r, u, 0.0)
        out.append(u)
    return jnp.concatenate(out, 1), upcoming


def unit(size):
    return (
        lax.broadcasted_iota(jnp.int32, (size, size), 0) == lax.broadcasted_iota(jnp.int32, (size, size), 1)
    ).astype(f32)


def factor_block(blocks, store):
    panels = [block[:8, :] for block in blocks]
    found = [None] * len(blocks)
    for r in range(0, HALF, 8):
        for leaf, block in enumerate(blocks):
            start = (r + 8) // 16 * 16
            if found[leaf] is not None and start < HALF:
                rank_update(block, found[leaf], start)
        for leaf, block in enumerate(blocks):
            upcoming = block[r + 8 : r + 16, :] if r + 8 < HALF else None
            found[leaf], panels[leaf] = factor_panel(panels[leaf], upcoming, r)
            store(leaf, r, found[leaf])


def head_kernel(scalars, mine, theirs, window, u_head, x_head, rest, gram, s0, s1):
    xl, core, bound = scalars[1], scalars[2], scalars[3]
    count = mine.shape[0] // 2
    half_rows = mine.shape[2]
    window_rows = 2 * half_rows
    for block in range(2 * count):
        lanes = slice(block // count * half_rows, (block // count + 1) * half_rows)
        for side in range(2):
            start = block % count * 32 + (side ^ xl) * 16
            for source, at in ((mine, core), (theirs, 1 - core)):
                there = pl.ds(pl.multiple_of(start + at * 8, 8), 8)
                window[there, lanes] = source[block, side * 8 : side * 8 + 8, :]
    edge = window_rows // 2 + HALF
    lane = lax.broadcasted_iota(jnp.int32, (R, edge), 1)
    head = window[:, :edge]
    tail = window[:, window_rows - edge :]
    for leaf, (inside, leaf_rows) in enumerate(
        ((lane < bound, head), (lane + (window_rows - edge) >= bound, tail))
    ):
        high_rows, low_rows = two_parts(leaf_rows)
        masked = two_parts(jnp.where(inside, leaf_rows, 0.0))[0]
        cross = dot(masked, low_rows, NT)
        gram[leaf] = dot(masked, high_rows, NT) + cross + cross.T
    blocks = (s0, s1)
    for leaf in range(2):
        rows = jnp.where(leaf == 0, bound, window_rows - bound)
        count_rows = jnp.full((1, 1), rows, jnp.int32).astype(f32)
        gram[leaf] = gram[leaf] / count_rows
        blocks[leaf][:, :R] = gram[leaf, :HALF, :]
        blocks[leaf][:, R:] = unit(HALF)

    def store(leaf, r, u):
        u_head[leaf, r : r + 8, :] = u[:, :R]
        x_head[leaf, r : r + 8, :] = u[:, R:]

    factor_block(blocks, store)
    for leaf in range(2):
        side = u_head[leaf, :, HALF:]
        change = dot(side, jnp.concatenate([side, x_head[leaf]], 1), TN, highest)
        rest[leaf, :, :HALF] = gram[leaf, HALF:, HALF:] - change[:, :HALF]
        rest[leaf, :, HALF:] = -change[:, HALF:]


def factor_head(scalars, mine, theirs):
    window_rows = 2 * mine.shape[2]
    return pl.pallas_call(
        head_kernel,
        in_specs=[SMEM, VMEM, VMEM],
        out_specs=[VMEM] * 4,
        out_shape=[
            shape(R, window_rows),
            shape(2, HALF, R),
            shape(2, HALF, HALF),
            shape(2, HALF, R),
        ],
        scratch_shapes=[pltpu.VMEM((2, R, R), f32)] + [pltpu.VMEM((HALF, R + HALF), f32)] * 2,
        compiler_params=PARAMS,
    )(scalars, mine, theirs)


def tail_kernel(scalars, u_head, x_head, rest, packed, u_own, x_own, u_tail, x_tail, s0, s1):
    group = scalars[4]
    blocks = (s0, s1)
    for leaf in range(2):
        blocks[leaf][:, :R] = rest[leaf]
        blocks[leaf][:, R:] = unit(HALF)

    def store(leaf, r, u):
        u_tail[leaf, r : r + 8, :] = u[:, :HALF]
        x_tail[leaf, r : r + 8, :] = u[:, HALF:]

    factor_block(blocks, store)
    row = lax.broadcasted_iota(jnp.int32, (HALF, HALF), 0)
    column = lax.broadcasted_iota(jnp.int32, (HALF, HALF), 1)
    packed[:HALF, :] = jnp.where(row <= column, u_tail[0], u_tail[1].T)
    diagonal = jnp.sum(jnp.where(row == column, u_tail[1], 0.0), axis=0, keepdims=True)
    packed[HALF:, :] = jnp.broadcast_to(diagonal, (8, HALF))
    start = pl.multiple_of(group % (HALF // 8) * 8, 8)
    in_head = group < HALF // 8
    for leaf in range(2):
        own = pl.ds(start, 8)
        zero = jnp.zeros((8, HALF), f32)
        u_own[leaf] = jnp.where(
            in_head, u_head[leaf, own, :], jnp.concatenate([zero, u_tail[leaf, own, :]], 1)
        )
        x_own[leaf] = jnp.where(
            in_head, jnp.concatenate([x_head[leaf, own, :], zero], 1), x_tail[leaf, own, :]
        )


def factor_tail(scalars, u_head, x_head, rest):
    return pl.pallas_call(
        tail_kernel,
        in_specs=[SMEM] + [VMEM] * 3,
        out_specs=[VMEM] * 3,
        out_shape=[shape(HALF + 8, HALF), shape(2, 8, R), shape(2, 8, R)],
        scratch_shapes=[pltpu.VMEM((2, HALF, HALF), f32), pltpu.VMEM((2, HALF, R), f32)]
        + [pltpu.VMEM((HALF, R + HALF), f32)] * 2,
        compiler_params=PARAMS,
        cost_estimate=pl.CostEstimate(flops=8 * 10**9, bytes_accessed=10**6, transcendentals=0),
    )(scalars, u_head, x_head, rest)


def bases_kernel(scalars, window, x_own, u_own, sib_head, out, head_part):
    high_x, low_x = two_parts(jnp.concatenate([x_own[0], x_own[1]], 0))
    high_w, low_w = two_parts(window[...])
    wide = dot(jnp.concatenate([high_x, low_x], 0), high_w, NN)
    solved = wide[:16] + wide[16:] + dot(high_x, low_w, NN)
    lane = lax.broadcasted_iota(jnp.int32, out.shape, 1)
    out[...] = jnp.where(lane < scalars[3], solved[:8], solved[8:])
    for leaf in range(2):
        head_part[leaf] = dot(u_own[leaf], sib_head[leaf], NT, highest)


def coupling_kernel(u_own, head_part, packed, out):
    row = lax.broadcasted_iota(jnp.int32, (HALF, HALF), 0)
    column = lax.broadcasted_iota(jnp.int32, (HALF, HALF), 1)
    square = packed[:HALF, :]
    second = jnp.where(row > column, square, 0.0).T
    sib_tail = [
        jnp.where(row <= column, square, 0.0),
        jnp.where(row == column, packed[HALF : HALF + 1, :], second),
    ]
    for leaf in range(2):
        out[leaf, :, :HALF] = head_part[leaf]
        out[leaf, :, HALF:] = dot(u_own[leaf, :, HALF:], sib_tail[leaf], NT, highest)


def local(contrib, assembled, pattern, omega, row_maps, leaf_bounds):
    tile_rows, tile_cols = contrib.shape[1:]
    window_rows, own_count = omega.shape
    half_rows = assembled.shape[1]
    z_count, y_count = lax.axis_size("z"), lax.axis_size("y")
    groups = lax.axis_size("child") * y_count
    width = R // (2 * groups)
    child = lax.axis_index("child")
    row_pos = lax.axis_index(("z", "xl"))
    col_pos = lax.axis_index(("y", "core"))
    sibling_block = lax.ppermute(contrib[0], "child", SWAP)
    columns = lax.dynamic_slice_in_dim(row_maps, col_pos * tile_cols, tile_cols, 1) - col_pos * window_rows
    targets = lax.dynamic_slice_in_dim(row_maps, row_pos * tile_rows, tile_rows, 1) - row_pos * window_rows
    maps = jnp.stack([columns, targets])
    sibling_maps = lax.ppermute(maps, "child", SWAP)
    scalars = jnp.stack(
        [
            child,
            lax.axis_index("xl"),
            lax.axis_index("core"),
            leaf_bounds[0],
            lax.axis_index(("child", "y", "core")),
        ]
    ).astype(jnp.int32)

    copies = pl.pallas_call(
        copies_kernel,
        in_specs=[VMEM],
        out_specs=VMEM,
        out_shape=shape(z_count, own_count, window_rows),
        compiler_params=PARAMS,
    )(omega.T)
    own = lax.all_to_all(copies, "z", 0, 0)
    total = own_operator(scalars, pattern, contrib[0], assembled[0], columns, targets)
    ring = lax.axis_size("child") * lax.axis_size("xl")
    other = [
        lax.ppermute(piece, ("child", "xl"), [(i, (i + step) % ring) for i in range(ring)])
        for piece, step in ((own[: z_count // 2], 1), (own[z_count // 2 :], -1))
    ]

    sibling_block, sibling_maps = lax.optimization_barrier((sibling_block, sibling_maps))
    top, low = whole_operator(scalars, total, sibling_block, sibling_maps)

    give, keep = apply_operator(scalars, own, *other, top, low)
    parts = keep + lax.ppermute(give, "core", SWAP)
    terms = lax.all_to_all(parts, "y", 0, 0)
    samples = jnp.sum(terms, axis=0)
    mine = lax.all_to_all(
        jnp.broadcast_to(samples, (groups,) + samples.shape), ("child", "y"), 0, 0
    )
    theirs = lax.ppermute(mine, "core", SWAP)

    window, u_head, x_head, rest = factor_head(scalars, mine, theirs)
    sib_head = lax.ppermute(u_head, "xl", SWAP)
    u_tail, u_own, x_own = factor_tail(scalars, u_head, x_head, rest)
    sib_tail = lax.ppermute(u_tail, "xl", SWAP)
    bases, head_part = pl.pallas_call(
        bases_kernel,
        in_specs=[SMEM] + [VMEM] * 4,
        out_specs=[VMEM, VMEM],
        out_shape=[shape(width, window_rows), shape(2, width, HALF)],
        compiler_params=PARAMS,
        cost_estimate=pl.CostEstimate(flops=10**9, bytes_accessed=10**6, transcendentals=0),
    )(scalars, window, x_own, u_own, sib_head)
    coupling = pl.pallas_call(
        coupling_kernel,
        in_specs=[VMEM] * 3,
        out_specs=VMEM,
        out_shape=shape(2, width, R),
        compiler_params=PARAMS,
    )(u_own, head_part, sib_tail)
    return (bases.T, coupling[None])


def solution(mesh):
    fine = Mesh(mesh.devices.reshape(2, 8, 2, 8, 2), ("child", "z", "xl", "y", "core"))
    row, col = ("z", "xl"), ("y", "core")
    in_specs = (
        P("child", row, col),
        P("child", row, col),
        P(row, col),
        P(col, row),
        P("child", None),
        P(row),
    )
    out_specs = (P(row, ("child",) + col), P(row, None, ("child",) + col, None))
    return jax.shard_map(local, mesh=fine, in_specs=in_specs, out_specs=out_specs, check_vma=False)
```

```python
import functools

import jax
import jax.numpy as jnp
from jax import lax
from jax.experimental import pallas as pl
from jax.experimental.pallas import tpu as pltpu
from jax.sharding import Mesh, PartitionSpec as P

R = 256
BT = 256
HALF = 128

f32, bf16 = jnp.float32, jnp.bfloat16
highest = lax.Precision.HIGHEST
SWAP = [(0, 1), (1, 0)]
NN = (((1,), (0,)), ((), ()))
NT = (((1,), (1,)), ((), ()))
TN = (((0,), (0,)), ((), ()))
VMEM = pl.BlockSpec(memory_space=pltpu.VMEM)
SMEM = pl.BlockSpec(memory_space=pltpu.SMEM)
PARAMS = pltpu.CompilerParams(vmem_limit_bytes=16 << 20)


def shape(*sizes, dtype=f32):
    return jax.ShapeDtypeStruct(sizes, dtype)


def dot(a, b, dims, precision=None):
    return lax.dot_general(a, b, dims, precision=precision, preferred_element_type=f32)


def two_parts(a):
    top = a.astype(bf16)
    return top, (a - top.astype(f32)).astype(bf16)


def copies_kernel(lines, out):
    for copy in range(out.shape[0]):
        out[copy] = lines[...]


def child_terms(child, block, targets, spread_rows, half_rows):
    places = lax.broadcasted_iota(jnp.int32, (half_rows, targets.shape[1]), 0) + child * half_rows
    spread = (places == targets[...]).astype(f32).astype(bf16)
    for part, piece in enumerate(two_parts(block[...])):
        spread_rows[part] = dot(spread, piece, NN).astype(bf16)


def picked_terms(columns, spread_rows, start, rows):
    places = lax.broadcasted_iota(jnp.int32, (rows, columns.shape[1]), 0) + start
    pick = (places == columns[...]).astype(f32).astype(bf16)
    return dot(pick, spread_rows[0], NT) + dot(pick, spread_rows[1], NT)


def own_kernel(scalars, pattern, block, assembled, columns, targets, total, spread_rows):
    child = scalars[0]
    window_rows, half_rows = total.shape
    child_terms(child, block, targets, spread_rows, half_rows)
    tiles = half_rows // BT
    for step in range(window_rows // BT):
        rows = slice(step * BT, (step + 1) * BT)
        terms = picked_terms(columns, spread_rows, step * BT, BT)
        for tile in range(tiles):
            keep = pattern[child * tiles + tile, step].astype(f32)
            lanes = slice(tile * BT, (tile + 1) * BT)
            total[rows, lanes] = terms[:, lanes] + assembled[lanes, rows].T * keep


def sibling_kernel(scalars, total, block, maps, top, low, spread_rows):
    window_rows, half_rows = total.shape
    child_terms(scalars[0], block, maps.at[1], spread_rows, half_rows)
    for step in range(window_rows // BT):
        rows = slice(step * BT, (step + 1) * BT)
        terms = picked_terms(maps.at[0], spread_rows, step * BT, BT)
        top[rows, :], low[rows, :] = two_parts(total[rows, :] + terms)


def own_operator(scalars, pattern, block, assembled, columns, targets):
    half_rows, window_rows = assembled.shape
    return pl.pallas_call(
        own_kernel,
        in_specs=[SMEM, SMEM] + [VMEM] * 4,
        out_specs=VMEM,
        out_shape=shape(window_rows, half_rows),
        scratch_shapes=[pltpu.VMEM((2, half_rows, block.shape[1]), bf16)],
        compiler_params=PARAMS,
        cost_estimate=pl.CostEstimate(flops=2 * 10**9, bytes_accessed=5 * 10**6, transcendentals=0),
    )(scalars, pattern, block, assembled, columns, targets)


def whole_operator(scalars, total, block, maps):
    window_rows, half_rows = total.shape
    return pl.pallas_call(
        sibling_kernel,
        in_specs=[SMEM] + [VMEM] * 3,
        out_specs=[VMEM, VMEM],
        out_shape=[shape(window_rows, half_rows, dtype=bf16)] * 2,
        scratch_shapes=[
            pltpu.VMEM((2, half_rows, block.shape[1]), bf16),
        ],
        compiler_params=PARAMS,
        cost_estimate=pl.CostEstimate(flops=2 * 10**9, bytes_accessed=5 * 10**6, transcendentals=0),
    )(scalars, total, block, maps)


def mapped(pieces, side, top, low, targets):
    depth, half_rows = top.shape
    lines = jnp.concatenate([piece[:, side].reshape(-1, depth) for piece in pieces])
    high_lines, low_lines = two_parts(lines)
    count, width, _ = targets.shape
    for tile in range(half_rows // BT):
        lanes = slice(tile * BT, (tile + 1) * BT)
        out = (
            dot(high_lines, top[:, lanes], NN)
            + dot(low_lines, top[:, lanes], NN)
            + dot(high_lines, low[:, lanes], NN)
        )
        targets[:, :, lanes] = out.reshape(count, width, BT)


def on_each_core(core, body):
    for value in range(2):
        pl.when(core == value)(lambda value=value: body(value))


def own_columns_kernel(scalars, own, top, low, give, keep):
    def body(core):
        mapped([own], 1 - core, top, low, give)
        mapped([own], core, top, low, keep)

    on_each_core(scalars[2], body)


def other_columns_kernel(given, scalars, first, ahead, behind, top, low, out):
    width = first.shape[1]
    out[:, :width, :] = first[...]

    def body(core):
        mapped([ahead, behind], 1 - core if given else core, top, low, out.at[:, width:, :])

    on_each_core(scalars[2], body)


def sides(gathered):
    count, both, depth = gathered.shape
    return gathered.reshape(count, 2, both // 2, depth)


def own_columns(scalars, own, top, low):
    lines = sides(own)
    return pl.pallas_call(
        own_columns_kernel,
        in_specs=[SMEM] + [VMEM] * 3,
        out_specs=[VMEM, VMEM],
        out_shape=[shape(lines.shape[0], lines.shape[2], top.shape[1])] * 2,
        compiler_params=PARAMS,
        cost_estimate=pl.CostEstimate(flops=5 * 10**8, bytes_accessed=10**6, transcendentals=0),
    )(scalars, lines, top, low)


def other_columns(given, scalars, first, ahead, behind, top, low):
    count, width, half_rows = first.shape
    return pl.pallas_call(
        functools.partial(other_columns_kernel, given),
        in_specs=[SMEM] + [VMEM] * 5,
        out_specs=VMEM,
        out_shape=shape(count, 2 * width, half_rows),
        compiler_params=PARAMS,
        cost_estimate=pl.CostEstimate(flops=5 * 10**8, bytes_accessed=10**6, transcendentals=0),
    )(scalars, first, sides(ahead), sides(behind), top, low)


def spread_out(row_or_column):
    return jnp.broadcast_to(row_or_column, (8, 128))


def lane_tiles(a):
    return [a[:, t : t + 128] for t in range(0, a.shape[1], 128)]


def rank_update(block, u, start):
    a = u.astype(bf16).astype(f32)
    b = (u - a).astype(bf16).astype(f32)
    c = u - a - b
    left = jnp.concatenate([v[:, :HALF] for v in (a, a, b, b, a, c)], 0).T[start:].astype(bf16)
    right = jnp.concatenate([a, b, a, b, c, a], 0).astype(bf16)
    block[start:, :] -= dot(left, right, NN)


def factor_panel(panel, upcoming, r):
    sub = lax.broadcasted_iota(jnp.int32, (8, 128), 0)
    lane = lax.broadcasted_iota(jnp.int32, (8, 128), 1)
    rows = lane_tiles(panel)
    columns = [spread_out(rows[0][:, r + j : r + j + 1]) for j in range(8)]
    solved = []
    for j in range(8):
        inverse = lax.rsqrt(spread_out(columns[j][j : j + 1]))
        column = columns[j] * inverse
        solved.append([spread_out(v[j : j + 1]) * inverse for v in rows])
        below = jnp.where(sub > j, column, 0.0)
        rows = [v - below * w for v, w in zip(rows, solved[j])]
        for k in range(j + 1, 8):
            columns[k] = columns[k] - column * spread_out(column[k : k + 1])
    if upcoming is not None:
        after = lane_tiles(upcoming)
        pick = lane == sub + (r + 8)
        for j in range(8):
            column = spread_out(jnp.sum(jnp.where(pick, solved[j][0], 0.0), axis=1, keepdims=True))
            after = [v - column * w for v, w in zip(after, solved[j])]
        upcoming = jnp.concatenate(after, 1)
    out = []
    for t in range(len(rows)):
        u = solved[7][t]
        for j in range(7):
            u = jnp.where(sub == j, solved[j][t], u)
        if t == 0:
            u = jnp.where(lane >= sub + r, u, 0.0)
        out.append(u)
    return jnp.concatenate(out, 1), upcoming


def unit(size):
    return (
        lax.broadcasted_iota(jnp.int32, (size, size), 0) == lax.broadcasted_iota(jnp.int32, (size, size), 1)
    ).astype(f32)


def factor_block(blocks, store):
    panels = [block[:8, :] for block in blocks]
    found = [None] * len(blocks)
    for r in range(0, HALF, 8):
        for leaf, block in enumerate(blocks):
            start = (r + 8) // 16 * 16
            if found[leaf] is not None and start < HALF:
                rank_update(block, found[leaf], start)
        for leaf, block in enumerate(blocks):
            upcoming = block[r + 8 : r + 16, :] if r + 8 < HALF else None
            found[leaf], panels[leaf] = factor_panel(panels[leaf], upcoming, r)
            store(leaf, r, found[leaf])


def head_kernel(scalars, mine, theirs, window, u_head, x_head, rest, gram, s0, s1):
    xl, core, bound = scalars[1], scalars[2], scalars[3]
    count = mine.shape[0] // 2
    half_rows = mine.shape[2]
    window_rows = 2 * half_rows
    for block in range(2 * count):
        lanes = slice(block // count * half_rows, (block // count + 1) * half_rows)
        for side in range(2):
            start = block % count * 32 + (side ^ xl) * 16
            for source, at in ((mine, core), (theirs, 1 - core)):
                there = pl.ds(pl.multiple_of(start + at * 8, 8), 8)
                window[there, lanes] = source[block, side * 8 : side * 8 + 8, :]
    edge = window_rows // 2 + HALF
    lane = lax.broadcasted_iota(jnp.int32, (R, edge), 1)
    head = window[:, :edge]
    tail = window[:, window_rows - edge :]
    for leaf, (inside, leaf_rows) in enumerate(
        ((lane < bound, head), (lane + (window_rows - edge) >= bound, tail))
    ):
        high_rows, low_rows = two_parts(leaf_rows)
        masked = two_parts(jnp.where(inside, leaf_rows, 0.0))[0]
        cross = dot(masked, low_rows, NT)
        gram[leaf] = dot(masked, high_rows, NT) + cross + cross.T
    blocks = (s0, s1)
    for leaf in range(2):
        rows = jnp.where(leaf == 0, bound, window_rows - bound)
        count_rows = jnp.full((1, 1), rows, jnp.int32).astype(f32)
        gram[leaf] = gram[leaf] / count_rows
        blocks[leaf][:, :R] = gram[leaf, :HALF, :]
        blocks[leaf][:, R:] = unit(HALF)

    def store(leaf, r, u):
        u_head[leaf, r : r + 8, :] = u[:, :R]
        x_head[leaf, r : r + 8, :] = u[:, R:]

    factor_block(blocks, store)
    for leaf in range(2):
        side = u_head[leaf, :, HALF:]
        change = dot(side, jnp.concatenate([side, x_head[leaf]], 1), TN, highest)
        rest[leaf, :, :HALF] = gram[leaf, HALF:, HALF:] - change[:, :HALF]
        rest[leaf, :, HALF:] = -change[:, HALF:]


def factor_head(scalars, mine, theirs):
    window_rows = 2 * mine.shape[2]
    return pl.pallas_call(
        head_kernel,
        in_specs=[SMEM, VMEM, VMEM],
        out_specs=[VMEM] * 4,
        out_shape=[
            shape(R, window_rows),
            shape(2, HALF, R),
            shape(2, HALF, HALF),
            shape(2, HALF, R),
        ],
        scratch_shapes=[pltpu.VMEM((2, R, R), f32)] + [pltpu.VMEM((HALF, R + HALF), f32)] * 2,
        compiler_params=PARAMS,
    )(scalars, mine, theirs)


def tail_kernel(scalars, u_head, x_head, rest, packed, u_own, x_own, u_tail, x_tail, s0, s1):
    group = scalars[4]
    blocks = (s0, s1)
    for leaf in range(2):
        blocks[leaf][:, :R] = rest[leaf]
        blocks[leaf][:, R:] = unit(HALF)

    def store(leaf, r, u):
        u_tail[leaf, r : r + 8, :] = u[:, :HALF]
        x_tail[leaf, r : r + 8, :] = u[:, HALF:]

    factor_block(blocks, store)
    row = lax.broadcasted_iota(jnp.int32, (HALF, HALF), 0)
    column = lax.broadcasted_iota(jnp.int32, (HALF, HALF), 1)
    packed[:HALF, :] = jnp.where(row <= column, u_tail[0], u_tail[1].T)
    diagonal = jnp.sum(jnp.where(row == column, u_tail[1], 0.0), axis=0, keepdims=True)
    packed[HALF:, :] = jnp.broadcast_to(diagonal, (8, HALF))
    start = pl.multiple_of(group % (HALF // 8) * 8, 8)
    in_head = group < HALF // 8
    for leaf in range(2):
        own = pl.ds(start, 8)
        zero = jnp.zeros((8, HALF), f32)
        u_own[leaf] = jnp.where(
            in_head, u_head[leaf, own, :], jnp.concatenate([zero, u_tail[leaf, own, :]], 1)
        )
        x_own[leaf] = jnp.where(
            in_head, jnp.concatenate([x_head[leaf, own, :], zero], 1), x_tail[leaf, own, :]
        )


def factor_tail(scalars, u_head, x_head, rest):
    return pl.pallas_call(
        tail_kernel,
        in_specs=[SMEM] + [VMEM] * 3,
        out_specs=[VMEM] * 3,
        out_shape=[shape(HALF + 8, HALF), shape(2, 8, R), shape(2, 8, R)],
        scratch_shapes=[pltpu.VMEM((2, HALF, HALF), f32), pltpu.VMEM((2, HALF, R), f32)]
        + [pltpu.VMEM((HALF, R + HALF), f32)] * 2,
        compiler_params=PARAMS,
        cost_estimate=pl.CostEstimate(flops=8 * 10**9, bytes_accessed=10**6, transcendentals=0),
    )(scalars, u_head, x_head, rest)


def bases_kernel(scalars, window, x_own, u_own, sib_head, out, head_part):
    high_x, low_x = two_parts(jnp.concatenate([x_own[0], x_own[1]], 0))
    high_w, low_w = two_parts(window[...])
    wide = dot(jnp.concatenate([high_x, low_x], 0), high_w, NN)
    solved = wide[:16] + wide[16:] + dot(high_x, low_w, NN)
    lane = lax.broadcasted_iota(jnp.int32, out.shape, 1)
    out[...] = jnp.where(lane < scalars[3], solved[:8], solved[8:])
    for leaf in range(2):
        head_part[leaf] = dot(u_own[leaf], sib_head[leaf], NT, highest)


def coupling_kernel(u_own, head_part, packed, out):
    row = lax.broadcasted_iota(jnp.int32, (HALF, HALF), 0)
    column = lax.broadcasted_iota(jnp.int32, (HALF, HALF), 1)
    square = packed[:HALF, :]
    second = jnp.where(row > column, square, 0.0).T
    sib_tail = [
        jnp.where(row <= column, square, 0.0),
        jnp.where(row == column, packed[HALF : HALF + 1, :], second),
    ]
    for leaf in range(2):
        out[leaf, :, :HALF] = head_part[leaf]
        out[leaf, :, HALF:] = dot(u_own[leaf, :, HALF:], sib_tail[leaf], NT, highest)


def local(contrib, assembled, pattern, omega, row_maps, leaf_bounds):
    tile_rows, tile_cols = contrib.shape[1:]
    window_rows, own_count = omega.shape
    half_rows = assembled.shape[1]
    z_count, y_count = lax.axis_size("z"), lax.axis_size("y")
    groups = lax.axis_size("child") * y_count
    width = R // (2 * groups)
    child = lax.axis_index("child")
    row_pos = lax.axis_index(("z", "xl"))
    col_pos = lax.axis_index(("y", "core"))
    sibling_block = lax.ppermute(contrib[0], "child", SWAP)
    columns = lax.dynamic_slice_in_dim(row_maps, col_pos * tile_cols, tile_cols, 1) - col_pos * window_rows
    targets = lax.dynamic_slice_in_dim(row_maps, row_pos * tile_rows, tile_rows, 1) - row_pos * window_rows
    maps = jnp.stack([columns, targets])
    sibling_maps = lax.ppermute(maps, "child", SWAP)
    scalars = jnp.stack(
        [
            child,
            lax.axis_index("xl"),
            lax.axis_index("core"),
            leaf_bounds[0],
            lax.axis_index(("child", "y", "core")),
        ]
    ).astype(jnp.int32)

    copies = pl.pallas_call(
        copies_kernel,
        in_specs=[VMEM],
        out_specs=VMEM,
        out_shape=shape(z_count, own_count, window_rows),
        compiler_params=PARAMS,
    )(omega.T)
    own = lax.all_to_all(copies, "z", 0, 0)
    total = own_operator(scalars, pattern, contrib[0], assembled[0], columns, targets)
    ring = lax.axis_size("child") * lax.axis_size("xl")
    other = [
        lax.ppermute(piece, ("child", "xl"), [(i, (i + step) % ring) for i in range(ring)])
        for piece, step in ((own[: z_count // 2], 1), (own[z_count // 2 :], -1))
    ]

    sibling_block, sibling_maps = lax.optimization_barrier((sibling_block, sibling_maps))
    top, low = whole_operator(scalars, total, sibling_block, sibling_maps)

    give, keep = own_columns(scalars, own, top, low)
    give = other_columns(True, scalars, give, *other, top, low)
    arrived = lax.ppermute(give, "core", SWAP)
    parts = other_columns(False, scalars, keep, *other, top, low) + arrived
    terms = lax.all_to_all(parts, "y", 0, 0)
    samples = jnp.sum(terms, axis=0)
    mine = lax.all_to_all(
        jnp.broadcast_to(samples, (groups,) + samples.shape), ("child", "y"), 0, 0
    )
    theirs = lax.ppermute(mine, "core", SWAP)

    window, u_head, x_head, rest = factor_head(scalars, mine, theirs)
    sib_head = lax.ppermute(u_head, "xl", SWAP)
    u_tail, u_own, x_own = factor_tail(scalars, u_head, x_head, rest)
    sib_tail = lax.ppermute(u_tail, "xl", SWAP)
    bases, head_part = pl.pallas_call(
        bases_kernel,
        in_specs=[SMEM] + [VMEM] * 4,
        out_specs=[VMEM, VMEM],
        out_shape=[shape(width, window_rows), shape(2, width, HALF)],
        compiler_params=PARAMS,
        cost_estimate=pl.CostEstimate(flops=10**9, bytes_accessed=10**6, transcendentals=0),
    )(scalars, window, x_own, u_own, sib_head)
    coupling = pl.pallas_call(
        coupling_kernel,
        in_specs=[VMEM] * 3,
        out_specs=VMEM,
        out_shape=shape(2, width, R),
        compiler_params=PARAMS,
    )(u_own, head_part, sib_tail)
    return (bases.T, coupling[None])


def solution(mesh):
    fine = Mesh(mesh.devices.reshape(2, 8, 2, 8, 2), ("child", "z", "xl", "y", "core"))
    row, col = ("z", "xl"), ("y", "core")
    in_specs = (
        P("child", row, col),
        P("child", row, col),
        P(row, col),
        P(col, row),
        P("child", None),
        P(row),
    )
    out_specs = (P(row, ("child",) + col), P(row, None, ("child",) + col, None))
    return jax.shard_map(local, mesh=fine, in_specs=in_specs, out_specs=out_specs, check_vma=False)
```

```python
import jax
import jax.numpy as jnp
from jax import lax
from jax.experimental import pallas as pl
from jax.experimental.pallas import tpu as pltpu
from jax.sharding import Mesh, PartitionSpec as P

R = 256
BT = 256
HALF = 128

f32, bf16 = jnp.float32, jnp.bfloat16
highest = lax.Precision.HIGHEST
SWAP = [(0, 1), (1, 0)]
NN = (((1,), (0,)), ((), ()))
NT = (((1,), (1,)), ((), ()))
TN = (((0,), (0,)), ((), ()))
VMEM = pl.BlockSpec(memory_space=pltpu.VMEM)
SMEM = pl.BlockSpec(memory_space=pltpu.SMEM)
PARAMS = pltpu.CompilerParams(vmem_limit_bytes=16 << 20)


def shape(*sizes, dtype=f32):
    return jax.ShapeDtypeStruct(sizes, dtype)


def dot(a, b, dims, precision=None):
    return lax.dot_general(a, b, dims, precision=precision, preferred_element_type=f32)


def two_parts(a):
    top = a.astype(bf16)
    return top, (a - top.astype(f32)).astype(bf16)


def copies_kernel(lines, out):
    for copy in range(out.shape[0]):
        out[copy] = lines[...]


def child_terms(child, block, targets, spread_rows, half_rows):
    places = lax.broadcasted_iota(jnp.int32, (half_rows, targets.shape[1]), 0) + child * half_rows
    spread = (places == targets[...]).astype(f32).astype(bf16)
    for part, piece in enumerate(two_parts(block[...])):
        spread_rows[part] = dot(spread, piece, NN).astype(bf16)


def picked_terms(columns, spread_rows, start, rows):
    places = lax.broadcasted_iota(jnp.int32, (rows, columns.shape[1]), 0) + start
    pick = (places == columns[...]).astype(f32).astype(bf16)
    return dot(pick, spread_rows[0], NT) + dot(pick, spread_rows[1], NT)


def own_kernel(scalars, pattern, block, assembled, columns, targets, total, spread_rows):
    child = scalars[0]
    window_rows, half_rows = total.shape
    child_terms(child, block, targets, spread_rows, half_rows)
    tiles = half_rows // BT
    for step in range(window_rows // BT):
        rows = slice(step * BT, (step + 1) * BT)
        terms = picked_terms(columns, spread_rows, step * BT, BT)
        for tile in range(tiles):
            keep = pattern[child * tiles + tile, step].astype(f32)
            lanes = slice(tile * BT, (tile + 1) * BT)
            total[rows, lanes] = terms[:, lanes] + assembled[lanes, rows].T * keep


def sibling_kernel(scalars, total, block, maps, top, low, spread_rows):
    window_rows, half_rows = total.shape
    child_terms(scalars[0], block, maps.at[1], spread_rows, half_rows)
    for step in range(window_rows // BT):
        rows = slice(step * BT, (step + 1) * BT)
        terms = picked_terms(maps.at[0], spread_rows, step * BT, BT)
        top[rows, :], low[rows, :] = two_parts(total[rows, :] + terms)


def own_operator(scalars, pattern, block, assembled, columns, targets):
    half_rows, window_rows = assembled.shape
    return pl.pallas_call(
        own_kernel,
        in_specs=[SMEM, SMEM] + [VMEM] * 4,
        out_specs=VMEM,
        out_shape=shape(window_rows, half_rows),
        scratch_shapes=[pltpu.VMEM((2, half_rows, block.shape[1]), bf16)],
        compiler_params=PARAMS,
        cost_estimate=pl.CostEstimate(flops=2 * 10**9, bytes_accessed=5 * 10**6, transcendentals=0),
    )(scalars, pattern, block, assembled, columns, targets)


def whole_operator(scalars, total, block, maps):
    window_rows, half_rows = total.shape
    return pl.pallas_call(
        sibling_kernel,
        in_specs=[SMEM] + [VMEM] * 3,
        out_specs=[VMEM, VMEM],
        out_shape=[shape(window_rows, half_rows, dtype=bf16)] * 2,
        scratch_shapes=[
            pltpu.VMEM((2, half_rows, block.shape[1]), bf16),
        ],
        compiler_params=PARAMS,
        cost_estimate=pl.CostEstimate(flops=2 * 10**9, bytes_accessed=5 * 10**6, transcendentals=0),
    )(scalars, total, block, maps)


def apply_kernel(scalars, own, ahead, behind, top, low, give, keep):
    depth, half_rows = top.shape
    count, width, _ = give.shape
    rows = count * width // 2

    def body(core):
        lines = jnp.concatenate(
            [
                piece[:, side].reshape(-1, depth)
                for side in (1 - core, core)
                for piece in (own, ahead, behind)
            ]
        )
        high_lines, low_lines = two_parts(lines)
        for tile in range(half_rows // BT):
            lanes = slice(tile * BT, (tile + 1) * BT)
            out = (
                dot(high_lines, top[:, lanes], NN)
                + dot(low_lines, top[:, lanes], NN)
                + dot(high_lines, low[:, lanes], NN)
            )
            for block in range(4):
                target = (give, keep)[block // 2]
                there = slice(block % 2 * width // 2, (block % 2 + 1) * width // 2)
                part = out[block * rows : (block + 1) * rows]
                target[:, there, lanes] = part.reshape(count, width // 2, BT)

    for value in range(2):
        pl.when(scalars[2] == value)(lambda value=value: body(value))


def apply_operator(scalars, own, ahead, behind, top, low):
    count, width, depth = own.shape
    half_rows = top.shape[1]
    lines = [v.reshape(v.shape[0], 2, width // 2, depth) for v in (own, ahead, behind)]
    return pl.pallas_call(
        apply_kernel,
        in_specs=[SMEM] + [VMEM] * 5,
        out_specs=[VMEM, VMEM],
        out_shape=[shape(count, width, half_rows)] * 2,
        compiler_params=PARAMS,
        cost_estimate=pl.CostEstimate(flops=10**9, bytes_accessed=6 * 10**6, transcendentals=0),
    )(scalars, *lines, top, low)


def spread_out(row_or_column):
    return jnp.broadcast_to(row_or_column, (8, 128))


def lane_tiles(a):
    return [a[:, t : t + 128] for t in range(0, a.shape[1], 128)]


def rank_update(block, u, start):
    a = u.astype(bf16).astype(f32)
    b = (u - a).astype(bf16).astype(f32)
    c = u - a - b
    left = jnp.concatenate([v[:, :HALF] for v in (a, a, b, b, a, c)], 0).T[start:].astype(bf16)
    right = jnp.concatenate([a, b, a, b, c, a], 0).astype(bf16)
    block[start:, :] -= dot(left, right, NN)


def factor_panel(panel, upcoming, r):
    sub = lax.broadcasted_iota(jnp.int32, (8, 128), 0)
    lane = lax.broadcasted_iota(jnp.int32, (8, 128), 1)
    rows = lane_tiles(panel)
    columns = [spread_out(rows[0][:, r + j : r + j + 1]) for j in range(8)]
    solved = []
    for j in range(8):
        inverse = lax.rsqrt(spread_out(columns[j][j : j + 1]))
        column = columns[j] * inverse
        solved.append([spread_out(v[j : j + 1]) * inverse for v in rows])
        below = jnp.where(sub > j, column, 0.0)
        rows = [v - below * w for v, w in zip(rows, solved[j])]
        for k in range(j + 1, 8):
            columns[k] = columns[k] - column * spread_out(column[k : k + 1])
    if upcoming is not None:
        after = lane_tiles(upcoming)
        pick = lane == sub + (r + 8)
        for j in range(8):
            column = spread_out(jnp.sum(jnp.where(pick, solved[j][0], 0.0), axis=1, keepdims=True))
            after = [v - column * w for v, w in zip(after, solved[j])]
        upcoming = jnp.concatenate(after, 1)
    out = []
    for t in range(len(rows)):
        u = solved[7][t]
        for j in range(7):
            u = jnp.where(sub == j, solved[j][t], u)
        if t == 0:
            u = jnp.where(lane >= sub + r, u, 0.0)
        out.append(u)
    return jnp.concatenate(out, 1), upcoming


def unit(size):
    return (
        lax.broadcasted_iota(jnp.int32, (size, size), 0) == lax.broadcasted_iota(jnp.int32, (size, size), 1)
    ).astype(f32)


def factor_block(blocks, store):
    panels = [block[:8, :] for block in blocks]
    found = [None] * len(blocks)
    for r in range(0, HALF, 8):
        for leaf, block in enumerate(blocks):
            start = (r + 8) // 16 * 16
            if found[leaf] is not None and start < HALF:
                rank_update(block, found[leaf], start)
        for leaf, block in enumerate(blocks):
            upcoming = block[r + 8 : r + 16, :] if r + 8 < HALF else None
            found[leaf], panels[leaf] = factor_panel(panels[leaf], upcoming, r)
            store(leaf, r, found[leaf])


def head_kernel(scalars, mine, theirs, window, u_head, x_head, rest, gram, s0, s1):
    xl, core, bound = scalars[1], scalars[2], scalars[3]
    count = mine.shape[0] // 2
    half_rows = mine.shape[2]
    window_rows = 2 * half_rows
    for block in range(2 * count):
        lanes = slice(block // count * half_rows, (block // count + 1) * half_rows)
        for side in range(2):
            start = block % count * 32 + (side ^ xl) * 16
            for source, at in ((mine, core), (theirs, 1 - core)):
                there = pl.ds(pl.multiple_of(start + at * 8, 8), 8)
                window[there, lanes] = source[block, side * 8 : side * 8 + 8, :]
    edge = window_rows // 2 + HALF
    lane = lax.broadcasted_iota(jnp.int32, (R, edge), 1)
    head = window[:, :edge]
    tail = window[:, window_rows - edge :]
    for leaf, (inside, leaf_rows) in enumerate(
        ((lane < bound, head), (lane + (window_rows - edge) >= bound, tail))
    ):
        high_rows, low_rows = two_parts(leaf_rows)
        masked = two_parts(jnp.where(inside, leaf_rows, 0.0))[0]
        cross = dot(masked, low_rows, NT)
        gram[leaf] = dot(masked, high_rows, NT) + cross + cross.T
    blocks = (s0, s1)
    for leaf in range(2):
        rows = jnp.where(leaf == 0, bound, window_rows - bound)
        count_rows = jnp.full((1, 1), rows, jnp.int32).astype(f32)
        gram[leaf] = gram[leaf] / count_rows
        blocks[leaf][:, :R] = gram[leaf, :HALF, :]
        blocks[leaf][:, R:] = unit(HALF)

    def store(leaf, r, u):
        u_head[leaf, r : r + 8, :] = u[:, :R]
        x_head[leaf, r : r + 8, :] = u[:, R:]

    factor_block(blocks, store)
    for leaf in range(2):
        side = u_head[leaf, :, HALF:]
        change = dot(side, jnp.concatenate([side, x_head[leaf]], 1), TN, highest)
        rest[leaf, :, :HALF] = gram[leaf, HALF:, HALF:] - change[:, :HALF]
        rest[leaf, :, HALF:] = -change[:, HALF:]


def factor_head(scalars, mine, theirs):
    window_rows = 2 * mine.shape[2]
    return pl.pallas_call(
        head_kernel,
        in_specs=[SMEM, VMEM, VMEM],
        out_specs=[VMEM] * 4,
        out_shape=[
            shape(R, window_rows),
            shape(2, HALF, R),
            shape(2, HALF, HALF),
            shape(2, HALF, R),
        ],
        scratch_shapes=[pltpu.VMEM((2, R, R), f32)] + [pltpu.VMEM((HALF, R + HALF), f32)] * 2,
        compiler_params=PARAMS,
    )(scalars, mine, theirs)


def tail_kernel(scalars, u_head, x_head, rest, packed, u_own, x_own, u_tail, x_tail, s0, s1):
    group = scalars[4]
    blocks = (s0, s1)
    for leaf in range(2):
        blocks[leaf][:, :R] = rest[leaf]
        blocks[leaf][:, R:] = unit(HALF)

    def store(leaf, r, u):
        u_tail[leaf, r : r + 8, :] = u[:, :HALF]
        x_tail[leaf, r : r + 8, :] = u[:, HALF:]

    factor_block(blocks, store)
    row = lax.broadcasted_iota(jnp.int32, (HALF, HALF), 0)
    column = lax.broadcasted_iota(jnp.int32, (HALF, HALF), 1)
    packed[:HALF, :] = jnp.where(row <= column, u_tail[0], u_tail[1].T)
    diagonal = jnp.sum(jnp.where(row == column, u_tail[1], 0.0), axis=0, keepdims=True)
    packed[HALF:, :] = jnp.broadcast_to(diagonal, (8, HALF))
    start = pl.multiple_of(group % (HALF // 8) * 8, 8)
    in_head = group < HALF // 8
    for leaf in range(2):
        own = pl.ds(start, 8)
        zero = jnp.zeros((8, HALF), f32)
        u_own[leaf] = jnp.where(
            in_head, u_head[leaf, own, :], jnp.concatenate([zero, u_tail[leaf, own, :]], 1)
        )
        x_own[leaf] = jnp.where(
            in_head, jnp.concatenate([x_head[leaf, own, :], zero], 1), x_tail[leaf, own, :]
        )


def factor_tail(scalars, u_head, x_head, rest):
    return pl.pallas_call(
        tail_kernel,
        in_specs=[SMEM] + [VMEM] * 3,
        out_specs=[VMEM] * 3,
        out_shape=[shape(HALF + 8, HALF), shape(2, 8, R), shape(2, 8, R)],
        scratch_shapes=[pltpu.VMEM((2, HALF, HALF), f32), pltpu.VMEM((2, HALF, R), f32)]
        + [pltpu.VMEM((HALF, R + HALF), f32)] * 2,
        compiler_params=PARAMS,
        cost_estimate=pl.CostEstimate(flops=8 * 10**9, bytes_accessed=10**6, transcendentals=0),
    )(scalars, u_head, x_head, rest)


def bases_kernel(scalars, window, x_own, u_own, sib_head, out, head_part):
    high_x, low_x = two_parts(jnp.concatenate([x_own[0], x_own[1]], 0))
    high_w, low_w = two_parts(window[...])
    wide = dot(jnp.concatenate([high_x, low_x], 0), high_w, NN)
    solved = wide[:16] + wide[16:] + dot(high_x, low_w, NN)
    lane = lax.broadcasted_iota(jnp.int32, out.shape, 1)
    out[...] = jnp.where(lane < scalars[3], solved[:8], solved[8:])
    for leaf in range(2):
        head_part[leaf] = dot(u_own[leaf], sib_head[leaf], NT, highest)


def coupling_kernel(u_own, head_part, packed, out):
    row = lax.broadcasted_iota(jnp.int32, (HALF, HALF), 0)
    column = lax.broadcasted_iota(jnp.int32, (HALF, HALF), 1)
    square = packed[:HALF, :]
    second = jnp.where(row > column, square, 0.0).T
    sib_tail = [
        jnp.where(row <= column, square, 0.0),
        jnp.where(row == column, packed[HALF : HALF + 1, :], second),
    ]
    for leaf in range(2):
        out[leaf, :, :HALF] = head_part[leaf]
        out[leaf, :, HALF:] = dot(u_own[leaf, :, HALF:], sib_tail[leaf], NT, highest)


def local(contrib, assembled, pattern, omega, row_maps, leaf_bounds):
    tile_rows, tile_cols = contrib.shape[1:]
    window_rows, own_count = omega.shape
    half_rows = assembled.shape[1]
    z_count, y_count = lax.axis_size("z"), lax.axis_size("y")
    groups = lax.axis_size("child") * y_count
    width = R // (2 * groups)
    child = lax.axis_index("child")
    row_pos = lax.axis_index(("z", "xl"))
    col_pos = lax.axis_index(("y", "core"))
    sibling_block = lax.ppermute(contrib[0], "child", SWAP)
    columns = lax.dynamic_slice_in_dim(row_maps, col_pos * tile_cols, tile_cols, 1) - col_pos * window_rows
    targets = lax.dynamic_slice_in_dim(row_maps, row_pos * tile_rows, tile_rows, 1) - row_pos * window_rows
    maps = jnp.stack([columns, targets])
    sibling_maps = lax.ppermute(maps, "child", SWAP)
    scalars = jnp.stack(
        [
            child,
            lax.axis_index("xl"),
            lax.axis_index("core"),
            leaf_bounds[0],
            lax.axis_index(("child", "y", "core")),
        ]
    ).astype(jnp.int32)

    copies = pl.pallas_call(
        copies_kernel,
        in_specs=[VMEM],
        out_specs=VMEM,
        out_shape=shape(z_count, own_count, window_rows),
        compiler_params=PARAMS,
    )(omega.T)
    own = lax.all_to_all(copies, "z", 0, 0)
    total = own_operator(scalars, pattern, contrib[0], assembled[0], columns, targets)
    ring = lax.axis_size("child") * lax.axis_size("xl")
    other = [
        lax.ppermute(piece, ("child", "xl"), [(i, (i + step) % ring) for i in range(ring)])
        for piece, step in ((own[: z_count // 2], 1), (own[z_count // 2 :], -1))
    ]

    sibling_block, sibling_maps = lax.optimization_barrier((sibling_block, sibling_maps))
    top, low = whole_operator(scalars, total, sibling_block, sibling_maps)

    give, keep = apply_operator(scalars, own, *other, top, low)
    parts = keep + lax.ppermute(give, "core", SWAP)
    terms = lax.all_to_all(parts, "y", 0, 0)
    samples = jnp.sum(terms, axis=0)
    mine = lax.all_to_all(
        jnp.broadcast_to(samples, (groups,) + samples.shape), ("child", "y"), 0, 0
    )
    theirs = lax.ppermute(mine, "core", SWAP)

    window, u_head, x_head, rest = factor_head(scalars, mine, theirs)
    sib_head = lax.ppermute(u_head, "xl", SWAP)
    u_tail, u_own, x_own = factor_tail(scalars, u_head, x_head, rest)
    sib_tail = lax.ppermute(u_tail, "xl", SWAP)
    bases, head_part = pl.pallas_call(
        bases_kernel,
        in_specs=[SMEM] + [VMEM] * 4,
        out_specs=[VMEM, VMEM],
        out_shape=[shape(width, window_rows), shape(2, width, HALF)],
        compiler_params=PARAMS,
        cost_estimate=pl.CostEstimate(flops=10**9, bytes_accessed=10**6, transcendentals=0),
    )(scalars, window, x_own, u_own, sib_head)
    coupling = pl.pallas_call(
        coupling_kernel,
        in_specs=[VMEM] * 3,
        out_specs=VMEM,
        out_shape=shape(2, width, R),
        compiler_params=PARAMS,
    )(u_own, head_part, sib_tail)
    return (bases.T, coupling[None])


def solution(mesh):
    fine = Mesh(mesh.devices.reshape(2, 8, 2, 8, 2), ("child", "z", "xl", "y", "core"))
    row, col = ("z", "xl"), ("y", "core")
    in_specs = (
        P("child", row, col),
        P("child", row, col),
        P(row, col),
        P(col, row),
        P("child", None),
        P(row),
    )
    out_specs = (P(row, ("child",) + col), P(row, None, ("child",) + col, None))
    return jax.shard_map(local, mesh=fine, in_specs=in_specs, out_specs=out_specs, check_vma=False)
```

```python
import jax
import jax.numpy as jnp
from jax import lax
from jax.experimental import pallas as pl
from jax.experimental.pallas import tpu as pltpu
from jax.sharding import Mesh, PartitionSpec as P

R = 256
BT = 256
HALF = 128

f32, bf16 = jnp.float32, jnp.bfloat16
highest = lax.Precision.HIGHEST
SWAP = [(0, 1), (1, 0)]
NN = (((1,), (0,)), ((), ()))
NT = (((1,), (1,)), ((), ()))
TN = (((0,), (0,)), ((), ()))
VMEM = pl.BlockSpec(memory_space=pltpu.VMEM)
SMEM = pl.BlockSpec(memory_space=pltpu.SMEM)
PARAMS = pltpu.CompilerParams(vmem_limit_bytes=16 << 20)


def shape(*sizes, dtype=f32):
    return jax.ShapeDtypeStruct(sizes, dtype)


def dot(a, b, dims, precision=None):
    return lax.dot_general(a, b, dims, precision=precision, preferred_element_type=f32)


def two_parts(a):
    top = a.astype(bf16)
    return top, (a - top.astype(f32)).astype(bf16)


def copies_kernel(lines, out):
    for copy in range(out.shape[0]):
        out[copy] = lines[...]


def child_terms(child, block, targets, spread_rows, half_rows):
    places = lax.broadcasted_iota(jnp.int32, (half_rows, targets.shape[1]), 0) + child * half_rows
    spread = (places == targets[...]).astype(f32).astype(bf16)
    for part, piece in enumerate(two_parts(block[...])):
        spread_rows[part] = dot(spread, piece, NN).astype(bf16)


def picked_terms(columns, spread_rows, start, rows):
    places = lax.broadcasted_iota(jnp.int32, (rows, columns.shape[1]), 0) + start
    pick = (places == columns[...]).astype(f32).astype(bf16)
    return dot(pick, spread_rows[0], NT) + dot(pick, spread_rows[1], NT)


def own_kernel(scalars, pattern, block, assembled, columns, targets, total, spread_rows):
    child = scalars[0]
    window_rows, half_rows = total.shape
    child_terms(child, block, targets, spread_rows, half_rows)
    tiles = half_rows // BT
    for step in range(window_rows // BT):
        rows = slice(step * BT, (step + 1) * BT)
        terms = picked_terms(columns, spread_rows, step * BT, BT)
        for tile in range(tiles):
            keep = pattern[child * tiles + tile, step].astype(f32)
            lanes = slice(tile * BT, (tile + 1) * BT)
            total[rows, lanes] = terms[:, lanes] + assembled[lanes, rows].T * keep


def sibling_kernel(scalars, total, block, maps, top, low, spread_rows):
    window_rows, half_rows = total.shape
    child_terms(scalars[0], block, maps.at[1], spread_rows, half_rows)
    for step in range(window_rows // BT):
        rows = slice(step * BT, (step + 1) * BT)
        terms = picked_terms(maps.at[0], spread_rows, step * BT, BT)
        top[rows, :], low[rows, :] = two_parts(total[rows, :] + terms)


def own_operator(scalars, pattern, block, assembled, columns, targets):
    half_rows, window_rows = assembled.shape
    return pl.pallas_call(
        own_kernel,
        in_specs=[SMEM, SMEM] + [VMEM] * 4,
        out_specs=VMEM,
        out_shape=shape(window_rows, half_rows),
        scratch_shapes=[pltpu.VMEM((2, half_rows, block.shape[1]), bf16)],
        compiler_params=PARAMS,
        cost_estimate=pl.CostEstimate(flops=2 * 10**9, bytes_accessed=5 * 10**6, transcendentals=0),
    )(scalars, pattern, block, assembled, columns, targets)


def whole_operator(scalars, total, block, maps):
    window_rows, half_rows = total.shape
    return pl.pallas_call(
        sibling_kernel,
        in_specs=[SMEM] + [VMEM] * 3,
        out_specs=[VMEM, VMEM],
        out_shape=[shape(window_rows, half_rows, dtype=bf16)] * 2,
        scratch_shapes=[
            pltpu.VMEM((2, half_rows, block.shape[1]), bf16),
        ],
        compiler_params=PARAMS,
        cost_estimate=pl.CostEstimate(flops=2 * 10**9, bytes_accessed=5 * 10**6, transcendentals=0),
    )(scalars, total, block, maps)


def apply_kernel(scalars, own, other, top, low, give, keep):
    core = scalars[2]
    count, width, half_rows = give.shape
    depth = top.shape[0]
    rows = count * width
    ordered = jnp.concatenate(
        [piece[:, side].reshape(-1, depth) for side in range(2) for piece in (own, other)]
    )
    high_lines, low_lines = two_parts(ordered)
    for tile in range(half_rows // BT):
        lanes = slice(tile * BT, (tile + 1) * BT)
        out = (
            dot(high_lines, top[:, lanes], NN)
            + dot(low_lines, top[:, lanes], NN)
            + dot(high_lines, low[:, lanes], NN)
        )
        first, second = out[:rows], out[rows:]
        for target, value in (
            (give, jnp.where(core == 0, second, first)),
            (keep, jnp.where(core == 0, first, second)),
        ):
            for piece in range(2):
                there = slice(piece * width // 2, (piece + 1) * width // 2)
                part = value[piece * rows // 2 : (piece + 1) * rows // 2]
                target[:, there, lanes] = part.reshape(count, width // 2, BT)


def apply_operator(scalars, own, other, top, low):
    count, width, depth = own.shape
    half_rows = top.shape[1]
    lines = [v.reshape(v.shape[0], 2, width // 2, depth) for v in (own, other)]
    return pl.pallas_call(
        apply_kernel,
        in_specs=[SMEM] + [VMEM] * 4,
        out_specs=[VMEM, VMEM],
        out_shape=[shape(count, width, half_rows)] * 2,
        compiler_params=PARAMS,
        cost_estimate=pl.CostEstimate(flops=10**9, bytes_accessed=6 * 10**6, transcendentals=0),
    )(scalars, *lines, top, low)


def spread_out(row_or_column):
    return jnp.broadcast_to(row_or_column, (8, 128))


def lane_tiles(a):
    return [a[:, t : t + 128] for t in range(0, a.shape[1], 128)]


def rank_update(block, u, start):
    a = u.astype(bf16).astype(f32)
    b = (u - a).astype(bf16).astype(f32)
    c = u - a - b
    left = jnp.concatenate([v[:, :HALF] for v in (a, a, b, b, a, c)], 0).T[start:].astype(bf16)
    right = jnp.concatenate([a, b, a, b, c, a], 0).astype(bf16)
    block[start:, :] -= dot(left, right, NN)


def factor_panel(panel, upcoming, r):
    sub = lax.broadcasted_iota(jnp.int32, (8, 128), 0)
    lane = lax.broadcasted_iota(jnp.int32, (8, 128), 1)
    rows = lane_tiles(panel)
    columns = [spread_out(rows[0][:, r + j : r + j + 1]) for j in range(8)]
    solved = []
    for j in range(8):
        inverse = lax.rsqrt(spread_out(columns[j][j : j + 1]))
        column = columns[j] * inverse
        solved.append([spread_out(v[j : j + 1]) * inverse for v in rows])
        below = jnp.where(sub > j, column, 0.0)
        rows = [v - below * w for v, w in zip(rows, solved[j])]
        for k in range(j + 1, 8):
            columns[k] = columns[k] - column * spread_out(column[k : k + 1])
    if upcoming is not None:
        after = lane_tiles(upcoming)
        pick = lane == sub + (r + 8)
        for j in range(8):
            column = spread_out(jnp.sum(jnp.where(pick, solved[j][0], 0.0), axis=1, keepdims=True))
            after = [v - column * w for v, w in zip(after, solved[j])]
        upcoming = jnp.concatenate(after, 1)
    out = []
    for t in range(len(rows)):
        u = solved[7][t]
        for j in range(7):
            u = jnp.where(sub == j, solved[j][t], u)
        if t == 0:
            u = jnp.where(lane >= sub + r, u, 0.0)
        out.append(u)
    return jnp.concatenate(out, 1), upcoming


def unit(size):
    return (
        lax.broadcasted_iota(jnp.int32, (size, size), 0) == lax.broadcasted_iota(jnp.int32, (size, size), 1)
    ).astype(f32)


def factor_block(blocks, store):
    panels = [block[:8, :] for block in blocks]
    found = [None] * len(blocks)
    for r in range(0, HALF, 8):
        for leaf, block in enumerate(blocks):
            start = (r + 8) // 16 * 16
            if found[leaf] is not None and start < HALF:
                rank_update(block, found[leaf], start)
        for leaf, block in enumerate(blocks):
            upcoming = block[r + 8 : r + 16, :] if r + 8 < HALF else None
            found[leaf], panels[leaf] = factor_panel(panels[leaf], upcoming, r)
            store(leaf, r, found[leaf])


def head_kernel(scalars, mine, theirs, window, u_head, x_head, rest, gram, s0, s1):
    xl, core, bound = scalars[1], scalars[2], scalars[3]
    count = mine.shape[0] // 2
    half_rows = mine.shape[2]
    window_rows = 2 * half_rows
    for block in range(2 * count):
        lanes = slice(block // count * half_rows, (block // count + 1) * half_rows)
        for side in range(2):
            start = block % count * 32 + (side ^ xl) * 16
            for source, at in ((mine, core), (theirs, 1 - core)):
                there = pl.ds(pl.multiple_of(start + at * 8, 8), 8)
                window[there, lanes] = source[block, side * 8 : side * 8 + 8, :]
    edge = window_rows // 2 + HALF
    lane = lax.broadcasted_iota(jnp.int32, (R, edge), 1)
    head = window[:, :edge]
    tail = window[:, window_rows - edge :]
    for leaf, (inside, leaf_rows) in enumerate(
        ((lane < bound, head), (lane + (window_rows - edge) >= bound, tail))
    ):
        high_rows, low_rows = two_parts(leaf_rows)
        masked = two_parts(jnp.where(inside, leaf_rows, 0.0))[0]
        cross = dot(masked, low_rows, NT)
        gram[leaf] = dot(masked, high_rows, NT) + cross + cross.T
    blocks = (s0, s1)
    for leaf in range(2):
        rows = jnp.where(leaf == 0, bound, window_rows - bound)
        count_rows = jnp.full((1, 1), rows, jnp.int32).astype(f32)
        gram[leaf] = gram[leaf] / count_rows
        blocks[leaf][:, :R] = gram[leaf, :HALF, :]
        blocks[leaf][:, R:] = unit(HALF)

    def store(leaf, r, u):
        u_head[leaf, r : r + 8, :] = u[:, :R]
        x_head[leaf, r : r + 8, :] = u[:, R:]

    factor_block(blocks, store)
    for leaf in range(2):
        side = u_head[leaf, :, HALF:]
        change = dot(side, jnp.concatenate([side, x_head[leaf]], 1), TN, highest)
        rest[leaf, :, :HALF] = gram[leaf, HALF:, HALF:] - change[:, :HALF]
        rest[leaf, :, HALF:] = -change[:, HALF:]


def factor_head(scalars, mine, theirs):
    window_rows = 2 * mine.shape[2]
    return pl.pallas_call(
        head_kernel,
        in_specs=[SMEM, VMEM, VMEM],
        out_specs=[VMEM] * 4,
        out_shape=[
            shape(R, window_rows),
            shape(2, HALF, R),
            shape(2, HALF, HALF),
            shape(2, HALF, R),
        ],
        scratch_shapes=[pltpu.VMEM((2, R, R), f32)] + [pltpu.VMEM((HALF, R + HALF), f32)] * 2,
        compiler_params=PARAMS,
    )(scalars, mine, theirs)


def tail_kernel(scalars, u_head, x_head, rest, packed, u_own, x_own, u_tail, x_tail, s0, s1):
    group = scalars[4]
    blocks = (s0, s1)
    for leaf in range(2):
        blocks[leaf][:, :R] = rest[leaf]
        blocks[leaf][:, R:] = unit(HALF)

    def store(leaf, r, u):
        u_tail[leaf, r : r + 8, :] = u[:, :HALF]
        x_tail[leaf, r : r + 8, :] = u[:, HALF:]

    factor_block(blocks, store)
    row = lax.broadcasted_iota(jnp.int32, (HALF, HALF), 0)
    column = lax.broadcasted_iota(jnp.int32, (HALF, HALF), 1)
    packed[:HALF, :] = jnp.where(row <= column, u_tail[0], u_tail[1].T)
    diagonal = jnp.sum(jnp.where(row == column, u_tail[1], 0.0), axis=0, keepdims=True)
    packed[HALF:, :] = jnp.broadcast_to(diagonal, (8, HALF))
    start = pl.multiple_of(group % (HALF // 8) * 8, 8)
    in_head = group < HALF // 8
    for leaf in range(2):
        own = pl.ds(start, 8)
        zero = jnp.zeros((8, HALF), f32)
        u_own[leaf] = jnp.where(
            in_head, u_head[leaf, own, :], jnp.concatenate([zero, u_tail[leaf, own, :]], 1)
        )
        x_own[leaf] = jnp.where(
            in_head, jnp.concatenate([x_head[leaf, own, :], zero], 1), x_tail[leaf, own, :]
        )


def factor_tail(scalars, u_head, x_head, rest):
    return pl.pallas_call(
        tail_kernel,
        in_specs=[SMEM] + [VMEM] * 3,
        out_specs=[VMEM] * 3,
        out_shape=[shape(HALF + 8, HALF), shape(2, 8, R), shape(2, 8, R)],
        scratch_shapes=[pltpu.VMEM((2, HALF, HALF), f32), pltpu.VMEM((2, HALF, R), f32)]
        + [pltpu.VMEM((HALF, R + HALF), f32)] * 2,
        compiler_params=PARAMS,
        cost_estimate=pl.CostEstimate(flops=8 * 10**9, bytes_accessed=10**6, transcendentals=0),
    )(scalars, u_head, x_head, rest)


def bases_kernel(scalars, window, x_own, u_own, sib_head, out, head_part):
    high_x, low_x = two_parts(jnp.concatenate([x_own[0], x_own[1]], 0))
    high_w, low_w = two_parts(window[...])
    wide = dot(jnp.concatenate([high_x, low_x], 0), high_w, NN)
    solved = wide[:16] + wide[16:] + dot(high_x, low_w, NN)
    lane = lax.broadcasted_iota(jnp.int32, out.shape, 1)
    out[...] = jnp.where(lane < scalars[3], solved[:8], solved[8:])
    for leaf in range(2):
        head_part[leaf] = dot(u_own[leaf], sib_head[leaf], NT, highest)


def coupling_kernel(u_own, head_part, packed, out):
    row = lax.broadcasted_iota(jnp.int32, (HALF, HALF), 0)
    column = lax.broadcasted_iota(jnp.int32, (HALF, HALF), 1)
    square = packed[:HALF, :]
    second = jnp.where(row > column, square, 0.0).T
    sib_tail = [
        jnp.where(row <= column, square, 0.0),
        jnp.where(row == column, packed[HALF : HALF + 1, :], second),
    ]
    for leaf in range(2):
        out[leaf, :, :HALF] = head_part[leaf]
        out[leaf, :, HALF:] = dot(u_own[leaf, :, HALF:], sib_tail[leaf], NT, highest)


def local(contrib, assembled, pattern, omega, row_maps, leaf_bounds):
    tile_rows, tile_cols = contrib.shape[1:]
    window_rows, own_count = omega.shape
    half_rows = assembled.shape[1]
    z_count, y_count = lax.axis_size("z"), lax.axis_size("y")
    groups = lax.axis_size("child") * y_count
    width = R // (2 * groups)
    child = lax.axis_index("child")
    row_pos = lax.axis_index(("z", "xl"))
    col_pos = lax.axis_index(("y", "core"))
    sibling_block = lax.ppermute(contrib[0], "child", SWAP)
    columns = lax.dynamic_slice_in_dim(row_maps, col_pos * tile_cols, tile_cols, 1) - col_pos * window_rows
    targets = lax.dynamic_slice_in_dim(row_maps, row_pos * tile_rows, tile_rows, 1) - row_pos * window_rows
    maps = jnp.stack([columns, targets])
    sibling_maps = lax.ppermute(maps, "child", SWAP)
    scalars = jnp.stack(
        [
            child,
            lax.axis_index("xl"),
            lax.axis_index("core"),
            leaf_bounds[0],
            lax.axis_index(("child", "y", "core")),
        ]
    ).astype(jnp.int32)

    copies = pl.pallas_call(
        copies_kernel,
        in_specs=[VMEM],
        out_specs=VMEM,
        out_shape=shape(z_count, own_count, window_rows),
        compiler_params=PARAMS,
    )(omega.T)
    own = lax.all_to_all(copies, "z", 0, 0)
    total = own_operator(scalars, pattern, contrib[0], assembled[0], columns, targets)
    other = lax.ppermute(own, "xl", SWAP)

    sibling_block, sibling_maps = lax.optimization_barrier((sibling_block, sibling_maps))
    top, low = whole_operator(scalars, total, sibling_block, sibling_maps)

    give, keep = apply_operator(scalars, own, other, top, low)
    parts = keep + lax.ppermute(give, "core", SWAP)
    terms = lax.all_to_all(parts, "y", 0, 0)
    samples = jnp.sum(terms, axis=0)
    mine = lax.all_to_all(
        jnp.broadcast_to(samples, (groups,) + samples.shape), ("child", "y"), 0, 0
    )
    theirs = lax.ppermute(mine, "core", SWAP)

    window, u_head, x_head, rest = factor_head(scalars, mine, theirs)
    sib_head = lax.ppermute(u_head, "xl", SWAP)
    u_tail, u_own, x_own = factor_tail(scalars, u_head, x_head, rest)
    sib_tail = lax.ppermute(u_tail, "xl", SWAP)
    bases, head_part = pl.pallas_call(
        bases_kernel,
        in_specs=[SMEM] + [VMEM] * 4,
        out_specs=[VMEM, VMEM],
        out_shape=[shape(width, window_rows), shape(2, width, HALF)],
        compiler_params=PARAMS,
        cost_estimate=pl.CostEstimate(flops=10**9, bytes_accessed=10**6, transcendentals=0),
    )(scalars, window, x_own, u_own, sib_head)
    coupling = pl.pallas_call(
        coupling_kernel,
        in_specs=[VMEM] * 3,
        out_specs=VMEM,
        out_shape=shape(2, width, R),
        compiler_params=PARAMS,
    )(u_own, head_part, sib_tail)
    return (bases.T, coupling[None])


def solution(mesh):
    fine = Mesh(mesh.devices.reshape(2, 8, 2, 8, 2), ("child", "z", "xl", "y", "core"))
    row, col = ("z", "xl"), ("y", "core")
    in_specs = (
        P("child", row, col),
        P("child", row, col),
        P(row, col),
        P(col, row),
        P("child", None),
        P(row),
    )
    out_specs = (P(row, ("child",) + col), P(row, None, ("child",) + col, None))
    return jax.shard_map(local, mesh=fine, in_specs=in_specs, out_specs=out_specs, check_vma=False)
```

```python
import jax
import jax.numpy as jnp
from jax import lax
from jax.experimental import pallas as pl
from jax.experimental.pallas import tpu as pltpu
from jax.sharding import Mesh, PartitionSpec as P

R = 256
BT = 256
HALF = 128

f32, bf16 = jnp.float32, jnp.bfloat16
highest = lax.Precision.HIGHEST
SWAP = [(0, 1), (1, 0)]
NN = (((1,), (0,)), ((), ()))
NT = (((1,), (1,)), ((), ()))
TN = (((0,), (0,)), ((), ()))
VMEM = pl.BlockSpec(memory_space=pltpu.VMEM)
SMEM = pl.BlockSpec(memory_space=pltpu.SMEM)
PARAMS = pltpu.CompilerParams(vmem_limit_bytes=16 << 20)


def shape(*sizes, dtype=f32):
    return jax.ShapeDtypeStruct(sizes, dtype)


def dot(a, b, dims, precision=None):
    return lax.dot_general(a, b, dims, precision=precision, preferred_element_type=f32)


def two_parts(a):
    top = a.astype(bf16)
    return top, (a - top.astype(f32)).astype(bf16)


def copies_kernel(lines, out):
    for copy in range(out.shape[0]):
        out[copy] = lines[...]


def child_terms(child, block, targets, spread_rows, half_rows):
    places = lax.broadcasted_iota(jnp.int32, (half_rows, targets.shape[1]), 0) + child * half_rows
    spread = (places == targets[...]).astype(f32).astype(bf16)
    for part, piece in enumerate(two_parts(block[...])):
        spread_rows[part] = dot(spread, piece, NN).astype(bf16)


def picked_terms(columns, spread_rows, start, rows):
    places = lax.broadcasted_iota(jnp.int32, (rows, columns.shape[1]), 0) + start
    pick = (places == columns[...]).astype(f32).astype(bf16)
    return dot(pick, spread_rows[0], NT) + dot(pick, spread_rows[1], NT)


def own_kernel(scalars, pattern, block, assembled, columns, targets, total, spread_rows):
    child = scalars[0]
    window_rows, half_rows = total.shape
    child_terms(child, block, targets, spread_rows, half_rows)
    tiles = half_rows // BT
    for step in range(window_rows // BT):
        rows = slice(step * BT, (step + 1) * BT)
        terms = picked_terms(columns, spread_rows, step * BT, BT)
        for tile in range(tiles):
            keep = pattern[child * tiles + tile, step].astype(f32)
            lanes = slice(tile * BT, (tile + 1) * BT)
            total[rows, lanes] = terms[:, lanes] + assembled[lanes, rows].T * keep


def sibling_kernel(scalars, total, block, maps, top, low, spread_rows):
    window_rows, half_rows = total.shape
    child_terms(scalars[0], block, maps.at[1], spread_rows, half_rows)
    for step in range(window_rows // BT):
        rows = slice(step * BT, (step + 1) * BT)
        terms = picked_terms(maps.at[0], spread_rows, step * BT, BT)
        top[rows, :], low[rows, :] = two_parts(total[rows, :] + terms)


def own_operator(scalars, pattern, block, assembled, columns, targets):
    half_rows, window_rows = assembled.shape
    return pl.pallas_call(
        own_kernel,
        in_specs=[SMEM, SMEM] + [VMEM] * 4,
        out_specs=VMEM,
        out_shape=shape(window_rows, half_rows),
        scratch_shapes=[pltpu.VMEM((2, half_rows, block.shape[1]), bf16)],
        compiler_params=PARAMS,
        cost_estimate=pl.CostEstimate(flops=2 * 10**9, bytes_accessed=5 * 10**6, transcendentals=0),
    )(scalars, pattern, block, assembled, columns, targets)


def whole_operator(scalars, total, block, maps):
    window_rows, half_rows = total.shape
    return pl.pallas_call(
        sibling_kernel,
        in_specs=[SMEM] + [VMEM] * 3,
        out_specs=[VMEM, VMEM],
        out_shape=[shape(window_rows, half_rows, dtype=bf16)] * 2,
        scratch_shapes=[
            pltpu.VMEM((2, half_rows, block.shape[1]), bf16),
        ],
        compiler_params=PARAMS,
        cost_estimate=pl.CostEstimate(flops=2 * 10**9, bytes_accessed=5 * 10**6, transcendentals=0),
    )(scalars, total, block, maps)


def apply_kernel(scalars, own, ahead, behind, top, low, give, keep):
    core = scalars[2]
    count, width, half_rows = give.shape
    depth = top.shape[0]
    rows = count * width
    ordered = jnp.concatenate(
        [piece[:, side].reshape(-1, depth) for side in range(2) for piece in (own, ahead, behind)]
    )
    high_lines, low_lines = two_parts(ordered)
    stacked = jnp.concatenate([high_lines, low_lines])
    for tile in range(half_rows // BT):
        lanes = slice(tile * BT, (tile + 1) * BT)
        wide = dot(stacked, top[:, lanes], NN)
        out = wide[: 2 * rows] + wide[2 * rows :] + dot(high_lines, low[:, lanes], NN)
        first, second = out[:rows], out[rows:]
        for target, value in (
            (give, jnp.where(core == 0, second, first)),
            (keep, jnp.where(core == 0, first, second)),
        ):
            for piece in range(2):
                there = slice(piece * width // 2, (piece + 1) * width // 2)
                part = value[piece * rows // 2 : (piece + 1) * rows // 2]
                target[:, there, lanes] = part.reshape(count, width // 2, BT)


def apply_operator(scalars, own, ahead, behind, top, low):
    count, width, depth = own.shape
    half_rows = top.shape[1]
    lines = [v.reshape(v.shape[0], 2, width // 2, depth) for v in (own, ahead, behind)]
    return pl.pallas_call(
        apply_kernel,
        in_specs=[SMEM] + [VMEM] * 5,
        out_specs=[VMEM, VMEM],
        out_shape=[shape(count, width, half_rows)] * 2,
        compiler_params=PARAMS,
        cost_estimate=pl.CostEstimate(flops=10**9, bytes_accessed=6 * 10**6, transcendentals=0),
    )(scalars, *lines, top, low)


def spread_out(row_or_column):
    return jnp.broadcast_to(row_or_column, (8, 128))


def lane_tiles(a):
    return [a[:, t : t + 128] for t in range(0, a.shape[1], 128)]


def rank_update(block, u, start):
    a = u.astype(bf16).astype(f32)
    b = (u - a).astype(bf16).astype(f32)
    c = u - a - b
    left = jnp.concatenate([v[:, :HALF] for v in (a, a, b, b, a, c)], 0).T[start:].astype(bf16)
    right = jnp.concatenate([a, b, a, b, c, a], 0).astype(bf16)
    block[start:, :] -= dot(left, right, NN)


def factor_panel(panel, upcoming, r):
    sub = lax.broadcasted_iota(jnp.int32, (8, 128), 0)
    lane = lax.broadcasted_iota(jnp.int32, (8, 128), 1)
    rows = lane_tiles(panel)
    columns = [spread_out(rows[0][:, r + j : r + j + 1]) for j in range(8)]
    solved = []
    for j in range(8):
        inverse = lax.rsqrt(spread_out(columns[j][j : j + 1]))
        column = columns[j] * inverse
        solved.append([spread_out(v[j : j + 1]) * inverse for v in rows])
        below = jnp.where(sub > j, column, 0.0)
        rows = [v - below * w for v, w in zip(rows, solved[j])]
        for k in range(j + 1, 8):
            columns[k] = columns[k] - column * spread_out(column[k : k + 1])
    if upcoming is not None:
        after = lane_tiles(upcoming)
        pick = lane == sub + (r + 8)
        for j in range(8):
            column = spread_out(jnp.sum(jnp.where(pick, solved[j][0], 0.0), axis=1, keepdims=True))
            after = [v - column * w for v, w in zip(after, solved[j])]
        upcoming = jnp.concatenate(after, 1)
    out = []
    for t in range(len(rows)):
        u = solved[7][t]
        for j in range(7):
            u = jnp.where(sub == j, solved[j][t], u)
        if t == 0:
            u = jnp.where(lane >= sub + r, u, 0.0)
        out.append(u)
    return jnp.concatenate(out, 1), upcoming


def unit(size):
    return (
        lax.broadcasted_iota(jnp.int32, (size, size), 0) == lax.broadcasted_iota(jnp.int32, (size, size), 1)
    ).astype(f32)


def factor_block(blocks, store):
    panels = [block[:8, :] for block in blocks]
    found = [None] * len(blocks)
    for r in range(0, HALF, 8):
        for leaf, block in enumerate(blocks):
            start = (r + 8) // 16 * 16
            if found[leaf] is not None and start < HALF:
                rank_update(block, found[leaf], start)
        for leaf, block in enumerate(blocks):
            upcoming = block[r + 8 : r + 16, :] if r + 8 < HALF else None
            found[leaf], panels[leaf] = factor_panel(panels[leaf], upcoming, r)
            store(leaf, r, found[leaf])


def head_kernel(scalars, mine, theirs, window, u_head, x_head, rest, gram, s0, s1):
    xl, core, bound = scalars[1], scalars[2], scalars[3]
    count = mine.shape[0] // 2
    half_rows = mine.shape[2]
    window_rows = 2 * half_rows
    for block in range(2 * count):
        lanes = slice(block // count * half_rows, (block // count + 1) * half_rows)
        for side in range(2):
            start = block % count * 32 + (side ^ xl) * 16
            for source, at in ((mine, core), (theirs, 1 - core)):
                there = pl.ds(pl.multiple_of(start + at * 8, 8), 8)
                window[there, lanes] = source[block, side * 8 : side * 8 + 8, :]
    edge = window_rows // 2 + HALF
    lane = lax.broadcasted_iota(jnp.int32, (R, edge), 1)
    head = window[:, :edge]
    tail = window[:, window_rows - edge :]
    for leaf, (inside, leaf_rows) in enumerate(
        ((lane < bound, head), (lane + (window_rows - edge) >= bound, tail))
    ):
        high_rows, low_rows = two_parts(leaf_rows)
        masked = two_parts(jnp.where(inside, leaf_rows, 0.0))[0]
        cross = dot(masked, low_rows, NT)
        gram[leaf] = dot(masked, high_rows, NT) + cross + cross.T
    blocks = (s0, s1)
    for leaf in range(2):
        rows = jnp.where(leaf == 0, bound, window_rows - bound)
        count_rows = jnp.full((1, 1), rows, jnp.int32).astype(f32)
        gram[leaf] = gram[leaf] / count_rows
        blocks[leaf][:, :R] = gram[leaf, :HALF, :]
        blocks[leaf][:, R:] = unit(HALF)

    def store(leaf, r, u):
        u_head[leaf, r : r + 8, :] = u[:, :R]
        x_head[leaf, r : r + 8, :] = u[:, R:]

    factor_block(blocks, store)
    for leaf in range(2):
        side = u_head[leaf, :, HALF:]
        change = dot(side, jnp.concatenate([side, x_head[leaf]], 1), TN, highest)
        rest[leaf, :, :HALF] = gram[leaf, HALF:, HALF:] - change[:, :HALF]
        rest[leaf, :, HALF:] = -change[:, HALF:]


def factor_head(scalars, mine, theirs):
    window_rows = 2 * mine.shape[2]
    return pl.pallas_call(
        head_kernel,
        in_specs=[SMEM, VMEM, VMEM],
        out_specs=[VMEM] * 4,
        out_shape=[
            shape(R, window_rows),
            shape(2, HALF, R),
            shape(2, HALF, HALF),
            shape(2, HALF, R),
        ],
        scratch_shapes=[pltpu.VMEM((2, R, R), f32)] + [pltpu.VMEM((HALF, R + HALF), f32)] * 2,
        compiler_params=PARAMS,
    )(scalars, mine, theirs)


def tail_kernel(scalars, u_head, x_head, rest, packed, u_own, x_own, u_tail, x_tail, s0, s1):
    group = scalars[4]
    blocks = (s0, s1)
    for leaf in range(2):
        blocks[leaf][:, :R] = rest[leaf]
        blocks[leaf][:, R:] = unit(HALF)

    def store(leaf, r, u):
        u_tail[leaf, r : r + 8, :] = u[:, :HALF]
        x_tail[leaf, r : r + 8, :] = u[:, HALF:]

    factor_block(blocks, store)
    row = lax.broadcasted_iota(jnp.int32, (HALF, HALF), 0)
    column = lax.broadcasted_iota(jnp.int32, (HALF, HALF), 1)
    packed[:HALF, :] = jnp.where(row <= column, u_tail[0], u_tail[1].T)
    diagonal = jnp.sum(jnp.where(row == column, u_tail[1], 0.0), axis=0, keepdims=True)
    packed[HALF:, :] = jnp.broadcast_to(diagonal, (8, HALF))
    start = pl.multiple_of(group % (HALF // 8) * 8, 8)
    in_head = group < HALF // 8
    for leaf in range(2):
        own = pl.ds(start, 8)
        zero = jnp.zeros((8, HALF), f32)
        u_own[leaf] = jnp.where(
            in_head, u_head[leaf, own, :], jnp.concatenate([zero, u_tail[leaf, own, :]], 1)
        )
        x_own[leaf] = jnp.where(
            in_head, jnp.concatenate([x_head[leaf, own, :], zero], 1), x_tail[leaf, own, :]
        )


def factor_tail(scalars, u_head, x_head, rest):
    return pl.pallas_call(
        tail_kernel,
        in_specs=[SMEM] + [VMEM] * 3,
        out_specs=[VMEM] * 3,
        out_shape=[shape(HALF + 8, HALF), shape(2, 8, R), shape(2, 8, R)],
        scratch_shapes=[pltpu.VMEM((2, HALF, HALF), f32), pltpu.VMEM((2, HALF, R), f32)]
        + [pltpu.VMEM((HALF, R + HALF), f32)] * 2,
        compiler_params=PARAMS,
        cost_estimate=pl.CostEstimate(flops=8 * 10**9, bytes_accessed=10**6, transcendentals=0),
    )(scalars, u_head, x_head, rest)


def bases_kernel(scalars, window, x_own, u_own, sib_head, out, head_part):
    high_x, low_x = two_parts(jnp.concatenate([x_own[0], x_own[1]], 0))
    high_w, low_w = two_parts(window[...])
    wide = dot(jnp.concatenate([high_x, low_x], 0), high_w, NN)
    solved = wide[:16] + wide[16:] + dot(high_x, low_w, NN)
    lane = lax.broadcasted_iota(jnp.int32, out.shape, 1)
    out[...] = jnp.where(lane < scalars[3], solved[:8], solved[8:])
    for leaf in range(2):
        head_part[leaf] = dot(u_own[leaf], sib_head[leaf], NT, highest)


def coupling_kernel(u_own, head_part, packed, out):
    row = lax.broadcasted_iota(jnp.int32, (HALF, HALF), 0)
    column = lax.broadcasted_iota(jnp.int32, (HALF, HALF), 1)
    square = packed[:HALF, :]
    second = jnp.where(row > column, square, 0.0).T
    sib_tail = [
        jnp.where(row <= column, square, 0.0),
        jnp.where(row == column, packed[HALF : HALF + 1, :], second),
    ]
    for leaf in range(2):
        out[leaf, :, :HALF] = head_part[leaf]
        out[leaf, :, HALF:] = dot(u_own[leaf, :, HALF:], sib_tail[leaf], NT, highest)


def local(contrib, assembled, pattern, omega, row_maps, leaf_bounds):
    tile_rows, tile_cols = contrib.shape[1:]
    window_rows, own_count = omega.shape
    half_rows = assembled.shape[1]
    z_count, y_count = lax.axis_size("z"), lax.axis_size("y")
    groups = lax.axis_size("child") * y_count
    width = R // (2 * groups)
    child = lax.axis_index("child")
    row_pos = lax.axis_index(("z", "xl"))
    col_pos = lax.axis_index(("y", "core"))
    sibling_block = lax.ppermute(contrib[0], "child", SWAP)
    columns = lax.dynamic_slice_in_dim(row_maps, col_pos * tile_cols, tile_cols, 1) - col_pos * window_rows
    targets = lax.dynamic_slice_in_dim(row_maps, row_pos * tile_rows, tile_rows, 1) - row_pos * window_rows
    maps = jnp.stack([columns, targets])
    sibling_maps = lax.ppermute(maps, "child", SWAP)
    scalars = jnp.stack(
        [
            child,
            lax.axis_index("xl"),
            lax.axis_index("core"),
            leaf_bounds[0],
            lax.axis_index(("child", "y", "core")),
        ]
    ).astype(jnp.int32)

    copies = pl.pallas_call(
        copies_kernel,
        in_specs=[VMEM],
        out_specs=VMEM,
        out_shape=shape(z_count, own_count, window_rows),
        compiler_params=PARAMS,
    )(omega.T)
    own = lax.all_to_all(copies, "z", 0, 0)
    total = own_operator(scalars, pattern, contrib[0], assembled[0], columns, targets)
    ring = lax.axis_size("child") * lax.axis_size("xl")
    other = [
        lax.ppermute(piece, ("child", "xl"), [(i, (i + step) % ring) for i in range(ring)])
        for piece, step in ((own[: z_count // 2], 1), (own[z_count // 2 :], -1))
    ]

    sibling_block, sibling_maps = lax.optimization_barrier((sibling_block, sibling_maps))
    top, low = whole_operator(scalars, total, sibling_block, sibling_maps)

    give, keep = apply_operator(scalars, own, *other, top, low)
    parts = keep + lax.ppermute(give, "core", SWAP)
    terms = lax.all_to_all(parts, "y", 0, 0)
    samples = jnp.sum(terms, axis=0)
    mine = lax.all_to_all(
        jnp.broadcast_to(samples, (groups,) + samples.shape), ("child", "y"), 0, 0
    )
    theirs = lax.ppermute(mine, "core", SWAP)

    window, u_head, x_head, rest = factor_head(scalars, mine, theirs)
    sib_head = lax.ppermute(u_head, "xl", SWAP)
    u_tail, u_own, x_own = factor_tail(scalars, u_head, x_head, rest)
    sib_tail = lax.ppermute(u_tail, "xl", SWAP)
    bases, head_part = pl.pallas_call(
        bases_kernel,
        in_specs=[SMEM] + [VMEM] * 4,
        out_specs=[VMEM, VMEM],
        out_shape=[shape(width, window_rows), shape(2, width, HALF)],
        compiler_params=PARAMS,
        cost_estimate=pl.CostEstimate(flops=10**9, bytes_accessed=10**6, transcendentals=0),
    )(scalars, window, x_own, u_own, sib_head)
    coupling = pl.pallas_call(
        coupling_kernel,
        in_specs=[VMEM] * 3,
        out_specs=VMEM,
        out_shape=shape(2, width, R),
        compiler_params=PARAMS,
    )(u_own, head_part, sib_tail)
    return (bases.T, coupling[None])


def solution(mesh):
    fine = Mesh(mesh.devices.reshape(2, 8, 2, 8, 2), ("child", "z", "xl", "y", "core"))
    row, col = ("z", "xl"), ("y", "core")
    in_specs = (
        P("child", row, col),
        P("child", row, col),
        P(row, col),
        P(col, row),
        P("child", None),
        P(row),
    )
    out_specs = (P(row, ("child",) + col), P(row, None, ("child",) + col, None))
    return jax.shard_map(local, mesh=fine, in_specs=in_specs, out_specs=out_specs, check_vma=False)
```
